32 devices in a mesh: seq: 16 (over z, y, core), tp: 2 (over x).
Axes of the slice: x: 2, y: 2, z: 4, core: 2. Of those that a mesh axis runs over, the one named last changes fastest.
Arguments:
- queries: bfloat16 [16384, 4096], P('seq', 'tp'), may hold values from -600 to 600
- neighbours: bfloat16 [128, 896, 128], P('seq', 'tp'), may hold values from -6 to 6
- key_weight: bfloat16 [896, 4096], P(None, 'tp'), may hold values from -0.1875 to 0.1875
- value_weight: bfloat16 [896, 4096], P(None, 'tp'), may hold values from -0.1875 to 0.1875
- neighbour_ids: int32 [256, 2], P('seq'), may hold values from 0 to 127, as said below
Outputs:
- attended: bfloat16 [16384, 4096], P('seq', 'tp')
The draws below stay inside these ranges and needn't reach their ends.
Inputs may be any that keep to these rules, and one draw needn't show every extreme that they name: `neighbour_ids`: block b is stored on index b // 8 of seq. Among the 32 neighbours of the spans of one index of seq, at most 2 are stored on any one index of seq, and exactly 2 on some.
All inputs are finite; a program needn't handle non-finite values.
Results may differ from the reference program's by a relative error of at most 0.014.
Values may be sent and summed in bfloat16 or wider, within the bound.
No kernel may reach another device: no remote copies, remote signals or barrier semaphores. Data moves between devices by JAX's collectives and lax.ppermute only.
A program may use at most 128 MiB of HBM per device.

```python
import jax
import jax.numpy as jnp
from jax import lax

HEADS = 32
HDIM = 128
DE = 896
SPAN = 64
NLEN = 128
CH_DEV = 16
NB_DEV = 8
SPANS = 256
TOKENS = 16384
NBLK = 128
N_SEQ = 16


def draw_queries(key, part):
    key = jax.random.fold_in(key, 11)
    base_key = jax.random.fold_in(key, 0)
    shape = (TOKENS, HEADS * HDIM)
    values = jax.random.truncated_normal(base_key, -4.0, 4.0, shape, jnp.float32)
    return values.astype(jnp.bfloat16)


def draw_neighbour_ids(key, part):
    key = jax.random.fold_in(key, 5)
    order_key, block_key = jax.random.split(key)
    seq_keys = jax.random.split(order_key, N_SEQ)
    orders = jax.vmap(lambda single: jax.random.permutation(single, N_SEQ))(seq_keys)
    slot_index = jnp.arange(2 * CH_DEV) % N_SEQ
    sources = orders[:, slot_index]
    within = jax.random.randint(block_key, (N_SEQ, 2 * CH_DEV), 0, NB_DEV)
    chosen_ids = sources * NB_DEV + within
    return chosen_ids.reshape(SPANS, 2).astype(jnp.int32)


def steps_of(rng, extent, pieces, smallest, top_value):
    loudness = 1.0
    for position, blocks in pieces:
        draws = jax.random.uniform(jax.random.fold_in(jax.random.fold_in(rng, 6), position), (blocks,), jnp.float32, smallest / len(pieces), top_value / len(pieces))
        loudness = loudness * jnp.repeat(jnp.exp(draws), extent[position] // blocks).reshape((-1,) + (1,) * (len(extent) - 1 - position))
    return loudness


def scatter_about(own_key, extent, scale, reach, pieces=(), dtype=jnp.bfloat16):
    drawn = scale * jax.random.normal(own_key, extent, jnp.float32)
    if pieces:
        drawn = drawn * steps_of(own_key, extent, pieces, -0.22, 0.18)
    return jnp.clip(drawn, -reach, reach).astype(dtype)


def setup_inputs(seed: int = 0) -> dict:
    streams_of = jax.random.split(jax.random.key(seed), 6)
    return {
        "queries": draw_queries(jax.random.fold_in(streams_of[5], 71), 0),
        "neighbours": scatter_about(streams_of[1], (NBLK, DE, NLEN), 1.0, 6.0, ((0, 16), (1, 2))),
        "key_weight": scatter_about(streams_of[2], (DE, HEADS * HDIM), DE ** -0.5, 0.1875, ((1, 2),)),
        "value_weight": scatter_about(streams_of[3], (DE, HEADS * HDIM), DE ** -0.5, 0.1875, ((1, 2),)),
        "neighbour_ids": draw_neighbour_ids(jax.random.fold_in(streams_of[5], 71), 0),
    }


def reference(queries, neighbours, key_weight, value_weight, neighbour_ids):
    feature_rows = jnp.swapaxes(neighbours, 1, 2).reshape(NBLK * NLEN, DE).astype(jnp.float32)
    edge_rows = SPAN - 1

    def one_head(operands):
        w_key, w_value, q_head = operands
        key_rows = jnp.dot(feature_rows, w_key.astype(jnp.float32), precision=lax.Precision.HIGHEST)
        key_rows = key_rows.astype(jnp.bfloat16).reshape(NBLK, NLEN, HDIM)
        value_rows = jnp.dot(feature_rows, w_value.astype(jnp.float32), precision=lax.Precision.HIGHEST)
        value_rows = value_rows.astype(jnp.bfloat16).reshape(NBLK, NLEN, HDIM)
        windows = jnp.concatenate([q_head[edge_rows:], jnp.zeros((edge_rows, HDIM), jnp.bfloat16)], axis=0)
        windows = windows.reshape(SPANS, SPAN, HDIM)
        chosen_keys = key_rows[neighbour_ids]
        chosen_values = value_rows[neighbour_ids]
        scores = jnp.einsum('cqd,cjkd->cjqk', windows.astype(jnp.float32), chosen_keys.astype(jnp.float32)) * (HDIM ** -0.5)
        highest = jnp.max(scores, axis=-1, keepdims=True)
        exponent = jnp.exp(scores - highest)
        totals = jnp.sum(exponent, axis=-1, keepdims=True)
        weights = (exponent / totals).astype(jnp.bfloat16)
        partials = jnp.einsum('cjqk,cjkd->cjqd', weights.astype(jnp.float32), chosen_values.astype(jnp.float32)).astype(jnp.bfloat16)
        log_totals = (highest + jnp.log(totals))[..., 0]
        largest = jnp.max(log_totals, axis=1, keepdims=True)
        shares = jnp.exp(log_totals - largest)
        shares = shares / jnp.sum(shares, axis=1, keepdims=True)
        blended = jnp.sum(shares[..., None] * partials.astype(jnp.float32), axis=1).astype(jnp.bfloat16)
        blended = blended.reshape(TOKENS, HDIM)
        return jnp.concatenate([jnp.zeros((edge_rows, HDIM), jnp.bfloat16), blended[:TOKENS - edge_rows]], axis=0)

    head_results = lax.map(one_head, (
        jnp.transpose(key_weight.reshape(DE, HEADS, HDIM), (1, 0, 2)),
        jnp.transpose(value_weight.reshape(DE, HEADS, HDIM), (1, 0, 2)),
        jnp.transpose(queries.reshape(TOKENS, HEADS, HDIM), (1, 0, 2))))
    return jnp.transpose(head_results, (1, 0, 2)).reshape(TOKENS, HEADS * HDIM)
```

```python
import functools

import jax
import jax.numpy as jnp
from jax import lax
from jax.experimental import pallas as pl
from jax.experimental.pallas import tpu as pltpu
from jax.sharding import PartitionSpec as P

HDIM = 128
SPAN = 64
GROUP = 4
PAIR = 2 * HDIM
VMEM_LIMIT = 56 * 1024 * 1024


def passed_along(x, axis, by):
    peers = lax.axis_size(axis)
    pairs = [(i, i + by) for i in range(peers) if 0 <= i + by < peers]
    return lax.ppermute(x, axis, pairs)


def slot_ranks(sources):
    positions = sources.shape[-1]
    alike = sources[..., :, None] == sources[..., None, :]
    earlier = jnp.arange(positions)[None, :] < jnp.arange(positions)[:, None]
    return jnp.sum(jnp.where(alike & earlier, 1, 0), axis=-1).astype(jnp.int32)


def pick_kernel(stored, blocks, picked, sems):
    count = picked.shape[0]
    copies = [
        pltpu.make_async_copy(blocks.at[stored[i]], picked.at[i], sems.at[i]) for i in range(count)
    ]
    for copy in copies:
        copy.start()
    for copy in copies:
        copy.wait()


def pick_blocks(stored, blocks):
    count = stored.shape[0]
    return pl.pallas_call(
        pick_kernel,
        grid_spec=pltpu.PrefetchScalarGridSpec(
            num_scalar_prefetch=1,
            grid=(1,),
            in_specs=[pl.BlockSpec(memory_space=pl.ANY)],
            out_specs=pl.BlockSpec(memory_space=pl.ANY),
            scratch_shapes=[pltpu.SemaphoreType.DMA((count,))],
        ),
        out_shape=jax.ShapeDtypeStruct((count,) + blocks.shape[1:], blocks.dtype),
        name="pick_blocks",
    )(stored, blocks)


def attend_kernel(sources, spans, *refs):
    x_refs = refs[:GROUP]
    q_refs = refs[GROUP : 2 * GROUP]
    wk_ref, wv_ref = refs[2 * GROUP : 2 * GROUP + 2]
    out_ref, lse_ref, xt, k_even, v_even, k_odd, v_odd = refs[-7:]
    nlen = x_refs[0].shape[-1]
    columns = wk_ref.shape[-1]
    pairs = columns // PAIR
    scale = HDIM ** (-0.5)
    for i in range(GROUP):
        xt[pl.ds(i * nlen, nlen), :] = x_refs[i][0].T
    lanes = lax.broadcasted_iota(jnp.int32, (SPAN, HDIM), 1)
    lse_ref[...] = jnp.zeros_like(lse_ref)

    def project(pair, k_ref, v_ref):
        cols = pl.ds(pl.multiple_of(pair * PAIR, PAIR), PAIR)
        rows = xt[...]
        k_ref[...] = jnp.dot(rows, wk_ref[:, cols], preferred_element_type=jnp.float32).astype(
            jnp.bfloat16
        )
        v_ref[...] = jnp.dot(rows, wv_ref[:, cols], preferred_element_type=jnp.float32).astype(
            jnp.bfloat16
        )

    def attend(pair, k_ref, v_ref):
        cols = pl.ds(pl.multiple_of(pair * PAIR, PAIR), PAIR)
        none = jnp.zeros((SPAN, HDIM), jnp.bfloat16)
        for i in range(GROUP):
            rows = pl.ds(i * nlen, nlen)
            q = q_refs[i][0, :, cols]
            upper = jnp.concatenate([q[:, :HDIM], none], axis=1)
            lower = jnp.concatenate([none, q[:, HDIM:]], axis=1)
            both = jnp.concatenate([upper, lower], axis=0)
            scores = lax.dot_general(
                both, k_ref[rows, :], (((1,), (1,)), ((), ())), preferred_element_type=jnp.float32
            )
            highest = jnp.max(scores, axis=-1, keepdims=True)
            exponent = jnp.exp((scores - highest) * scale)
            totals = jnp.sum(exponent, axis=-1, keepdims=True)
            blended = jnp.dot(
                exponent.astype(jnp.bfloat16), v_ref[rows, :], preferred_element_type=jnp.float32
            )
            inverse = 1.0 / totals
            first = blended[:SPAN, :HDIM] * inverse[:SPAN]
            second = blended[SPAN:, HDIM:] * inverse[SPAN:]
            out_ref[i, :, cols] = jnp.concatenate([first, second], axis=1).astype(jnp.bfloat16)
            lse = highest * scale + jnp.log(totals)
            held = lse_ref[i]
            held = jnp.where(lanes == 2 * pair, lse[:SPAN], held)
            lse_ref[i] = jnp.where(lanes == 2 * pair + 1, lse[SPAN:], held)

    project(0, k_even, v_even)

    def step(t, carry):
        project(2 * t + 1, k_odd, v_odd)
        attend(2 * t, k_even, v_even)
        project(2 * t + 2, k_even, v_even)
        attend(2 * t + 1, k_odd, v_odd)
        return carry

    lax.fori_loop(0, pairs // 2 - 1, step, 0)
    project(pairs - 1, k_odd, v_odd)
    attend(pairs - 2, k_even, v_even)
    attend(pairs - 1, k_odd, v_odd)


def attend_part(sources, spans, segment, windows, key_weight, value_weight, first, slots, held):
    count = sources.shape[0]
    features, nlen = segment.shape[1:]
    columns = windows.shape[-1]
    start = first // GROUP

    def block_at(i):
        return lambda g, sources, spans: (sources[g * GROUP + i], 0, 0)

    def window_at(i):
        return lambda g, sources, spans: (spans[g * GROUP + i], 0, 0)

    whole = pl.BlockSpec((features, columns), lambda g, *_: (0, 0))
    in_specs = [pl.BlockSpec((1, features, nlen), block_at(i)) for i in range(GROUP)]
    in_specs += [pl.BlockSpec((1, SPAN, columns), window_at(i)) for i in range(GROUP)]
    in_specs += [whole, whole]
    operands = [segment] * GROUP + [windows] * GROUP + [key_weight, value_weight]
    aliases = {}
    if held is not None:
        in_specs += [pl.BlockSpec(memory_space=pl.ANY)] * 2
        aliases = {2 + len(operands): 0, 3 + len(operands): 1}
        operands += list(held)
    kv = pltpu.VMEM((GROUP * nlen, PAIR), jnp.bfloat16)
    return pl.pallas_call(
        attend_kernel,
        grid_spec=pltpu.PrefetchScalarGridSpec(
            num_scalar_prefetch=2,
            grid=(count // GROUP,),
            in_specs=in_specs,
            out_specs=[
                pl.BlockSpec((GROUP, SPAN, columns), lambda g, *_: (g + start, 0, 0)),
                pl.BlockSpec((GROUP, SPAN, HDIM), lambda g, *_: (g + start, 0, 0)),
            ],
            scratch_shapes=[pltpu.VMEM((GROUP * nlen, features), jnp.bfloat16), kv, kv, kv, kv],
        ),
        out_shape=[
            jax.ShapeDtypeStruct((slots, SPAN, columns), jnp.bfloat16),
            jax.ShapeDtypeStruct((slots, SPAN, HDIM), jnp.float32),
        ],
        input_output_aliases=aliases,
        compiler_params=pltpu.CompilerParams(vmem_limit_bytes=VMEM_LIMIT),
        name="attend_part",
    )(sources, spans, *operands)


def mixed(p0, p1, l0, l1, head):
    cols = slice(head * HDIM, (head + 1) * HDIM)
    a, b = l0[:, head : head + 1], l1[:, head : head + 1]
    largest = jnp.maximum(a, b)
    ea, eb = jnp.exp(a - largest), jnp.exp(b - largest)
    inverse = 1.0 / (ea + eb)
    return p0[:, cols].astype(jnp.float32) * (ea * inverse) + p1[:, cols].astype(jnp.float32) * (
        eb * inverse
    )


def mix_last_kernel(places, p0, p1, l0, l1, out_ref):
    a, b = l0[0], l1[0]
    for head in range(out_ref.shape[-1] // HDIM):
        cols = slice(head * HDIM, (head + 1) * HDIM)
        out_ref[:, cols] = mixed(p0[0], p1[0], a, b, head).astype(jnp.bfloat16)


def mix_kernel(places, p0, p1, l0, l1, carried, out_ref, before):
    @pl.when(pl.program_id(0) == 0)
    def _():
        before[...] = carried[...]

    a, b = l0[0], l1[0]
    early = lax.broadcasted_iota(jnp.int32, (SPAN, HDIM), 0) < SPAN - 1
    for head in range(out_ref.shape[-1] // HDIM):
        cols = slice(head * HDIM, (head + 1) * HDIM)
        result = mixed(p0[0], p1[0], a, b, head)
        out_ref[:, cols] = jnp.where(early, before[:, cols].astype(jnp.float32), result).astype(
            jnp.bfloat16
        )
        before[:, cols] = result.astype(jnp.bfloat16)


def mix_specs(columns, span_of):
    def place(j, *shape):
        return pl.BlockSpec((1, SPAN) + shape, lambda k, places: (places[2 * span_of(k) + j], 0, 0))

    return [place(0, columns), place(1, columns), place(0, HDIM), place(1, HDIM)]


def mix_last(places, partials, log_totals, span_count):
    columns = partials.shape[-1]
    return pl.pallas_call(
        mix_last_kernel,
        grid_spec=pltpu.PrefetchScalarGridSpec(
            num_scalar_prefetch=1,
            grid=(1,),
            in_specs=mix_specs(columns, lambda k: span_count - 1),
            out_specs=pl.BlockSpec((SPAN, columns), lambda k, places: (0, 0)),
        ),
        out_shape=jax.ShapeDtypeStruct((SPAN, columns), jnp.bfloat16),
        name="mix_last",
    )(places, partials, partials, log_totals, log_totals)


def mix(places, partials, log_totals, carried, span_count):
    columns = partials.shape[-1]
    return pl.pallas_call(
        mix_kernel,
        grid_spec=pltpu.PrefetchScalarGridSpec(
            num_scalar_prefetch=1,
            grid=(span_count,),
            in_specs=mix_specs(columns, lambda k: k)
            + [pl.BlockSpec((SPAN, columns), lambda k, places: (0, 0))],
            out_specs=pl.BlockSpec((SPAN, columns), lambda k, places: (k, 0)),
            scratch_shapes=[pltpu.VMEM((SPAN, columns), jnp.bfloat16)],
        ),
        out_shape=jax.ShapeDtypeStruct((span_count * SPAN, columns), jnp.bfloat16),
        compiler_params=pltpu.CompilerParams(vmem_limit_bytes=VMEM_LIMIT),
        name="mix",
    )(places, partials, partials, log_totals, log_totals, carried)


def shards(queries, neighbours, key_weight, value_weight, neighbour_ids):
    tok_rows, columns = queries.shape
    span_count = neighbour_ids.shape[0]
    seq_count = lax.axis_size("seq")
    block_count = neighbours.shape[0]
    slots = 2 * span_count
    slots_per = (slots + seq_count - 1) // seq_count
    own_index = lax.axis_index("seq")

    all_ids = lax.all_gather(neighbour_ids, "seq", axis=0, tiled=True).reshape(seq_count, slots)
    wanted = all_ids // block_count == own_index
    order = jnp.arange(slots)
    earlier = order[None, :] < order[:, None]
    wanted_rank = jnp.sum(jnp.where(wanted[:, None, :] & earlier[None], 1, 0), axis=-1)
    local = all_ids % block_count

    own_ids = neighbour_ids.reshape(slots)
    own_sources = own_ids // block_count
    own_ranks = slot_ranks(own_sources)

    incoming = passed_along(queries[:SPAN], "seq", -1)
    later = jnp.concatenate([queries[SPAN:], incoming], axis=0).reshape(span_count, SPAN, columns)
    same = queries.reshape(span_count, SPAN, columns)
    early = (jnp.arange(SPAN) < SPAN - 1)[None, :, None]
    windows = jnp.where(early, later, same)

    held = None
    part = slots // slots_per
    every = slots == slots_per * seq_count
    for rank in range(slots_per):
        stored = jnp.sum(jnp.where(wanted & (wanted_rank == rank), local, 0), axis=1)
        outgoing = pick_blocks(stored.astype(jnp.int32), neighbours)
        arrived = lax.all_to_all(outgoing, "seq", split_axis=0, concat_axis=0, tiled=True)
        segment = lax.all_gather(arrived, "tp", axis=1, tiled=True)
        if every:
            sources = jnp.arange(seq_count, dtype=jnp.int32)
            hit = (own_sources[None, :] == sources[:, None]) & (own_ranks == rank)[None, :]
            spans = jnp.sum(jnp.where(hit, order[None, :] // 2, 0), axis=1).astype(jnp.int32)
        else:
            sources = own_sources.astype(jnp.int32)
            spans = (order // 2).astype(jnp.int32)
        held = attend_part(
            sources, spans, segment, windows, key_weight, value_weight, rank * part, slots, held
        )
    partials, log_totals = held
    places = own_ranks * seq_count + own_sources if every else order
    places = places.astype(jnp.int32)
    last = mix_last(places, partials, log_totals, span_count)
    carried = passed_along(last, "seq", 1)
    return mix(places, partials, log_totals, carried, span_count)


def solution(mesh):
    in_specs = (P("seq", "tp"), P("seq", "tp", None), P(None, "tp"), P(None, "tp"), P("seq", None))
    out_specs = P("seq", "tp")
    return jax.shard_map(shards, mesh=mesh, in_specs=in_specs, out_specs=out_specs, check_vma=False)
```

```python
import jax
import jax.numpy as jnp
from jax import lax
from jax.experimental import pallas as pl
from jax.experimental.pallas import tpu as pltpu
from jax.sharding import PartitionSpec as P

HDIM = 128
SPAN = 64
PAIR = 2 * HDIM
INNER = 4
VMEM_LIMIT = 56 * 1024 * 1024


def passed_along(x, axis, by):
    peers = lax.axis_size(axis)
    pairs = [(i, i + by) for i in range(peers) if 0 <= i + by < peers]
    return lax.ppermute(x, axis, pairs)


def swapped(x, axis, offset):
    peers = lax.axis_size(axis)
    return lax.ppermute(x, axis, [(i, i ^ offset) for i in range(peers)])


def slot_ranks(sources):
    positions = sources.shape[-1]
    alike = sources[..., :, None] == sources[..., None, :]
    earlier = jnp.arange(positions)[None, :] < jnp.arange(positions)[:, None]
    return jnp.sum(jnp.where(alike & earlier, 1, 0), axis=-1).astype(jnp.int32)


def windows_kernel(own_ref, next_ref, incoming_ref, out_ref):
    last = pl.program_id(0) == pl.num_programs(0) - 1
    early = lax.broadcasted_iota(jnp.int32, (SPAN, HDIM), 0) < SPAN - 1
    pairs = out_ref.shape[1]
    for pair in range(pairs):
        halves = []
        for head in (2 * pair, 2 * pair + 1):
            cols = slice(head * HDIM, (head + 1) * HDIM)
            later = jnp.where(last, incoming_ref[:, cols], next_ref[:, cols])
            halves.append(
                jnp.where(early, later.astype(jnp.float32), own_ref[:, cols].astype(jnp.float32))
            )
        out_ref[0, pair] = jnp.concatenate(halves, axis=0).astype(jnp.bfloat16).T


def transposed_windows(queries, incoming, span_count):
    columns = queries.shape[-1]
    pairs = columns // PAIR
    return pl.pallas_call(
        windows_kernel,
        grid=(span_count,),
        in_specs=[
            pl.BlockSpec((SPAN, columns), lambda u: (u, 0)),
            pl.BlockSpec((SPAN, columns), lambda u: (jnp.minimum(u + 1, span_count - 1), 0)),
            pl.BlockSpec((SPAN, columns), lambda u: (0, 0)),
        ],
        out_specs=pl.BlockSpec((1, pairs, HDIM, 2 * SPAN), lambda u: (u, 0, 0, 0)),
        out_shape=jax.ShapeDtypeStruct((span_count, pairs, HDIM, 2 * SPAN), jnp.bfloat16),
        compiler_params=pltpu.CompilerParams(vmem_limit_bytes=VMEM_LIMIT),
        name="windows",
    )(queries, queries, incoming)


def pick_kernel(table, *refs):
    outs = refs[-(INNER - 1) :]
    ins = refs[: -(INNER - 1)]
    parts = len(ins) // (INNER - 1)
    for k, out_ref in enumerate(outs):
        for part in range(parts):
            out_ref[0, part] = ins[k * parts + part][0]


def pick_blocks(table, parts):
    ranks = table.shape[-1]
    shape = parts[0].shape[1:]

    def wanted(k):
        return lambda r, table: (table[k, r], 0, 0)

    return pl.pallas_call(
        pick_kernel,
        grid_spec=pltpu.PrefetchScalarGridSpec(
            num_scalar_prefetch=1,
            grid=(ranks,),
            in_specs=[
                pl.BlockSpec((1,) + shape, wanted(k)) for k in range(1, INNER) for _ in parts
            ],
            out_specs=[
                pl.BlockSpec((1, len(parts)) + shape, lambda r, table: (r, 0, 0, 0))
                for _ in range(INNER - 1)
            ],
        ),
        out_shape=[
            jax.ShapeDtypeStruct((ranks, len(parts)) + shape, parts[0].dtype)
            for _ in range(INNER - 1)
        ],
        compiler_params=pltpu.CompilerParams(vmem_limit_bytes=VMEM_LIMIT),
        name="pick_blocks",
    )(table, *(list(parts) * (INNER - 1)))


def attend_kernel(ranks, parts, held, tp_index, picked, spans, *refs):
    cap = INNER * ranks
    own_refs = refs[: ranks * parts]
    got_refs = refs[ranks * parts : ranks * parts + INNER - 1]
    q_refs = refs[ranks * parts + INNER - 1 :][:cap]
    at = ranks * parts + INNER - 1 + cap
    wk_first, wk_odd, wk_even, wv_first, wv_odd, wv_even = refs[at : at + 6]
    out_ref, lse_ref, xt, k_even, v_even, k_odd, v_odd = refs[-7:]
    nlen = own_refs[0].shape[-1]
    step = pl.program_id(0)
    scale = HDIM ** (-0.5)
    low_lanes = lax.broadcasted_iota(jnp.int32, (HDIM, 2 * SPAN), 1) < SPAN

    def project(wk_ref, wv_ref, k_ref, v_ref):
        rows = xt[...]
        k_ref[...] = jnp.dot(rows, wk_ref[...], preferred_element_type=jnp.float32).astype(
            jnp.bfloat16
        )
        v_ref[...] = jnp.dot(rows, wv_ref[...], preferred_element_type=jnp.float32).astype(
            jnp.bfloat16
        )

    def attend(which, k_ref, v_ref):
        cols = slice(which * PAIR, (which + 1) * PAIR)
        none = jnp.zeros((HDIM, 2 * SPAN), jnp.bfloat16)
        for i in range(cap):
            rows = slice(i * nlen, (i + 1) * nlen)
            q = q_refs[i][0, which]
            both = jnp.concatenate(
                [jnp.where(low_lanes, q, none), jnp.where(low_lanes, none, q)], axis=0
            )
            scores = jnp.dot(k_ref[rows, :], both, preferred_element_type=jnp.float32)
            highest = jnp.max(scores, axis=0, keepdims=True)
            exponent = jnp.exp((scores - highest) * scale)
            totals = jnp.sum(exponent, axis=0, keepdims=True)
            weights = (exponent * (1.0 / totals)).astype(jnp.bfloat16)
            blended = lax.dot_general(
                weights,
                v_ref[rows, :],
                (((0,), (0,)), ((), ())),
                preferred_element_type=jnp.float32,
            )
            out_ref[i, :, cols] = jnp.concatenate(
                [blended[:SPAN, :HDIM], blended[SPAN:, HDIM:]], axis=1
            ).astype(jnp.bfloat16)
            lse_ref[i, pl.ds(2 * step + which, 1), :] = highest * scale + jnp.log(totals)

    @pl.when(step == 0)
    def _():
        lse_ref[...] = jnp.zeros_like(lse_ref)
        for i in range(cap):
            if i < ranks:
                pieces = [own_refs[i * parts + part][0] for part in range(parts)]
            else:
                block = got_refs[i // ranks - 1]
                pieces = [block[i % ranks, part] for part in range(parts)]
            if parts == 2:
                lower = tp_index[0] == 0
                pieces = [
                    jnp.where(lower, pieces[0], pieces[1]),
                    jnp.where(lower, pieces[1], pieces[0]),
                ]
            xt[i * nlen : (i + 1) * nlen, :] = jnp.concatenate(pieces, axis=0).T
        project(wk_first, wv_first, k_even, v_even)

    project(wk_odd, wv_odd, k_odd, v_odd)
    attend(0, k_even, v_even)
    project(wk_even, wv_even, k_even, v_even)
    attend(1, k_odd, v_odd)


def attend_part(tp_index, picked, spans, own, got, windows, weights, part_index, slots, held):
    ranks, parts = picked.shape[0], len(own)
    cap = INNER * ranks
    width, nlen = own[0].shape[1:]
    features = width * parts
    span_count, pairs = windows.shape[:2]
    steps = pairs // 2
    stat_rows = max(pairs, 8)

    def own_at(r):
        return lambda t, tp_index, picked, spans: (picked[r], 0, 0)

    def window_at(i):
        return lambda t, tp_index, picked, spans: (spans[i], t, 0, 0)

    in_specs = [pl.BlockSpec((1, width, nlen), own_at(r)) for r in range(ranks) for _ in own]
    operands = list(own) * ranks
    in_specs += [pl.BlockSpec(g.shape, lambda t, *_: (0, 0, 0, 0)) for g in got]
    operands += list(got)
    in_specs += [pl.BlockSpec((1, 2, HDIM, 2 * SPAN), window_at(i)) for i in range(cap)]
    operands += [windows] * cap
    for weight in weights:
        in_specs += [
            pl.BlockSpec((features, PAIR), lambda t, *_: (0, 0)),
            pl.BlockSpec((features, PAIR), lambda t, *_: (0, 2 * t + 1)),
            pl.BlockSpec((features, PAIR), lambda t, *_: (0, jnp.minimum(2 * t + 2, pairs - 1))),
        ]
        operands += [weight] * 3
    aliases = {}
    if held is not None:
        in_specs += [pl.BlockSpec(memory_space=pl.ANY)] * 2
        aliases = {3 + len(operands): 0, 4 + len(operands): 1}
        operands += list(held)
    kv = pltpu.VMEM((cap * nlen, PAIR), jnp.bfloat16)

    def body(*refs):
        attend_kernel(ranks, parts, held, *refs)

    return pl.pallas_call(
        body,
        grid_spec=pltpu.PrefetchScalarGridSpec(
            num_scalar_prefetch=3,
            grid=(steps,),
            in_specs=in_specs,
            out_specs=[
                pl.BlockSpec((cap, SPAN, 2 * PAIR), lambda t, *_: (part_index, 0, t)),
                pl.BlockSpec((cap, stat_rows, 2 * SPAN), lambda t, *_: (part_index, 0, 0)),
            ],
            scratch_shapes=[pltpu.VMEM((cap * nlen, features), jnp.bfloat16), kv, kv, kv, kv],
        ),
        out_shape=[
            jax.ShapeDtypeStruct((slots, SPAN, pairs * PAIR), jnp.bfloat16),
            jax.ShapeDtypeStruct((slots, stat_rows, 2 * SPAN), jnp.float32),
        ],
        input_output_aliases=aliases,
        compiler_params=pltpu.CompilerParams(vmem_limit_bytes=VMEM_LIMIT),
        name="attend_part",
    )(tp_index, picked, spans, *operands)


def first_shares(l0, l1):
    largest = jnp.maximum(l0, l1)
    e0, e1 = jnp.exp(l0 - largest), jnp.exp(l1 - largest)
    return (e0 / (e0 + e1)).T


def mixed(p0, p1, shares, head):
    cols = slice(head * HDIM, (head + 1) * HDIM)
    half = slice((head % 2) * SPAN, (head % 2 + 1) * SPAN)
    share = shares[half, head // 2 : head // 2 + 1]
    return p0[0, :, cols].astype(jnp.float32) * share + p1[0, :, cols].astype(jnp.float32) * (
        1.0 - share
    )


def mix_last_kernel(places, p0, p1, l0, l1, out_ref):
    shares = first_shares(l0[0], l1[0])
    for head in range(out_ref.shape[-1] // HDIM):
        cols = slice(head * HDIM, (head + 1) * HDIM)
        out_ref[:, cols] = mixed(p0, p1, shares, head).astype(jnp.bfloat16)


def mix_kernel(places, p0, p1, l0, l1, carried, out_ref, before):
    @pl.when(pl.program_id(0) == 0)
    def _():
        before[...] = carried[...]

    shares = first_shares(l0[0], l1[0])
    early = lax.broadcasted_iota(jnp.int32, (SPAN, HDIM), 0) < SPAN - 1
    for head in range(out_ref.shape[-1] // HDIM):
        cols = slice(head * HDIM, (head + 1) * HDIM)
        result = mixed(p0, p1, shares, head)
        out_ref[:, cols] = jnp.where(early, before[:, cols].astype(jnp.float32), result).astype(
            jnp.bfloat16
        )
        before[:, cols] = result.astype(jnp.bfloat16)


def mix_specs(partials, log_totals, span_of):
    def place(j, shape):
        return pl.BlockSpec((1,) + shape, lambda k, places: (places[2 * span_of(k) + j], 0, 0))

    rows, stats = partials.shape[1:], log_totals.shape[1:]
    return [place(0, rows), place(1, rows), place(0, stats), place(1, stats)]


def mix_last(places, partials, log_totals, span_count):
    columns = partials.shape[-1]
    return pl.pallas_call(
        mix_last_kernel,
        grid_spec=pltpu.PrefetchScalarGridSpec(
            num_scalar_prefetch=1,
            grid=(1,),
            in_specs=mix_specs(partials, log_totals, lambda k: span_count - 1),
            out_specs=pl.BlockSpec((SPAN, columns), lambda k, places: (0, 0)),
        ),
        out_shape=jax.ShapeDtypeStruct((SPAN, columns), jnp.bfloat16),
        name="mix_last",
    )(places, partials, partials, log_totals, log_totals)


def mix(places, partials, log_totals, carried, span_count):
    columns = partials.shape[-1]
    return pl.pallas_call(
        mix_kernel,
        grid_spec=pltpu.PrefetchScalarGridSpec(
            num_scalar_prefetch=1,
            grid=(span_count,),
            in_specs=mix_specs(partials, log_totals, lambda k: k)
            + [pl.BlockSpec((SPAN, columns), lambda k, places: (0, 0))],
            out_specs=pl.BlockSpec((SPAN, columns), lambda k, places: (k, 0)),
            scratch_shapes=[pltpu.VMEM((SPAN, columns), jnp.bfloat16)],
        ),
        out_shape=jax.ShapeDtypeStruct((span_count * SPAN, columns), jnp.bfloat16),
        compiler_params=pltpu.CompilerParams(vmem_limit_bytes=VMEM_LIMIT),
        name="mix",
    )(places, partials, partials, log_totals, log_totals, carried)


def shards(queries, neighbours, key_weight, value_weight, neighbour_ids):
    span_count = neighbour_ids.shape[0]
    seq_count, tp_count = lax.axis_size("seq"), lax.axis_size("tp")
    block_count = neighbours.shape[0]
    wants = 2 * span_count
    ranks = (wants + seq_count - 1) // seq_count
    outer = seq_count // INNER
    slots = seq_count * ranks
    own_index = lax.axis_index("seq")
    tp_index = lax.axis_index("tp").astype(jnp.int32).reshape(1)

    held_parts = [neighbours]
    for j in range(1, outer):
        low = j & -j
        held_parts.append(swapped(held_parts[j ^ low], "seq", INNER * low))

    def all_features(part):
        if tp_count == 2:
            return [part, swapped(part, "tp", 1)]
        return [lax.all_gather(part, "tp", axis=1, tiled=True)]

    incoming = passed_along(queries[:SPAN], "seq", -1)
    windows = transposed_windows(queries, incoming, span_count)

    all_ids = lax.all_gather(neighbour_ids, "seq", axis=0, tiled=True).reshape(seq_count, wants)
    group_ids = all_ids[own_index ^ jnp.arange(INNER)]
    group_sources = group_ids // block_count
    group_ranks = slot_ranks(group_sources)
    part_sources = own_index ^ (INNER * jnp.arange(outer))
    hit = (group_sources[None, :, None, :] == part_sources[:, None, None, None]) & (
        group_ranks[None, :, None, :] == jnp.arange(ranks)[None, None, :, None]
    )
    table = jnp.sum(jnp.where(hit, (group_ids % block_count)[None, :, None, :], 0), axis=-1)
    table = table.astype(jnp.int32)

    own_ids = neighbour_ids.reshape(wants)
    own_sources = own_ids // block_count
    places = ((own_sources ^ own_index) * ranks + slot_ranks(own_sources)).astype(jnp.int32)
    order = jnp.arange(wants)
    spans = jnp.sum(
        jnp.where(places[None, :] == jnp.arange(slots)[:, None], order[None, :] // 2, 0), axis=1
    ).astype(jnp.int32)
    spans = spans.reshape(outer, INNER * ranks)

    held = None
    for j in range(outer):
        own = all_features(held_parts[j])
        outgoing = pick_blocks(table[j], own)
        got = [swapped(outgoing[k - 1], "seq", k) for k in range(1, INNER)]
        held = attend_part(
            tp_index, table[j, 0], spans[j], own, got, windows,
            (key_weight, value_weight), j, slots, held,
        )
    partials, log_totals = held
    last = mix_last(places, partials, log_totals, span_count)
    carried = passed_along(last, "seq", 1)
    return mix(places, partials, log_totals, carried, span_count)


def solution(mesh):
    in_specs = (P("seq", "tp"), P("seq", "tp", None), P(None, "tp"), P(None, "tp"), P("seq", None))
    out_specs = P("seq", "tp")
    return jax.shard_map(shards, mesh=mesh, in_specs=in_specs, out_specs=out_specs, check_vma=False)
```

```python
import jax
import jax.numpy as jnp
from jax import lax
from jax.experimental import pallas as pl
from jax.experimental.pallas import tpu as pltpu
from jax.sharding import PartitionSpec as P

HDIM = 128
SPAN = 64
PAIR = 2 * HDIM
INNER = 4
VMEM_LIMIT = 56 * 1024 * 1024


def passed_along(x, axis, by):
    peers = lax.axis_size(axis)
    pairs = [(i, i + by) for i in range(peers) if 0 <= i + by < peers]
    return lax.ppermute(x, axis, pairs)


def swapped(x, axis, offset):
    peers = lax.axis_size(axis)
    return lax.ppermute(x, axis, [(i, i ^ offset) for i in range(peers)])


def slot_ranks(sources):
    positions = sources.shape[-1]
    alike = sources[..., :, None] == sources[..., None, :]
    earlier = jnp.arange(positions)[None, :] < jnp.arange(positions)[:, None]
    return jnp.sum(jnp.where(alike & earlier, 1, 0), axis=-1).astype(jnp.int32)


def windows_kernel(own_ref, next_ref, incoming_ref, out_ref):
    last = pl.program_id(0) == pl.num_programs(0) - 1
    early = lax.broadcasted_iota(jnp.int32, (SPAN, HDIM), 0) < SPAN - 1
    pairs = out_ref.shape[1]
    for pair in range(pairs):
        halves = []
        for head in (2 * pair, 2 * pair + 1):
            cols = slice(head * HDIM, (head + 1) * HDIM)
            later = jnp.where(last, incoming_ref[:, cols], next_ref[:, cols])
            halves.append(
                jnp.where(early, later.astype(jnp.float32), own_ref[:, cols].astype(jnp.float32))
            )
        out_ref[0, pair] = jnp.concatenate(halves, axis=0).astype(jnp.bfloat16).T


def transposed_windows(queries, incoming, span_count):
    columns = queries.shape[-1]
    pairs = columns // PAIR
    return pl.pallas_call(
        windows_kernel,
        grid=(span_count,),
        in_specs=[
            pl.BlockSpec((SPAN, columns), lambda u: (u, 0)),
            pl.BlockSpec((SPAN, columns), lambda u: (jnp.minimum(u + 1, span_count - 1), 0)),
            pl.BlockSpec((SPAN, columns), lambda u: (0, 0)),
        ],
        out_specs=pl.BlockSpec((1, pairs, HDIM, 2 * SPAN), lambda u: (u, 0, 0, 0)),
        out_shape=jax.ShapeDtypeStruct((span_count, pairs, HDIM, 2 * SPAN), jnp.bfloat16),
        compiler_params=pltpu.CompilerParams(vmem_limit_bytes=VMEM_LIMIT),
        name="windows",
    )(queries, queries, incoming)


def pick_kernel(count, table, *refs):
    outs = refs[-count:]
    ins = refs[:-count]
    parts = len(ins) // count
    for k, out_ref in enumerate(outs):
        for part in range(parts):
            out_ref[0, part] = ins[k * parts + part][0]


def pick_blocks(table, parts):
    count, ranks = table.shape
    shape = parts[0].shape[1:]

    def wanted(k):
        return lambda r, table: (table[k, r], 0, 0)

    def body(*refs):
        pick_kernel(count, *refs)

    return pl.pallas_call(
        body,
        grid_spec=pltpu.PrefetchScalarGridSpec(
            num_scalar_prefetch=1,
            grid=(ranks,),
            in_specs=[pl.BlockSpec((1,) + shape, wanted(k)) for k in range(count) for _ in parts],
            out_specs=[
                pl.BlockSpec((1, len(parts)) + shape, lambda r, table: (r, 0, 0, 0))
                for _ in range(count)
            ],
        ),
        out_shape=[
            jax.ShapeDtypeStruct((ranks, len(parts)) + shape, parts[0].dtype) for _ in range(count)
        ],
        compiler_params=pltpu.CompilerParams(vmem_limit_bytes=VMEM_LIMIT),
        name="pick_blocks",
    )(table, *(list(parts) * count))


def attend_kernel(cap, piece_of, count, parts, tp_index, picked, spans, *refs):
    x_refs = refs[:count]
    q_refs = refs[count : count + cap]
    wk_first, wk_odd, wk_even, wv_first, wv_odd, wv_even = refs[count + cap : count + cap + 6]
    out_ref, lse_ref, xt, scores_ref, weights_ref, k_even, v_even, k_odd, v_odd = refs[-9:]
    nlen = scores_ref.shape[1]
    step = pl.program_id(0)
    scale = HDIM ** (-0.5)
    low_lanes = lax.broadcasted_iota(jnp.int32, (HDIM, 2 * SPAN), 1) < SPAN

    def project(w_ref, out):
        out[...] = jnp.dot(xt[...], w_ref[...], preferred_element_type=jnp.float32).astype(
            jnp.bfloat16
        )

    def score(which, k_ref):
        none = jnp.zeros((HDIM, 2 * SPAN), jnp.bfloat16)
        for i in range(cap):
            q = q_refs[i][0, which]
            both = jnp.concatenate(
                [jnp.where(low_lanes, q, none), jnp.where(low_lanes, none, q)], axis=0
            )
            scores_ref[i] = jnp.dot(
                k_ref[i * nlen : (i + 1) * nlen, :], both, preferred_element_type=jnp.float32
            )

    def soften(which):
        for i in range(cap):
            scores = scores_ref[i]
            highest = jnp.max(scores, axis=0, keepdims=True)
            exponent = jnp.exp((scores - highest) * scale)
            totals = jnp.sum(exponent, axis=0, keepdims=True)
            weights_ref[i] = (exponent * (1.0 / totals)).astype(jnp.bfloat16)
            lse_ref[i, pl.ds(2 * step + which, 1), :] = highest * scale + jnp.log(totals)

    def blend(which, v_ref):
        cols = slice(which * PAIR, (which + 1) * PAIR)
        for i in range(cap):
            blended = lax.dot_general(
                weights_ref[i],
                v_ref[i * nlen : (i + 1) * nlen, :],
                (((0,), (0,)), ((), ())),
                preferred_element_type=jnp.float32,
            )
            out_ref[i, :, cols] = jnp.concatenate(
                [blended[:SPAN, :HDIM], blended[SPAN:, HDIM:]], axis=1
            ).astype(jnp.bfloat16)

    @pl.when(step == 0)
    def _():
        lse_ref[...] = jnp.zeros_like(lse_ref)
        for i in range(cap):
            pieces = [piece_of(x_refs, i, part) for part in range(parts)]
            if parts == 2:
                lower = tp_index[0] == 0
                pieces = [
                    jnp.where(lower, pieces[0], pieces[1]),
                    jnp.where(lower, pieces[1], pieces[0]),
                ]
            xt[i * nlen : (i + 1) * nlen, :] = jnp.concatenate(pieces, axis=0).T
        project(wk_first, k_even)
        project(wv_first, v_even)

    score(0, k_even)
    project(wk_odd, k_odd)
    soften(0)
    project(wv_odd, v_odd)
    blend(0, v_even)
    score(1, k_odd)
    project(wk_even, k_even)
    soften(1)
    project(wv_even, v_even)
    blend(1, v_odd)


def attend_part(tp_index, picked, spans, own, got, windows, weights, part_index, slots, held):
    ranks, parts = picked.shape[0], len(own)
    cap = spans.shape[0]
    width, nlen = own[0].shape[1:]
    features = width * parts
    pairs = windows.shape[1]
    stat_rows = max(pairs, 8)

    def own_at(r):
        return lambda t, tp_index, picked, spans: (picked[r], 0, 0)

    def window_at(i):
        return lambda t, tp_index, picked, spans: (spans[i], t, 0, 0)

    if got is None:
        in_specs = [pl.BlockSpec(x.shape, lambda t, *_: (0, 0, 0)) for x in own]
        operands = list(own)

        def piece_of(refs, i, part):
            return refs[part][i]

    else:
        in_specs = [pl.BlockSpec((1, width, nlen), own_at(r)) for r in range(ranks) for _ in own]
        operands = list(own) * ranks
        in_specs += [pl.BlockSpec(g.shape, lambda t, *_: (0, 0, 0, 0)) for g in got]
        operands += list(got)

        def piece_of(refs, i, part):
            if i < ranks:
                return refs[i * parts + part][0]
            return refs[ranks * parts + i // ranks - 1][i % ranks, part]

    count = len(operands)
    in_specs += [pl.BlockSpec((1, 2, HDIM, 2 * SPAN), window_at(i)) for i in range(cap)]
    operands += [windows] * cap
    for weight in weights:
        in_specs += [
            pl.BlockSpec((features, PAIR), lambda t, *_: (0, 0)),
            pl.BlockSpec((features, PAIR), lambda t, *_: (0, 2 * t + 1)),
            pl.BlockSpec((features, PAIR), lambda t, *_: (0, jnp.minimum(2 * t + 2, pairs - 1))),
        ]
        operands += [weight] * 3
    aliases = {}
    if held is not None:
        in_specs += [pl.BlockSpec(memory_space=pl.ANY)] * 2
        aliases = {3 + len(operands): 0, 4 + len(operands): 1}
        operands += list(held)
    kv = pltpu.VMEM((cap * nlen, PAIR), jnp.bfloat16)

    def body(*refs):
        attend_kernel(cap, piece_of, count, parts, *refs)

    return pl.pallas_call(
        body,
        grid_spec=pltpu.PrefetchScalarGridSpec(
            num_scalar_prefetch=3,
            grid=(pairs // 2,),
            in_specs=in_specs,
            out_specs=[
                pl.BlockSpec((cap, SPAN, 2 * PAIR), lambda t, *_: (part_index, 0, t)),
                pl.BlockSpec((cap, stat_rows, 2 * SPAN), lambda t, *_: (part_index, 0, 0)),
            ],
            scratch_shapes=[
                pltpu.VMEM((cap * nlen, features), jnp.bfloat16),
                pltpu.VMEM((cap, nlen, 2 * SPAN), jnp.float32),
                pltpu.VMEM((cap, nlen, 2 * SPAN), jnp.bfloat16),
                kv, kv, kv, kv,
            ],
        ),
        out_shape=[
            jax.ShapeDtypeStruct((slots, SPAN, pairs * PAIR), jnp.bfloat16),
            jax.ShapeDtypeStruct((slots, stat_rows, 2 * SPAN), jnp.float32),
        ],
        input_output_aliases=aliases,
        compiler_params=pltpu.CompilerParams(vmem_limit_bytes=VMEM_LIMIT),
        name="attend_part",
    )(tp_index, picked, spans, *operands)


def first_shares(l0, l1):
    largest = jnp.maximum(l0, l1)
    e0, e1 = jnp.exp(l0 - largest), jnp.exp(l1 - largest)
    return (e0 / (e0 + e1)).T


def mixed(p0, p1, shares, head):
    cols = slice(head * HDIM, (head + 1) * HDIM)
    half = slice((head % 2) * SPAN, (head % 2 + 1) * SPAN)
    share = shares[half, head // 2 : head // 2 + 1]
    return p0[0, :, cols].astype(jnp.float32) * share + p1[0, :, cols].astype(jnp.float32) * (
        1.0 - share
    )


def mix_last_kernel(places, p0, p1, l0, l1, out_ref):
    shares = first_shares(l0[0], l1[0])
    for head in range(out_ref.shape[-1] // HDIM):
        cols = slice(head * HDIM, (head + 1) * HDIM)
        out_ref[:, cols] = mixed(p0, p1, shares, head).astype(jnp.bfloat16)


def mix_kernel(places, *refs):
    ins, (out_ref, before) = refs[:-2], refs[-2:]
    heads = out_ref.shape[-1] // HDIM
    tile = 16
    late = lax.broadcasted_iota(jnp.int32, (tile, HDIM), 0) == tile - 1
    for n in range(len(ins) // 4):
        p0, p1, l0, l1 = ins[4 * n : 4 * n + 4]
        shares = first_shares(l0[0], l1[0])
        top = n * SPAN
        cut = top + SPAN - tile
        out_ref[top:cut, :] = before[: SPAN - tile, :]
        for head in range(heads):
            cols = slice(head * HDIM, (head + 1) * HDIM)
            result = mixed(p0, p1, shares, head)
            out_ref[cut : cut + tile, cols] = jnp.where(
                late, result[SPAN - tile :], before[SPAN - tile :, cols].astype(jnp.float32)
            ).astype(jnp.bfloat16)
            before[:, cols] = result.astype(jnp.bfloat16)


def mix_specs(partials, log_totals, span_of):
    def place(j, shape):
        return pl.BlockSpec((1,) + shape, lambda k, places: (places[2 * span_of(k) + j], 0, 0))

    rows, stats = partials.shape[1:], log_totals.shape[1:]
    return [place(0, rows), place(1, rows), place(0, stats), place(1, stats)]


def mix_last(places, partials, log_totals, span_count):
    columns = partials.shape[-1]
    return pl.pallas_call(
        mix_last_kernel,
        grid_spec=pltpu.PrefetchScalarGridSpec(
            num_scalar_prefetch=1,
            grid=(1,),
            in_specs=mix_specs(partials, log_totals, lambda k: span_count - 1),
            out_specs=pl.BlockSpec((SPAN, columns), lambda k, places: (0, 0)),
        ),
        out_shape=jax.ShapeDtypeStruct((SPAN, columns), jnp.bfloat16),
        name="mix_last",
    )(places, partials, partials, log_totals, log_totals)


def mix(places, partials, log_totals, span_count):
    columns = partials.shape[-1]
    per = 2
    in_specs = []
    for n in range(per):
        in_specs += mix_specs(partials, log_totals, lambda k, n=n: per * k + n)
    return pl.pallas_call(
        mix_kernel,
        grid_spec=pltpu.PrefetchScalarGridSpec(
            num_scalar_prefetch=1,
            grid=(span_count // per,),
            in_specs=in_specs,
            out_specs=pl.BlockSpec((per * SPAN, columns), lambda k, places: (k, 0)),
            scratch_shapes=[pltpu.VMEM((SPAN, columns), jnp.bfloat16)],
        ),
        out_shape=jax.ShapeDtypeStruct((span_count * SPAN, columns), jnp.bfloat16),
        compiler_params=pltpu.CompilerParams(vmem_limit_bytes=VMEM_LIMIT),
        name="mix",
    )(places, *([partials, partials, log_totals, log_totals] * per))


def head_kernel(carried, rows, out_ref):
    early = lax.broadcasted_iota(jnp.int32, out_ref.shape, 0) < SPAN - 1
    out_ref[...] = jnp.where(
        early, carried[...].astype(jnp.float32), rows[...].astype(jnp.float32)
    ).astype(jnp.bfloat16)


def with_head(carried, mixed_rows):
    spec = pl.BlockSpec((SPAN, mixed_rows.shape[-1]), lambda k: (0, 0))
    return pl.pallas_call(
        head_kernel,
        grid=(1,),
        in_specs=[spec, spec],
        out_specs=spec,
        out_shape=jax.ShapeDtypeStruct(mixed_rows.shape, mixed_rows.dtype),
        input_output_aliases={1: 0},
        name="with_head",
    )(carried, mixed_rows)


def after(values, *others):
    return lax.optimization_barrier((values, others))[0]


def shards(queries, neighbours, key_weight, value_weight, neighbour_ids):
    span_count = neighbour_ids.shape[0]
    seq_count, tp_count = lax.axis_size("seq"), lax.axis_size("tp")
    block_count = neighbours.shape[0]
    wants = 2 * span_count
    ranks = (wants + seq_count - 1) // seq_count
    outer = seq_count // INNER
    slots = seq_count * ranks
    own_index = lax.axis_index("seq")
    tp_index = lax.axis_index("tp").astype(jnp.int32).reshape(1)

    own_ids = neighbour_ids.reshape(wants)
    group_ids = jnp.stack([own_ids] + [swapped(own_ids, "seq", k) for k in range(1, INNER)])
    incoming = passed_along(queries[:SPAN], "seq", -1)

    held_parts = [neighbours]
    for j in range(1, outer):
        low = j & -j
        held_parts.append(swapped(held_parts[j ^ low], "seq", INNER * low))

    def all_features(part):
        if tp_count == 2:
            return [part, swapped(part, "tp", 1)]
        return [lax.all_gather(part, "tp", axis=1, tiled=True)]

    windows = transposed_windows(queries, incoming, span_count)

    group_sources = group_ids // block_count
    group_ranks = slot_ranks(group_sources)
    part_sources = own_index ^ (INNER * jnp.arange(outer))
    hit = (group_sources[None, :, None, :] == part_sources[:, None, None, None]) & (
        group_ranks[None, :, None, :] == jnp.arange(ranks)[None, None, :, None]
    )
    table = jnp.sum(jnp.where(hit, (group_ids % block_count)[None, :, None, :], 0), axis=-1)
    table = table.astype(jnp.int32)

    own_sources = own_ids // block_count
    places = ((own_sources ^ own_index) * ranks + slot_ranks(own_sources)).astype(jnp.int32)
    order = jnp.arange(wants)
    spans = jnp.sum(
        jnp.where(places[None, :] == jnp.arange(slots)[:, None], order[None, :] // 2, 0), axis=1
    ).astype(jnp.int32)
    spans = spans.reshape(outer, INNER * ranks)

    weights = (key_weight, value_weight)

    def attend(j, own, got, held):
        return attend_part(
            tp_index, table[j, 0], spans[j], own, got, windows, weights, j, slots, held
        )

    def features_first(j, *others):
        own = all_features(held_parts[j])
        outgoing = pick_blocks(table[j, 1:], after(own, *others))
        return own, [swapped(outgoing[k - 1], "seq", k) for k in range(1, INNER)]

    def wanted_first(j, *others):
        outgoing = pick_blocks(table[j], after([held_parts[j]], *others))
        wanted = [outgoing[0]] + [swapped(outgoing[k], "seq", k) for k in range(1, INNER)]
        return outgoing, jnp.concatenate([w[:, 0] for w in wanted], axis=0)

    own, got = features_first(0, windows)
    picked, wanted = wanted_first(2)
    held = attend(0, own, after(got, picked), None)
    later = [(2, all_features(wanted))]
    for j in range(3, outer):
        _, wanted = wanted_first(j, held)
        later.append((j, all_features(wanted)))
    own, got = features_first(1, held)
    held = attend(1, own, after(got, wanted), held)
    for j, own in later:
        held = attend(j, own, None, held)

    partials, log_totals = held
    last = mix_last(places, partials, log_totals, span_count)
    carried = passed_along(last, "seq", 1)
    rows = mix(places, partials, log_totals, span_count)
    return with_head(carried, rows)


def solution(mesh):
    in_specs = (P("seq", "tp"), P("seq", "tp", None), P(None, "tp"), P(None, "tp"), P("seq", None))
    out_specs = P("seq", "tp")
    return jax.shard_map(shards, mesh=mesh, in_specs=in_specs, out_specs=out_specs, check_vma=False)
```

```python
import jax
import jax.numpy as jnp
from jax import lax
from jax.experimental import pallas as pl
from jax.experimental.pallas import tpu as pltpu
from jax.sharding import PartitionSpec as P

HDIM = 128
SPAN = 64
PAIR = 2 * HDIM
INNER = 4
LANES = 128
VMEM_LIMIT = 56 * 1024 * 1024


def passed_along(x, axis, by):
    peers = lax.axis_size(axis)
    pairs = [(i, i + by) for i in range(peers) if 0 <= i + by < peers]
    return lax.ppermute(x, axis, pairs)


def swapped(x, axis, offset):
    peers = lax.axis_size(axis)
    return lax.ppermute(x, axis, [(i, i ^ offset) for i in range(peers)])


def slot_ranks(sources):
    positions = sources.shape[-1]
    alike = sources[..., :, None] == sources[..., None, :]
    earlier = jnp.arange(positions)[None, :] < jnp.arange(positions)[:, None]
    return jnp.sum(jnp.where(alike & earlier, 1, 0), axis=-1).astype(jnp.int32)


def windows_kernel(own_ref, next_ref, incoming_ref, out_ref):
    spans = out_ref.shape[0]
    last = pl.program_id(0) == pl.num_programs(0) - 1
    tile = 16
    cut = SPAN - tile
    late = lax.broadcasted_iota(jnp.int32, (tile, out_ref.shape[-1]), 0) == tile - 1
    for n in range(spans):
        if n + 1 < spans:
            later = own_ref[(n + 1) * SPAN : (n + 2) * SPAN, :]
        else:
            later = jnp.where(last, incoming_ref[...], next_ref[...])
        out_ref[n, :cut, :] = later[:cut]
        own = own_ref[n * SPAN + cut : (n + 1) * SPAN, :]
        out_ref[n, cut:, :] = jnp.where(
            late, own.astype(jnp.float32), later[cut:].astype(jnp.float32)
        ).astype(jnp.bfloat16)


def span_windows(queries, incoming, span_count):
    columns = queries.shape[-1]
    per = 4
    steps = span_count // per
    return pl.pallas_call(
        windows_kernel,
        grid=(steps,),
        in_specs=[
            pl.BlockSpec((per * SPAN, columns), lambda u: (u, 0)),
            pl.BlockSpec(
                (SPAN, columns), lambda u: (jnp.minimum(per * (u + 1), span_count - 1), 0)
            ),
            pl.BlockSpec((SPAN, columns), lambda u: (0, 0)),
        ],
        out_specs=pl.BlockSpec((per, SPAN, columns), lambda u: (u, 0, 0)),
        out_shape=jax.ShapeDtypeStruct((span_count, SPAN, columns), jnp.bfloat16),
        compiler_params=pltpu.CompilerParams(vmem_limit_bytes=VMEM_LIMIT),
        name="windows",
    )(queries, queries, incoming)


def pick_kernel(count, which, table, *refs):
    options = len(refs) - count - 3
    sources, outs = refs[:options], refs[options : options + count]
    held, in_sems, out_sems = refs[-3:]
    ranks = table.shape[1]
    places = [(k, r) for k in range(count) for r in range(ranks)]

    def fetch(source, n):
        return pltpu.make_async_copy(source.at[table[places[n]]], held.at[n], in_sems.at[n])

    for option, source in enumerate(sources):

        @pl.when(which[0] == option)
        def _(source=source):
            for n in range(len(places)):
                fetch(source, n).start()

    stores = []
    for n, (k, r) in enumerate(places):
        fetch(sources[0], n).wait()
        stores.append(pltpu.make_async_copy(held.at[n], outs[k].at[r], out_sems.at[n]))
        stores[-1].start()
    for store in stores:
        store.wait()


def pick_blocks(which, table, sources):
    count, ranks = table.shape
    shape = sources[0].shape[1:]
    copies = count * ranks

    def body(*refs):
        pick_kernel(count, *refs)

    return pl.pallas_call(
        body,
        grid_spec=pltpu.PrefetchScalarGridSpec(
            num_scalar_prefetch=2,
            grid=(1,),
            in_specs=[pl.BlockSpec(memory_space=pl.ANY)] * len(sources),
            out_specs=[pl.BlockSpec(memory_space=pl.ANY)] * count,
            scratch_shapes=[
                pltpu.VMEM((copies,) + shape, sources[0].dtype),
                pltpu.SemaphoreType.DMA((copies,)),
                pltpu.SemaphoreType.DMA((copies,)),
            ],
        ),
        out_shape=[jax.ShapeDtypeStruct((ranks,) + shape, sources[0].dtype) for _ in range(count)],
        compiler_params=pltpu.CompilerParams(vmem_limit_bytes=VMEM_LIMIT),
        name="pick_blocks",
    )(which, table, *sources)


def attend_kernel(cap, parts, steps, tp_index, spans, *refs):
    x_refs = refs[:parts]
    q_ref, wk_first, wk_next, wv_first, wv_next = refs[parts : parts + 5]
    out_ref, lse_ref, x_all, weights_ref, k_even, v_even, k_odd, v_odd = refs[-8:]
    nlen = x_refs[0].shape[-1]
    width = x_refs[0].shape[1]
    columns = q_ref.shape[-1]
    pairs = columns // PAIR
    step = pl.program_id(0)
    scale = HDIM ** (-0.5)
    lanes = lax.broadcasted_iota(jnp.int32, (SPAN, LANES), 1)
    rows = 2 * SPAN

    def two_slots(n):
        return pl.ds(pl.multiple_of(n * 2 * nlen, 2 * nlen), 2 * nlen)

    def project(n, w_ref, out):
        out[:, two_slots(n)] = jnp.dot(
            w_ref[...], x_all[:, two_slots(n)], preferred_element_type=jnp.float32
        ).astype(jnp.bfloat16)

    def window(slot, pair):
        q = q_ref[spans[slot], :, pair * PAIR : (pair + 1) * PAIR]
        none = jnp.zeros((SPAN, HDIM), jnp.bfloat16)
        upper = jnp.concatenate([q[:, :HDIM], none], axis=1)
        lower = jnp.concatenate([none, q[:, HDIM:]], axis=1)
        return [upper, lower]

    def soften(n, pair, both):
        for a in range(2):
            scores = both[a * rows : (a + 1) * rows, a * nlen : (a + 1) * nlen]
            highest = jnp.max(scores, axis=1, keepdims=True)
            exponent = jnp.exp((scores - highest) * scale)
            totals = jnp.sum(exponent, axis=1, keepdims=True)
            weights_ref[pair, a * rows : (a + 1) * rows, a * nlen : (a + 1) * nlen] = (
                exponent * (1.0 / totals)
            ).astype(jnp.bfloat16)
            lse = highest * scale + jnp.log(totals)
            at = pairs * step + pair
            held = jnp.where(lanes == at, lse[:SPAN], lse_ref[2 * n + a])
            lse_ref[2 * n + a] = jnp.where(lanes == LANES // 8 + at, lse[SPAN:], held)

    def attend(n, k_now, v_now, between):
        scores = []
        for pair in range(pairs):
            q = jnp.concatenate(window(2 * n, pair) + window(2 * n + 1, pair), axis=0)
            keys = k_now[pair * PAIR : (pair + 1) * PAIR, two_slots(n)]
            scores.append(jnp.dot(q, keys, preferred_element_type=jnp.float32))
        between[0]()
        for pair in range(pairs):
            soften(n, pair, scores[pair])
        between[1]()
        for pair in range(pairs):
            cols = slice(pair * PAIR, (pair + 1) * PAIR)
            blended = lax.dot_general(
                weights_ref[pair],
                v_now[cols, two_slots(n)],
                (((1,), (1,)), ((), ())),
                preferred_element_type=jnp.float32,
            )
            for a in range(2):
                top = a * rows
                out_ref[2 * n + a, :, cols] = jnp.concatenate(
                    [blended[top : top + SPAN, :HDIM], blended[top + SPAN : top + rows, HDIM:]],
                    axis=1,
                ).astype(jnp.bfloat16)

    def over_slots(body):
        def one(n, carry):
            body(n)
            return carry

        lax.fori_loop(0, cap // 2, one, 0)

    @pl.when(step == 0)
    def _():
        lse_ref[...] = jnp.zeros_like(lse_ref)
        weights_ref[...] = jnp.zeros_like(weights_ref)
        for part, x_ref in enumerate(x_refs):
            top = 0
            if parts == 2:
                top = pl.multiple_of((tp_index[0] if part == 0 else 1 - tp_index[0]) * width, 16)
            for i in range(cap):
                x_all[pl.ds(top, width), i * nlen : (i + 1) * nlen] = x_ref[i]

        def first(n):
            project(n, wk_first, k_even)
            project(n, wv_first, v_even)

        over_slots(first)

    def work(k_now, v_now, k_later, v_later):
        def body(n):
            between = [
                lambda: project(n, wk_next, k_later),
                lambda: project(n, wv_next, v_later),
            ]
            attend(n, k_now, v_now, between)

        over_slots(body)

    def finish(k_now, v_now):
        over_slots(lambda n: attend(n, k_now, v_now, [lambda: None] * 2))

    if steps > 1:
        pl.when((step < steps - 1) & (step % 2 == 0))(lambda: work(k_even, v_even, k_odd, v_odd))
    if steps > 2:
        pl.when((step < steps - 1) & (step % 2 == 1))(lambda: work(k_odd, v_odd, k_even, v_even))
    ends = (k_even, v_even) if steps % 2 == 1 else (k_odd, v_odd)
    pl.when(step == steps - 1)(lambda: finish(*ends))


def attend_part(tp_index, spans, blocks, windows, weights, part_index, slots, held):
    parts, cap = len(blocks), spans.shape[0]
    width, nlen = blocks[0].shape[1:]
    features = width * parts
    columns = 2 * PAIR
    steps = windows.shape[-1] // columns

    in_specs = [pl.BlockSpec(x.shape, lambda t, *_: (0, 0, 0)) for x in blocks]
    in_specs += [pl.BlockSpec((windows.shape[0], SPAN, columns), lambda t, *_: (0, 0, t))]
    operands = list(blocks) + [windows]
    for weight in weights:
        in_specs += [
            pl.BlockSpec((columns, features), lambda t, *_: (0, 0)),
            pl.BlockSpec((columns, features), lambda t, *_: (jnp.minimum(t + 1, steps - 1), 0)),
        ]
        operands += [weight] * 2
    aliases = {}
    if held is not None:
        in_specs += [pl.BlockSpec(memory_space=pl.ANY)] * 2
        aliases = {2 + len(operands): 0, 3 + len(operands): 1}
        operands += list(held)
    kv = pltpu.VMEM((columns, cap * nlen), jnp.bfloat16)

    def body(*refs):
        attend_kernel(cap, parts, steps, *refs)

    return pl.pallas_call(
        body,
        grid_spec=pltpu.PrefetchScalarGridSpec(
            num_scalar_prefetch=2,
            grid=(steps,),
            in_specs=in_specs,
            out_specs=[
                pl.BlockSpec((cap, SPAN, columns), lambda t, *_: (part_index, 0, t)),
                pl.BlockSpec((cap, SPAN, LANES), lambda t, *_: (part_index, 0, 0)),
            ],
            scratch_shapes=[
                pltpu.VMEM((features, cap * nlen), jnp.bfloat16),
                pltpu.VMEM((2, 4 * SPAN, 2 * nlen), jnp.bfloat16),
                kv, kv, kv, kv,
            ],
        ),
        out_shape=[
            jax.ShapeDtypeStruct((slots,) + windows.shape[1:], jnp.bfloat16),
            jax.ShapeDtypeStruct((slots, SPAN, LANES), jnp.float32),
        ],
        input_output_aliases=aliases,
        compiler_params=pltpu.CompilerParams(vmem_limit_bytes=VMEM_LIMIT),
        name="attend_part",
    )(tp_index, spans, *operands)


def spread_matrix(columns):
    per = LANES // 8
    row = lax.broadcasted_iota(jnp.int32, (4 * per, columns), 0)
    head = lax.broadcasted_iota(jnp.int32, (4 * per, columns), 1) // HDIM
    own = 2 * (row % per) + (row // per) % 2
    return jnp.where(head == own, 1.0, 0.0).astype(jnp.bfloat16)


def first_shares(l0, l1):
    largest = jnp.maximum(l0, l1)
    e0, e1 = jnp.exp(l0 - largest), jnp.exp(l1 - largest)
    share = e0 / (e0 + e1)
    high = share.astype(jnp.bfloat16).astype(jnp.float32)
    low = pltpu.roll(share - high, LANES // 4, 1)
    lanes = lax.broadcasted_iota(jnp.int32, share.shape, 1)
    return jnp.where(lanes < LANES // 4, high, low).astype(jnp.bfloat16)[:, : LANES // 2]


def mixed(p0, p1, shares, spread, cols):
    share = jnp.dot(shares, spread[:, cols], preferred_element_type=jnp.float32)
    return p0[0, :, cols].astype(jnp.float32) * share + p1[0, :, cols].astype(jnp.float32) * (
        1.0 - share
    )


def mix_last_kernel(places, p0, p1, l0, l1, out_ref, spread):
    spread[...] = spread_matrix(out_ref.shape[-1])
    shares = first_shares(l0[0], l1[0])
    for pair in range(out_ref.shape[-1] // PAIR):
        cols = slice(pair * PAIR, (pair + 1) * PAIR)
        out_ref[:, cols] = mixed(p0, p1, shares, spread, cols).astype(jnp.bfloat16)


def mix_kernel(places, *refs):
    ins, (out_ref, before, spread) = refs[:-3], refs[-3:]
    tile = 16
    late = lax.broadcasted_iota(jnp.int32, (tile, PAIR), 0) == tile - 1

    @pl.when(pl.program_id(0) == 0)
    def _():
        spread[...] = spread_matrix(out_ref.shape[-1])

    for n in range(len(ins) // 4):
        p0, p1, l0, l1 = ins[4 * n : 4 * n + 4]
        shares = first_shares(l0[0], l1[0])
        top = n * SPAN
        cut = top + SPAN - tile
        out_ref[top:cut, :] = before[: SPAN - tile, :]
        for pair in range(out_ref.shape[-1] // PAIR):
            cols = slice(pair * PAIR, (pair + 1) * PAIR)
            result = mixed(p0, p1, shares, spread, cols)
            out_ref[cut : cut + tile, cols] = jnp.where(
                late, result[SPAN - tile :], before[SPAN - tile :, cols].astype(jnp.float32)
            ).astype(jnp.bfloat16)
            before[:, cols] = result.astype(jnp.bfloat16)


def mix_specs(partials, log_totals, span_of):
    def place(j, shape):
        return pl.BlockSpec((1,) + shape, lambda k, places: (places[2 * span_of(k) + j], 0, 0))

    rows, stats = partials.shape[1:], log_totals.shape[1:]
    return [place(0, rows), place(1, rows), place(0, stats), place(1, stats)]


def mix_last(places, partials, log_totals, span_count):
    columns = partials.shape[-1]
    return pl.pallas_call(
        mix_last_kernel,
        grid_spec=pltpu.PrefetchScalarGridSpec(
            num_scalar_prefetch=1,
            grid=(1,),
            in_specs=mix_specs(partials, log_totals, lambda k: span_count - 1),
            out_specs=pl.BlockSpec((SPAN, columns), lambda k, places: (0, 0)),
            scratch_shapes=[pltpu.VMEM((LANES // 2, columns), jnp.bfloat16)],
        ),
        out_shape=jax.ShapeDtypeStruct((SPAN, columns), jnp.bfloat16),
        name="mix_last",
    )(places, partials, partials, log_totals, log_totals)


def mix(places, partials, log_totals, span_count):
    columns = partials.shape[-1]
    per = 4
    in_specs = []
    for n in range(per):
        in_specs += mix_specs(partials, log_totals, lambda k, n=n: per * k + n)
    return pl.pallas_call(
        mix_kernel,
        grid_spec=pltpu.PrefetchScalarGridSpec(
            num_scalar_prefetch=1,
            grid=(span_count // per,),
            in_specs=in_specs,
            out_specs=pl.BlockSpec((per * SPAN, columns), lambda k, places: (k, 0)),
            scratch_shapes=[
                pltpu.VMEM((SPAN, columns), jnp.bfloat16),
                pltpu.VMEM((LANES // 2, columns), jnp.bfloat16),
            ],
        ),
        out_shape=jax.ShapeDtypeStruct((span_count * SPAN, columns), jnp.bfloat16),
        compiler_params=pltpu.CompilerParams(vmem_limit_bytes=VMEM_LIMIT),
        name="mix",
    )(places, *([partials, partials, log_totals, log_totals] * per))


def head_kernel(carried, rows, out_ref):
    early = lax.broadcasted_iota(jnp.int32, out_ref.shape, 0) < SPAN - 1
    out_ref[...] = jnp.where(
        early, carried[...].astype(jnp.float32), rows[...].astype(jnp.float32)
    ).astype(jnp.bfloat16)


def with_head(carried, mixed_rows):
    spec = pl.BlockSpec((SPAN, mixed_rows.shape[-1]), lambda k: (0, 0))
    return pl.pallas_call(
        head_kernel,
        grid=(1,),
        in_specs=[spec, spec],
        out_specs=spec,
        out_shape=jax.ShapeDtypeStruct(mixed_rows.shape, mixed_rows.dtype),
        input_output_aliases={1: 0},
        name="with_head",
    )(carried, mixed_rows)


def after(values, *others):
    return lax.optimization_barrier((values, others))[0]


def shards(queries, neighbours, key_weight, value_weight, neighbour_ids):
    span_count = neighbour_ids.shape[0]
    seq_count, tp_count = lax.axis_size("seq"), lax.axis_size("tp")
    block_count = neighbours.shape[0]
    wants = 2 * span_count
    ranks = (wants + seq_count - 1) // seq_count
    outer = seq_count // INNER
    slots = seq_count * ranks
    own_index = lax.axis_index("seq")
    tp_index = lax.axis_index("tp").astype(jnp.int32).reshape(1)

    own_ids = neighbour_ids.reshape(wants)
    group_ids = jnp.stack([own_ids] + [swapped(own_ids, "seq", k) for k in range(1, INNER)])
    incoming = passed_along(queries[:SPAN], "seq", -1)

    def all_features(part):
        if tp_count == 2:
            return [part, swapped(part, "tp", 1)]
        return [lax.all_gather(part, "tp", axis=1, tiled=True)]

    group_sources = group_ids // block_count
    group_ranks = slot_ranks(group_sources)
    part_sources = own_index ^ (INNER * jnp.arange(outer))
    hit = (group_sources[None, :, None, :] == part_sources[:, None, None, None]) & (
        group_ranks[None, :, None, :] == jnp.arange(ranks)[None, None, :, None]
    )
    table = jnp.sum(jnp.where(hit, (group_ids % block_count)[None, :, None, :], 0), axis=-1)
    table = table.astype(jnp.int32)

    own_sources = own_ids // block_count
    places = ((own_sources ^ own_index) * ranks + slot_ranks(own_sources)).astype(jnp.int32)
    order = jnp.arange(wants)
    spans = jnp.sum(
        jnp.where(places[None, :] == jnp.arange(slots)[:, None], order[None, :] // 2, 0), axis=1
    ).astype(jnp.int32)
    spans = spans.reshape(outer, INNER * ranks)

    def along(x, offset, senders):
        pairs = [(i, i ^ offset) for i in range(seq_count) if i // INNER in senders]
        return lax.ppermute(x, "seq", pairs)

    first = jnp.zeros((1,), jnp.int32)
    held_parts = [([neighbours], first)]
    near = swapped(neighbours, "seq", INNER)
    if outer == 4:
        across = along(neighbours, 3 * INNER, (1, 2))

    def fetch(j, *others):
        sources, which = held_parts[j]
        picked = pick_blocks(which, after(table[j], *others), sources)
        wanted = [picked[0]] + [swapped(picked[k], "seq", k) for k in range(1, INNER)]
        return picked, jnp.concatenate(wanted, axis=0)

    picked, wanted = fetch(0)
    weights = tuple(after(w, picked).T for w in (key_weight, value_weight))

    if outer == 4:
        near, across = after((near, across), weights)
        outer_index = own_index // INNER
        inside = ((outer_index == 1) | (outer_index == 2)).astype(jnp.int32).reshape(1)
        second = along(near, 3 * INNER, (1, 2))
        outward = along(across, INNER, (1, 2))
        third = along(second, INNER, (1, 2))
        held_parts += [([near], first), ([outward, second], inside), ([third, across], inside)]
    else:
        held_parts.append(([near], first))
        for j in range(2, outer):
            low = j & -j
            part = swapped(held_parts[j ^ low][0][0], "seq", INNER * low)
            held_parts.append(([part], first))

    def attend(j, blocks, held, *others):
        return attend_part(
            tp_index, after(spans[j], *others), blocks, windows, weights, j, slots, held
        )

    held = None
    blocks = [all_features(wanted)]
    picked, wanted = fetch(1, wanted)
    windows = span_windows(after(queries, picked), incoming, span_count)
    for j in range(2, outer):
        blocks.append(all_features(wanted))
        picked, wanted_next = fetch(j, windows if held is None else held)
        held = attend(j - 2, blocks[j - 2], held, picked, wanted)
        wanted = wanted_next
    blocks.append(all_features(wanted))
    held = attend(outer - 2, blocks[outer - 2], held, wanted)
    held = attend(outer - 1, blocks[outer - 1], held)

    partials, log_totals = held
    last = mix_last(places, partials, log_totals, span_count)
    carried = passed_along(last, "seq", 1)
    rows = mix(places, partials, log_totals, span_count)
    return with_head(carried, rows)


def solution(mesh):
    in_specs = (P("seq", "tp"), P("seq", "tp", None), P(None, "tp"), P(None, "tp"), P("seq", None))
    out_specs = P("seq", "tp")
    return jax.shard_map(shards, mesh=mesh, in_specs=in_specs, out_specs=out_specs, check_vma=False)
```

```python
import jax
import jax.numpy as jnp
from jax import lax
from jax.experimental import pallas as pl
from jax.experimental.pallas import tpu as pltpu
from jax.sharding import PartitionSpec as P

HDIM = 128
SPAN = 64
PAIR = 2 * HDIM
INNER = 4
LANES = 128
VMEM_LIMIT = 56 * 1024 * 1024


def passed_along(x, axis, by):
    peers = lax.axis_size(axis)
    pairs = [(i, i + by) for i in range(peers) if 0 <= i + by < peers]
    return lax.ppermute(x, axis, pairs)


def swapped(x, axis, offset):
    peers = lax.axis_size(axis)
    return lax.ppermute(x, axis, [(i, i ^ offset) for i in range(peers)])


def slot_ranks(sources):
    positions = sources.shape[-1]
    alike = sources[..., :, None] == sources[..., None, :]
    earlier = jnp.arange(positions)[None, :] < jnp.arange(positions)[:, None]
    return jnp.sum(jnp.where(alike & earlier, 1, 0), axis=-1).astype(jnp.int32)


def windows_kernel(own_ref, next_ref, incoming_ref, out_ref):
    spans = out_ref.shape[0]
    last = pl.program_id(0) == pl.num_programs(0) - 1
    tile = 16
    cut = SPAN - tile
    late = lax.broadcasted_iota(jnp.int32, (tile, out_ref.shape[-1]), 0) == tile - 1
    for n in range(spans):
        if n + 1 < spans:
            later = own_ref[(n + 1) * SPAN : (n + 2) * SPAN, :]
        else:
            later = jnp.where(last, incoming_ref[...], next_ref[...])
        out_ref[n, :cut, :] = later[:cut]
        own = own_ref[n * SPAN + cut : (n + 1) * SPAN, :]
        out_ref[n, cut:, :] = jnp.where(
            late, own.astype(jnp.float32), later[cut:].astype(jnp.float32)
        ).astype(jnp.bfloat16)


def span_windows(queries, incoming, span_count):
    columns = queries.shape[-1]
    per = 4
    steps = span_count // per
    return pl.pallas_call(
        windows_kernel,
        grid=(steps,),
        in_specs=[
            pl.BlockSpec((per * SPAN, columns), lambda u: (u, 0)),
            pl.BlockSpec(
                (SPAN, columns), lambda u: (jnp.minimum(per * (u + 1), span_count - 1), 0)
            ),
            pl.BlockSpec((SPAN, columns), lambda u: (0, 0)),
        ],
        out_specs=pl.BlockSpec((per, SPAN, columns), lambda u: (u, 0, 0)),
        out_shape=jax.ShapeDtypeStruct((span_count, SPAN, columns), jnp.bfloat16),
        compiler_params=pltpu.CompilerParams(vmem_limit_bytes=VMEM_LIMIT),
        name="windows",
    )(queries, queries, incoming)


def pick_kernel(count, which, table, *refs):
    options = len(refs) - count - 3
    sources, outs = refs[:options], refs[options : options + count]
    held, in_sems, out_sems = refs[-3:]
    ranks = table.shape[1]
    places = [(k, r) for k in range(count) for r in range(ranks)]

    def fetch(source, n):
        return pltpu.make_async_copy(source.at[table[places[n]]], held.at[n], in_sems.at[n])

    for option, source in enumerate(sources):

        @pl.when(which[0] == option)
        def _(source=source):
            for n in range(len(places)):
                fetch(source, n).start()

    stores = []
    for n, (k, r) in enumerate(places):
        fetch(sources[0], n).wait()
        stores.append(pltpu.make_async_copy(held.at[n], outs[k].at[r], out_sems.at[n]))
        stores[-1].start()
    for store in stores:
        store.wait()


def pick_blocks(which, table, sources):
    count, ranks = table.shape
    shape = sources[0].shape[1:]
    copies = count * ranks

    def body(*refs):
        pick_kernel(count, *refs)

    return pl.pallas_call(
        body,
        grid_spec=pltpu.PrefetchScalarGridSpec(
            num_scalar_prefetch=2,
            grid=(1,),
            in_specs=[pl.BlockSpec(memory_space=pl.ANY)] * len(sources),
            out_specs=[pl.BlockSpec(memory_space=pl.ANY)] * count,
            scratch_shapes=[
                pltpu.VMEM((copies,) + shape, sources[0].dtype),
                pltpu.SemaphoreType.DMA((copies,)),
                pltpu.SemaphoreType.DMA((copies,)),
            ],
        ),
        out_shape=[jax.ShapeDtypeStruct((ranks,) + shape, sources[0].dtype) for _ in range(count)],
        compiler_params=pltpu.CompilerParams(vmem_limit_bytes=VMEM_LIMIT),
        name="pick_blocks",
    )(which, table, *sources)


def attend_kernel(cap, parts, steps, tp_index, spans, *refs):
    x_refs = refs[:parts]
    q_ref, wk_first, wk_next, wv_first, wv_next = refs[parts : parts + 5]
    out_ref, lse_ref, x_all, weights_ref, k_even, v_even, k_odd, v_odd = refs[-8:]
    nlen = x_refs[0].shape[-1]
    width = x_refs[0].shape[1]
    columns = q_ref.shape[-1]
    pairs = columns // PAIR
    step = pl.program_id(0)
    scale = HDIM ** (-0.5)
    lanes = lax.broadcasted_iota(jnp.int32, (SPAN, LANES), 1)
    rows = 2 * SPAN

    def two_slots(n):
        return pl.ds(n * 2 * nlen, 2 * nlen)

    def project(n, w_ref, out):
        out[:, two_slots(n)] = jnp.dot(
            w_ref[...], x_all[:, two_slots(n)], preferred_element_type=jnp.float32
        ).astype(jnp.bfloat16)

    def window(slot, pair):
        q = q_ref[spans[slot], :, pair * PAIR : (pair + 1) * PAIR]
        none = jnp.zeros((SPAN, HDIM), jnp.bfloat16)
        upper = jnp.concatenate([q[:, :HDIM], none], axis=1)
        lower = jnp.concatenate([none, q[:, HDIM:]], axis=1)
        return [upper, lower]

    def soften(n, pair, both):
        for a in range(2):
            scores = both[a * rows : (a + 1) * rows, a * nlen : (a + 1) * nlen]
            highest = jnp.max(scores, axis=1, keepdims=True)
            exponent = jnp.exp((scores - highest) * scale)
            totals = jnp.sum(exponent, axis=1, keepdims=True)
            weights_ref[pair, a * rows : (a + 1) * rows, a * nlen : (a + 1) * nlen] = (
                exponent * (1.0 / totals)
            ).astype(jnp.bfloat16)
            lse = highest * scale + jnp.log(totals)
            at = pairs * step + pair
            held = jnp.where(lanes == at, lse[:SPAN], lse_ref[2 * n + a])
            lse_ref[2 * n + a] = jnp.where(lanes == LANES // 8 + at, lse[SPAN:], held)

    def attend(n, k_now, v_now, between):
        scores = []
        for pair in range(pairs):
            q = jnp.concatenate(window(2 * n, pair) + window(2 * n + 1, pair), axis=0)
            keys = k_now[pair * PAIR : (pair + 1) * PAIR, two_slots(n)]
            scores.append(jnp.dot(q, keys, preferred_element_type=jnp.float32))
        between[0]()
        for pair in range(pairs):
            soften(n, pair, scores[pair])
        between[1]()
        for pair in range(pairs):
            cols = slice(pair * PAIR, (pair + 1) * PAIR)
            blended = lax.dot_general(
                weights_ref[pair],
                v_now[cols, two_slots(n)],
                (((1,), (1,)), ((), ())),
                preferred_element_type=jnp.float32,
            )
            for a in range(2):
                top = a * rows
                out_ref[2 * n + a, :, cols] = jnp.concatenate(
                    [blended[top : top + SPAN, :HDIM], blended[top + SPAN : top + rows, HDIM:]],
                    axis=1,
                ).astype(jnp.bfloat16)

    def over_slots(body):
        for n in range(cap // 2):
            body(n)

    @pl.when(step == 0)
    def _():
        lse_ref[...] = jnp.zeros_like(lse_ref)
        weights_ref[...] = jnp.zeros_like(weights_ref)
        for part, x_ref in enumerate(x_refs):
            top = 0
            if parts == 2:
                top = pl.multiple_of((tp_index[0] if part == 0 else 1 - tp_index[0]) * width, 16)
            for i in range(cap):
                x_all[pl.ds(top, width), i * nlen : (i + 1) * nlen] = x_ref[i]

        def first(n):
            project(n, wk_first, k_even)
            project(n, wv_first, v_even)

        over_slots(first)

    def work(k_now, v_now, k_later, v_later):
        def body(n):
            between = [
                lambda: project(n, wk_next, k_later),
                lambda: project(n, wv_next, v_later),
            ]
            attend(n, k_now, v_now, between)

        over_slots(body)

    def finish(k_now, v_now):
        over_slots(lambda n: attend(n, k_now, v_now, [lambda: None] * 2))

    if steps > 1:
        pl.when((step < steps - 1) & (step % 2 == 0))(lambda: work(k_even, v_even, k_odd, v_odd))
    if steps > 2:
        pl.when((step < steps - 1) & (step % 2 == 1))(lambda: work(k_odd, v_odd, k_even, v_even))
    ends = (k_even, v_even) if steps % 2 == 1 else (k_odd, v_odd)
    pl.when(step == steps - 1)(lambda: finish(*ends))


def attend_part(tp_index, spans, blocks, windows, weights, part_index, slots, held):
    parts, cap = len(blocks), spans.shape[0]
    width, nlen = blocks[0].shape[1:]
    features = width * parts
    columns = 2 * PAIR
    steps = windows.shape[-1] // columns

    in_specs = [pl.BlockSpec(x.shape, lambda t, *_: (0, 0, 0)) for x in blocks]
    in_specs += [pl.BlockSpec((windows.shape[0], SPAN, columns), lambda t, *_: (0, 0, t))]
    operands = list(blocks) + [windows]
    for weight in weights:
        in_specs += [
            pl.BlockSpec((columns, features), lambda t, *_: (0, 0)),
            pl.BlockSpec((columns, features), lambda t, *_: (jnp.minimum(t + 1, steps - 1), 0)),
        ]
        operands += [weight] * 2
    aliases = {}
    if held is not None:
        in_specs += [pl.BlockSpec(memory_space=pl.ANY)] * 2
        aliases = {2 + len(operands): 0, 3 + len(operands): 1}
        operands += list(held)
    kv = pltpu.VMEM((columns, cap * nlen), jnp.bfloat16)

    def body(*refs):
        attend_kernel(cap, parts, steps, *refs)

    return pl.pallas_call(
        body,
        grid_spec=pltpu.PrefetchScalarGridSpec(
            num_scalar_prefetch=2,
            grid=(steps,),
            in_specs=in_specs,
            out_specs=[
                pl.BlockSpec((cap, SPAN, columns), lambda t, *_: (part_index, 0, t)),
                pl.BlockSpec((cap, SPAN, LANES), lambda t, *_: (part_index, 0, 0)),
            ],
            scratch_shapes=[
                pltpu.VMEM((features, cap * nlen), jnp.bfloat16),
                pltpu.VMEM((2, 4 * SPAN, 2 * nlen), jnp.bfloat16),
                kv, kv, kv, kv,
            ],
        ),
        out_shape=[
            jax.ShapeDtypeStruct((slots,) + windows.shape[1:], jnp.bfloat16),
            jax.ShapeDtypeStruct((slots, SPAN, LANES), jnp.float32),
        ],
        input_output_aliases=aliases,
        compiler_params=pltpu.CompilerParams(vmem_limit_bytes=VMEM_LIMIT),
        name="attend_part",
    )(tp_index, spans, *operands)


def spread_matrix(columns):
    per = LANES // 8
    row = lax.broadcasted_iota(jnp.int32, (4 * per, columns), 0)
    head = lax.broadcasted_iota(jnp.int32, (4 * per, columns), 1) // HDIM
    own = 2 * (row % per) + (row // per) % 2
    return jnp.where(head == own, 1.0, 0.0).astype(jnp.bfloat16)


def first_shares(l0, l1):
    largest = jnp.maximum(l0, l1)
    e0, e1 = jnp.exp(l0 - largest), jnp.exp(l1 - largest)
    share = e0 / (e0 + e1)
    high = share.astype(jnp.bfloat16).astype(jnp.float32)
    low = pltpu.roll(share - high, LANES // 4, 1)
    lanes = lax.broadcasted_iota(jnp.int32, share.shape, 1)
    return jnp.where(lanes < LANES // 4, high, low).astype(jnp.bfloat16)[:, : LANES // 2]


def mixed(p0, p1, shares, spread, cols):
    share = jnp.dot(shares, spread[:, cols], preferred_element_type=jnp.float32)
    return p0[0, :, cols].astype(jnp.float32) * share + p1[0, :, cols].astype(jnp.float32) * (
        1.0 - share
    )


def mix_last_kernel(places, p0, p1, l0, l1, out_ref, spread):
    spread[...] = spread_matrix(out_ref.shape[-1])
    shares = first_shares(l0[0], l1[0])
    for pair in range(out_ref.shape[-1] // PAIR):
        cols = slice(pair * PAIR, (pair + 1) * PAIR)
        out_ref[:, cols] = mixed(p0, p1, shares, spread, cols).astype(jnp.bfloat16)


def mix_kernel(places, *refs):
    ins, (out_ref, before, spread) = refs[:-3], refs[-3:]
    tile = 16
    late = lax.broadcasted_iota(jnp.int32, (tile, PAIR), 0) == tile - 1

    @pl.when(pl.program_id(0) == 0)
    def _():
        spread[...] = spread_matrix(out_ref.shape[-1])

    for n in range(len(ins) // 4):
        p0, p1, l0, l1 = ins[4 * n : 4 * n + 4]
        shares = first_shares(l0[0], l1[0])
        top = n * SPAN
        cut = top + SPAN - tile
        out_ref[top:cut, :] = before[: SPAN - tile, :]
        for pair in range(out_ref.shape[-1] // PAIR):
            cols = slice(pair * PAIR, (pair + 1) * PAIR)
            result = mixed(p0, p1, shares, spread, cols)
            out_ref[cut : cut + tile, cols] = jnp.where(
                late, result[SPAN - tile :], before[SPAN - tile :, cols].astype(jnp.float32)
            ).astype(jnp.bfloat16)
            before[:, cols] = result.astype(jnp.bfloat16)


def mix_specs(partials, log_totals, span_of):
    def place(j, shape):
        return pl.BlockSpec((1,) + shape, lambda k, places: (places[2 * span_of(k) + j], 0, 0))

    rows, stats = partials.shape[1:], log_totals.shape[1:]
    return [place(0, rows), place(1, rows), place(0, stats), place(1, stats)]


def mix_last(places, partials, log_totals, span_count):
    columns = partials.shape[-1]
    return pl.pallas_call(
        mix_last_kernel,
        grid_spec=pltpu.PrefetchScalarGridSpec(
            num_scalar_prefetch=1,
            grid=(1,),
            in_specs=mix_specs(partials, log_totals, lambda k: span_count - 1),
            out_specs=pl.BlockSpec((SPAN, columns), lambda k, places: (0, 0)),
            scratch_shapes=[pltpu.VMEM((LANES // 2, columns), jnp.bfloat16)],
        ),
        out_shape=jax.ShapeDtypeStruct((SPAN, columns), jnp.bfloat16),
        name="mix_last",
    )(places, partials, partials, log_totals, log_totals)


def mix(places, partials, log_totals, span_count):
    columns = partials.shape[-1]
    per = 4
    in_specs = []
    for n in range(per):
        in_specs += mix_specs(partials, log_totals, lambda k, n=n: per * k + n)
    return pl.pallas_call(
        mix_kernel,
        grid_spec=pltpu.PrefetchScalarGridSpec(
            num_scalar_prefetch=1,
            grid=(span_count // per,),
            in_specs=in_specs,
            out_specs=pl.BlockSpec((per * SPAN, columns), lambda k, places: (k, 0)),
            scratch_shapes=[
                pltpu.VMEM((SPAN, columns), jnp.bfloat16),
                pltpu.VMEM((LANES // 2, columns), jnp.bfloat16),
            ],
        ),
        out_shape=jax.ShapeDtypeStruct((span_count * SPAN, columns), jnp.bfloat16),
        compiler_params=pltpu.CompilerParams(vmem_limit_bytes=VMEM_LIMIT),
        name="mix",
    )(places, *([partials, partials, log_totals, log_totals] * per))


def head_kernel(carried, rows, out_ref):
    early = lax.broadcasted_iota(jnp.int32, out_ref.shape, 0) < SPAN - 1
    out_ref[...] = jnp.where(
        early, carried[...].astype(jnp.float32), rows[...].astype(jnp.float32)
    ).astype(jnp.bfloat16)


def with_head(carried, mixed_rows):
    spec = pl.BlockSpec((SPAN, mixed_rows.shape[-1]), lambda k: (0, 0))
    return pl.pallas_call(
        head_kernel,
        grid=(1,),
        in_specs=[spec, spec],
        out_specs=spec,
        out_shape=jax.ShapeDtypeStruct(mixed_rows.shape, mixed_rows.dtype),
        input_output_aliases={1: 0},
        name="with_head",
    )(carried, mixed_rows)


def after(values, *others):
    return lax.optimization_barrier((values, others))[0]


def shards(queries, neighbours, key_weight, value_weight, neighbour_ids):
    span_count = neighbour_ids.shape[0]
    seq_count, tp_count = lax.axis_size("seq"), lax.axis_size("tp")
    block_count = neighbours.shape[0]
    wants = 2 * span_count
    ranks = (wants + seq_count - 1) // seq_count
    outer = seq_count // INNER
    slots = seq_count * ranks
    own_index = lax.axis_index("seq")
    tp_index = lax.axis_index("tp").astype(jnp.int32).reshape(1)

    own_ids = neighbour_ids.reshape(wants)
    group_ids = jnp.stack([own_ids] + [swapped(own_ids, "seq", k) for k in range(1, INNER)])

    def all_features(part):
        if tp_count == 2:
            return [part, swapped(part, "tp", 1)]
        return [lax.all_gather(part, "tp", axis=1, tiled=True)]

    group_sources = group_ids // block_count
    group_ranks = slot_ranks(group_sources)
    part_sources = own_index ^ (INNER * jnp.arange(outer))
    hit = (group_sources[None, :, None, :] == part_sources[:, None, None, None]) & (
        group_ranks[None, :, None, :] == jnp.arange(ranks)[None, None, :, None]
    )
    table = jnp.sum(jnp.where(hit, (group_ids % block_count)[None, :, None, :], 0), axis=-1)
    table = table.astype(jnp.int32)

    own_sources = own_ids // block_count
    places = ((own_sources ^ own_index) * ranks + slot_ranks(own_sources)).astype(jnp.int32)
    order = jnp.arange(wants)
    spans = jnp.sum(
        jnp.where(places[None, :] == jnp.arange(slots)[:, None], order[None, :] // 2, 0), axis=1
    ).astype(jnp.int32)
    spans = spans.reshape(outer, INNER * ranks)

    def along(x, offset, senders):
        pairs = [(i, i ^ offset) for i in range(seq_count) if i // INNER in senders]
        return lax.ppermute(x, "seq", pairs)

    first = jnp.zeros((1,), jnp.int32)
    held_parts = [([neighbours], first)]

    def fetch(j, *others):
        sources, which = held_parts[j]
        picked = pick_blocks(which, after(table[j], *others), sources)
        wanted = [picked[0]] + [swapped(picked[k], "seq", k) for k in range(1, INNER)]
        return picked, jnp.concatenate(wanted, axis=0)

    picked, wanted = fetch(0)
    own_blocks, edge = after((neighbours, queries[:SPAN]), picked)
    near = swapped(own_blocks, "seq", INNER)
    if outer == 4:
        across = along(own_blocks, 3 * INNER, (1, 2))
    incoming = passed_along(edge, "seq", -1)
    weights = tuple(after(w, picked).T for w in (key_weight, value_weight))

    if outer == 4:
        near, across = after((near, across), weights)
        outer_index = own_index // INNER
        inside = ((outer_index == 1) | (outer_index == 2)).astype(jnp.int32).reshape(1)
        second = along(near, 3 * INNER, (1, 2))
        outward = along(across, INNER, (1, 2))
        third = along(second, INNER, (1, 2))
        held_parts += [([near], first), ([outward, second], inside), ([third, across], inside)]
    else:
        held_parts.append(([near], first))
        for j in range(2, outer):
            low = j & -j
            part = swapped(held_parts[j ^ low][0][0], "seq", INNER * low)
            held_parts.append(([part], first))

    def attend(j, blocks, held, *others):
        return attend_part(
            tp_index, after(spans[j], *others), blocks, windows, weights, j, slots, held
        )

    held = None
    blocks = [all_features(wanted)]
    picked, wanted = fetch(1, wanted)
    windows = span_windows(after(queries, picked), incoming, span_count)
    for j in range(2, outer):
        blocks.append(all_features(wanted))
        picked, wanted_next = fetch(j, windows if held is None else held)
        held = attend(j - 2, blocks[j - 2], held, picked, wanted)
        wanted = wanted_next
    blocks.append(all_features(wanted))
    held = attend(outer - 2, blocks[outer - 2], held, wanted)
    held = attend(outer - 1, blocks[outer - 1], held)

    partials, log_totals = held
    last = mix_last(places, partials, log_totals, span_count)
    carried = passed_along(last, "seq", 1)
    rows = mix(places, partials, log_totals, span_count)
    return with_head(carried, rows)


def solution(mesh):
    in_specs = (P("seq", "tp"), P("seq", "tp", None), P(None, "tp"), P(None, "tp"), P("seq", None))
    out_specs = P("seq", "tp")
    return jax.shard_map(shards, mesh=mesh, in_specs=in_specs, out_specs=out_specs, check_vma=False)
```

```python
import jax
import jax.numpy as jnp
from jax import lax
from jax.experimental import pallas as pl
from jax.experimental.pallas import tpu as pltpu
from jax.sharding import PartitionSpec as P

HDIM = 128
SPAN = 64
PAIR = 2 * HDIM
INNER = 4
LANES = 128
VMEM_LIMIT = 56 * 1024 * 1024


def passed_along(x, axis, by):
    peers = lax.axis_size(axis)
    pairs = [(i, i + by) for i in range(peers) if 0 <= i + by < peers]
    return lax.ppermute(x, axis, pairs)


def swapped(x, axis, offset):
    peers = lax.axis_size(axis)
    return lax.ppermute(x, axis, [(i, i ^ offset) for i in range(peers)])


def slot_ranks(sources):
    positions = sources.shape[-1]
    alike = sources[..., :, None] == sources[..., None, :]
    earlier = jnp.arange(positions)[None, :] < jnp.arange(positions)[:, None]
    return jnp.sum(jnp.where(alike & earlier, 1, 0), axis=-1).astype(jnp.int32)


def windows_kernel(own_ref, next_ref, incoming_ref, out_ref):
    spans = out_ref.shape[0]
    last = pl.program_id(0) == pl.num_programs(0) - 1
    tile = 16
    cut = SPAN - tile
    late = lax.broadcasted_iota(jnp.int32, (tile, out_ref.shape[-1]), 0) == tile - 1
    for n in range(spans):
        if n + 1 < spans:
            later = own_ref[(n + 1) * SPAN : (n + 2) * SPAN, :]
        else:
            later = jnp.where(last, incoming_ref[...], next_ref[...])
        out_ref[n, :cut, :] = later[:cut]
        own = own_ref[n * SPAN + cut : (n + 1) * SPAN, :]
        out_ref[n, cut:, :] = jnp.where(
            late, own.astype(jnp.float32), later[cut:].astype(jnp.float32)
        ).astype(jnp.bfloat16)


def span_windows(queries, incoming, span_count):
    columns = queries.shape[-1]
    per = 4
    steps = span_count // per
    return pl.pallas_call(
        windows_kernel,
        grid=(steps,),
        in_specs=[
            pl.BlockSpec((per * SPAN, columns), lambda u: (u, 0)),
            pl.BlockSpec(
                (SPAN, columns), lambda u: (jnp.minimum(per * (u + 1), span_count - 1), 0)
            ),
            pl.BlockSpec((SPAN, columns), lambda u: (0, 0)),
        ],
        out_specs=pl.BlockSpec((per, SPAN, columns), lambda u: (u, 0, 0)),
        out_shape=jax.ShapeDtypeStruct((span_count, SPAN, columns), jnp.bfloat16),
        compiler_params=pltpu.CompilerParams(vmem_limit_bytes=VMEM_LIMIT),
        name="windows",
    )(queries, queries, incoming)


def pick_kernel(part, ranks, table, *refs):
    count = INNER - 1
    pieces = len(refs) - count - 3
    sources, outs = refs[:pieces], refs[pieces : pieces + count]
    held, in_sems, out_sems = refs[-3:]
    fetches, stores = [], []
    for k in range(1, INNER):
        for r in range(ranks):
            block = table[(part * INNER + k) * ranks + r]
            for piece in range(pieces):
                n = len(fetches)
                fetches.append(
                    pltpu.make_async_copy(sources[piece].at[block], held.at[n], in_sems.at[n])
                )
                stores.append(
                    pltpu.make_async_copy(held.at[n], outs[k - 1].at[r, piece], out_sems.at[n])
                )
    for fetch in fetches:
        fetch.start()
    for fetch, store in zip(fetches, stores):
        fetch.wait()
        store.start()
    for store in stores:
        store.wait()


def pick_blocks(part, ranks, table, sources):
    shape = sources[0].shape[1:]
    pieces = len(sources)
    copies = (INNER - 1) * ranks * pieces

    def body(*refs):
        pick_kernel(part, ranks, *refs)

    return pl.pallas_call(
        body,
        grid_spec=pltpu.PrefetchScalarGridSpec(
            num_scalar_prefetch=1,
            grid=(1,),
            in_specs=[pl.BlockSpec(memory_space=pl.ANY)] * pieces,
            out_specs=[pl.BlockSpec(memory_space=pl.ANY)] * (INNER - 1),
            scratch_shapes=[
                pltpu.VMEM((copies,) + shape, sources[0].dtype),
                pltpu.SemaphoreType.DMA((copies,)),
                pltpu.SemaphoreType.DMA((copies,)),
            ],
        ),
        out_shape=[
            jax.ShapeDtypeStruct((ranks, pieces) + shape, sources[0].dtype)
            for _ in range(INNER - 1)
        ],
        compiler_params=pltpu.CompilerParams(vmem_limit_bytes=VMEM_LIMIT),
        name="pick_blocks",
    )(table, *sources)


def attend_kernel(part, cap, ranks, pieces, steps, tp_index, table, spans, *refs):
    count = ranks * pieces + INNER - 1
    own_refs, got_refs = refs[: ranks * pieces], refs[ranks * pieces : count]
    q_ref, wk_first, wk_next, wv_first, wv_next = refs[count : count + 5]
    out_ref, lse_ref, x_all, scores_ref, weights_ref, k_even, v_even, k_odd, v_odd = refs[-9:]
    nlen = scores_ref.shape[-1]
    pairs = scores_ref.shape[0] // cap
    step = pl.program_id(0)
    scale = HDIM ** (-0.5)
    lanes = lax.broadcasted_iota(jnp.int32, (SPAN, LANES), 1)

    def project(w_ref, out):
        out[...] = jnp.dot(w_ref[...], x_all[...], preferred_element_type=jnp.float32).astype(
            jnp.bfloat16
        )

    def block(ref, pair, i):
        return ref[pair * PAIR : (pair + 1) * PAIR, i * nlen : (i + 1) * nlen]

    def score(k_ref):
        none = jnp.zeros((SPAN, HDIM), jnp.bfloat16)
        for pair in range(pairs):
            for i in range(cap):
                q = q_ref[spans[part * cap + i], :, pair * PAIR : (pair + 1) * PAIR]
                upper = jnp.concatenate([q[:, :HDIM], none], axis=1)
                lower = jnp.concatenate([none, q[:, HDIM:]], axis=1)
                scores_ref[pair * cap + i] = jnp.dot(
                    jnp.concatenate([upper, lower], axis=0),
                    block(k_ref, pair, i),
                    preferred_element_type=jnp.float32,
                )

    def soften():
        for i in range(cap):
            held = lse_ref[i]
            for pair in range(pairs):
                scores = scores_ref[pair * cap + i]
                highest = jnp.max(scores, axis=1, keepdims=True)
                exponent = jnp.exp((scores - highest) * scale)
                totals = jnp.sum(exponent, axis=1, keepdims=True)
                weights_ref[pair * cap + i] = (exponent * (1.0 / totals)).astype(jnp.bfloat16)
                lse = highest * scale + jnp.log(totals)
                at = pairs * step + pair
                held = jnp.where(lanes == at, lse[:SPAN], held)
                held = jnp.where(lanes == LANES // 8 + at, lse[SPAN:], held)
            lse_ref[i] = held

    def blend(v_ref):
        for pair in range(pairs):
            cols = slice(pair * PAIR, (pair + 1) * PAIR)
            for i in range(cap):
                blended = lax.dot_general(
                    weights_ref[pair * cap + i],
                    block(v_ref, pair, i),
                    (((1,), (1,)), ((), ())),
                    preferred_element_type=jnp.float32,
                )
                out_ref[i, :, cols] = jnp.concatenate(
                    [blended[:SPAN, :HDIM], blended[SPAN:, HDIM:]], axis=1
                ).astype(jnp.bfloat16)

    @pl.when(step == 0)
    def _():
        lse_ref[...] = jnp.zeros_like(lse_ref)
        for i in range(cap):
            for piece in range(pieces):
                if i < ranks:
                    block = own_refs[i * pieces + piece][0]
                else:
                    block = got_refs[i // ranks - 1][i % ranks, piece]
                width = block.shape[0]
                top = 0
                if pieces == 2:
                    place = tp_index[0] if piece == 0 else 1 - tp_index[0]
                    top = pl.multiple_of(place * width, 16)
                x_all[pl.ds(top, width), i * nlen : (i + 1) * nlen] = block
        project(wk_first, k_even)
        project(wv_first, v_even)

    def work(k_now, v_now, k_later, v_later):
        score(k_now)
        project(wk_next, k_later)
        soften()
        project(wv_next, v_later)
        blend(v_now)

    def finish(k_now, v_now):
        score(k_now)
        soften()
        blend(v_now)

    if steps > 1:
        pl.when((step < steps - 1) & (step % 2 == 0))(lambda: work(k_even, v_even, k_odd, v_odd))
    if steps > 2:
        pl.when((step < steps - 1) & (step % 2 == 1))(lambda: work(k_odd, v_odd, k_even, v_even))
    ends = (k_even, v_even) if steps % 2 == 1 else (k_odd, v_odd)
    pl.when(step == steps - 1)(lambda: finish(*ends))


def attend_part(part, cap, scalars, own, got, windows, weights, slots, held):
    pieces = len(own)
    ranks = got[0].shape[0]
    width, nlen = own[0].shape[1:]
    features = width * pieces
    columns = 2 * PAIR
    steps = windows.shape[-1] // columns

    def own_at(r):
        return lambda t, tp_index, table, spans: (table[part * cap + r], 0, 0)

    in_specs = [pl.BlockSpec((1, width, nlen), own_at(r)) for r in range(ranks) for _ in own]
    operands = list(own) * ranks
    in_specs += [pl.BlockSpec(g.shape, lambda t, *_: (0, 0, 0, 0)) for g in got]
    operands += list(got)
    in_specs += [pl.BlockSpec((windows.shape[0], SPAN, columns), lambda t, *_: (0, 0, t))]
    operands += [windows]
    for weight in weights:
        in_specs += [
            pl.BlockSpec((columns, features), lambda t, *_: (0, 0)),
            pl.BlockSpec((columns, features), lambda t, *_: (jnp.minimum(t + 1, steps - 1), 0)),
        ]
        operands += [weight] * 2
    aliases = {}
    if held is not None:
        in_specs += [pl.BlockSpec(memory_space=pl.ANY)] * 2
        aliases = {3 + len(operands): 0, 4 + len(operands): 1}
        operands += list(held)
    kv = pltpu.VMEM((columns, cap * nlen), jnp.bfloat16)

    def body(*refs):
        attend_kernel(part, cap, ranks, pieces, steps, *refs)

    return pl.pallas_call(
        body,
        grid_spec=pltpu.PrefetchScalarGridSpec(
            num_scalar_prefetch=3,
            grid=(steps,),
            in_specs=in_specs,
            out_specs=[
                pl.BlockSpec((cap, SPAN, columns), lambda t, *_: (part, 0, t)),
                pl.BlockSpec((cap, SPAN, LANES), lambda t, *_: (part, 0, 0)),
            ],
            scratch_shapes=[
                pltpu.VMEM((features, cap * nlen), jnp.bfloat16),
                pltpu.VMEM((2 * cap, 2 * SPAN, nlen), jnp.float32),
                pltpu.VMEM((2 * cap, 2 * SPAN, nlen), jnp.bfloat16),
                kv, kv, kv, kv,
            ],
        ),
        out_shape=[
            jax.ShapeDtypeStruct((slots,) + windows.shape[1:], jnp.bfloat16),
            jax.ShapeDtypeStruct((slots, SPAN, LANES), jnp.float32),
        ],
        input_output_aliases=aliases,
        compiler_params=pltpu.CompilerParams(vmem_limit_bytes=VMEM_LIMIT),
        name="attend_part",
    )(*scalars, *operands)


def spread_matrix(columns):
    per = LANES // 8
    row = lax.broadcasted_iota(jnp.int32, (4 * per, columns), 0)
    head = lax.broadcasted_iota(jnp.int32, (4 * per, columns), 1) // HDIM
    own = 2 * (row % per) + (row // per) % 2
    return jnp.where(head == own, 1.0, 0.0).astype(jnp.bfloat16)


def first_shares(l0, l1):
    largest = jnp.maximum(l0, l1)
    e0, e1 = jnp.exp(l0 - largest), jnp.exp(l1 - largest)
    share = e0 / (e0 + e1)
    high = share.astype(jnp.bfloat16).astype(jnp.float32)
    low = pltpu.roll(share - high, LANES // 4, 1)
    lanes = lax.broadcasted_iota(jnp.int32, share.shape, 1)
    return jnp.where(lanes < LANES // 4, high, low).astype(jnp.bfloat16)[:, : LANES // 2]


def mixed(p0, p1, shares, spread, cols):
    share = jnp.dot(shares, spread[:, cols], preferred_element_type=jnp.float32)
    return p0[0, :, cols].astype(jnp.float32) * share + p1[0, :, cols].astype(jnp.float32) * (
        1.0 - share
    )


def mix_last_kernel(places, p0, p1, l0, l1, out_ref, spread):
    spread[...] = spread_matrix(out_ref.shape[-1])
    shares = first_shares(l0[0], l1[0])
    for pair in range(out_ref.shape[-1] // PAIR):
        cols = slice(pair * PAIR, (pair + 1) * PAIR)
        out_ref[:, cols] = mixed(p0, p1, shares, spread, cols).astype(jnp.bfloat16)


def mix_kernel(places, *refs):
    ins, (out_ref, before, spread) = refs[:-3], refs[-3:]
    tile = 16
    late = lax.broadcasted_iota(jnp.int32, (tile, PAIR), 0) == tile - 1

    @pl.when(pl.program_id(0) == 0)
    def _():
        spread[...] = spread_matrix(out_ref.shape[-1])

    for n in range(len(ins) // 4):
        p0, p1, l0, l1 = ins[4 * n : 4 * n + 4]
        shares = first_shares(l0[0], l1[0])
        top = n * SPAN
        cut = top + SPAN - tile
        out_ref[top:cut, :] = before[: SPAN - tile, :]
        for pair in range(out_ref.shape[-1] // PAIR):
            cols = slice(pair * PAIR, (pair + 1) * PAIR)
            result = mixed(p0, p1, shares, spread, cols)
            out_ref[cut : cut + tile, cols] = jnp.where(
                late, result[SPAN - tile :], before[SPAN - tile :, cols].astype(jnp.float32)
            ).astype(jnp.bfloat16)
            before[:, cols] = result.astype(jnp.bfloat16)


def mix_specs(partials, log_totals, span_of):
    def place(j, shape):
        return pl.BlockSpec((1,) + shape, lambda k, places: (places[2 * span_of(k) + j], 0, 0))

    rows, stats = partials.shape[1:], log_totals.shape[1:]
    return [place(0, rows), place(1, rows), place(0, stats), place(1, stats)]


def mix_last(places, partials, log_totals, span_count):
    columns = partials.shape[-1]
    return pl.pallas_call(
        mix_last_kernel,
        grid_spec=pltpu.PrefetchScalarGridSpec(
            num_scalar_prefetch=1,
            grid=(1,),
            in_specs=mix_specs(partials, log_totals, lambda k: span_count - 1),
            out_specs=pl.BlockSpec((SPAN, columns), lambda k, places: (0, 0)),
            scratch_shapes=[pltpu.VMEM((LANES // 2, columns), jnp.bfloat16)],
        ),
        out_shape=jax.ShapeDtypeStruct((SPAN, columns), jnp.bfloat16),
        name="mix_last",
    )(places, partials, partials, log_totals, log_totals)


def mix(places, partials, log_totals, span_count):
    columns = partials.shape[-1]
    per = 4
    in_specs = []
    for n in range(per):
        in_specs += mix_specs(partials, log_totals, lambda k, n=n: per * k + n)
    return pl.pallas_call(
        mix_kernel,
        grid_spec=pltpu.PrefetchScalarGridSpec(
            num_scalar_prefetch=1,
            grid=(span_count // per,),
            in_specs=in_specs,
            out_specs=pl.BlockSpec((per * SPAN, columns), lambda k, places: (k, 0)),
            scratch_shapes=[
                pltpu.VMEM((SPAN, columns), jnp.bfloat16),
                pltpu.VMEM((LANES // 2, columns), jnp.bfloat16),
            ],
        ),
        out_shape=jax.ShapeDtypeStruct((span_count * SPAN, columns), jnp.bfloat16),
        compiler_params=pltpu.CompilerParams(vmem_limit_bytes=VMEM_LIMIT),
        name="mix",
    )(places, *([partials, partials, log_totals, log_totals] * per))


def head_kernel(carried, rows, out_ref):
    early = lax.broadcasted_iota(jnp.int32, out_ref.shape, 0) < SPAN - 1
    out_ref[...] = jnp.where(
        early, carried[...].astype(jnp.float32), rows[...].astype(jnp.float32)
    ).astype(jnp.bfloat16)


def with_head(carried, mixed_rows):
    spec = pl.BlockSpec((SPAN, mixed_rows.shape[-1]), lambda k: (0, 0))
    return pl.pallas_call(
        head_kernel,
        grid=(1,),
        in_specs=[spec, spec],
        out_specs=spec,
        out_shape=jax.ShapeDtypeStruct(mixed_rows.shape, mixed_rows.dtype),
        input_output_aliases={1: 0},
        name="with_head",
    )(carried, mixed_rows)


def after(values, *others):
    return lax.optimization_barrier((values, others))[0]


def shards(queries, neighbours, key_weight, value_weight, neighbour_ids):
    span_count = neighbour_ids.shape[0]
    seq_count, tp_count = lax.axis_size("seq"), lax.axis_size("tp")
    block_count = neighbours.shape[0]
    wants = 2 * span_count
    ranks = (wants + seq_count - 1) // seq_count
    outer = seq_count // INNER
    slots = seq_count * ranks
    cap = INNER * ranks
    own_index = lax.axis_index("seq")
    tp_index = lax.axis_index("tp").astype(jnp.int32).reshape(1)

    def all_features(part):
        if tp_count == 2:
            return [part, swapped(part, "tp", 1)]
        return [lax.all_gather(part, "tp", axis=1, tiled=True)]

    def along(x, offset, senders):
        pairs = [(i, i ^ offset) for i in range(seq_count) if i // INNER in senders]
        return lax.ppermute(x, "seq", pairs)

    near = swapped(neighbours, "seq", INNER)
    across = along(neighbours, 3 * INNER, (1, 2)) if outer == 4 else near
    own = all_features(neighbours)
    own_ids = neighbour_ids.reshape(wants)
    group_ids = jnp.stack([own_ids] + [swapped(own_ids, "seq", k) for k in range(1, INNER)])
    incoming = passed_along(queries[:SPAN], "seq", -1)
    weights = (key_weight.T, value_weight.T)
    near, across = after((near, across), weights)

    group_sources = group_ids // block_count
    group_ranks = slot_ranks(group_sources)
    part_sources = own_index ^ (INNER * jnp.arange(outer))
    hit = (group_sources[None, :, None, :] == part_sources[:, None, None, None]) & (
        group_ranks[None, :, None, :] == jnp.arange(ranks)[None, None, :, None]
    )
    table = jnp.sum(jnp.where(hit, (group_ids % block_count)[None, :, None, :], 0), axis=-1)
    table = table.astype(jnp.int32).reshape(outer * cap)

    own_sources = own_ids // block_count
    places = ((own_sources ^ own_index) * ranks + slot_ranks(own_sources)).astype(jnp.int32)
    order = jnp.arange(wants)
    spans = jnp.sum(
        jnp.where(places[None, :] == jnp.arange(slots)[:, None], order[None, :] // 2, 0), axis=1
    ).astype(jnp.int32)

    def send(j, own, *others):
        picked = pick_blocks(j, ranks, after(table, *others), own)
        return picked, [swapped(picked[k - 1], "seq", k) for k in range(1, INNER)]

    def attend(j, own, got, held, *others):
        scalars = (tp_index, table, after(spans, *others))
        return attend_part(j, cap, scalars, own, got, windows, weights, slots, held)

    inside = (own_index // INNER == 1) | (own_index // INNER == 2)
    if outer == 4:
        second = along(near, 3 * INNER, (1, 2))
        outward = along(across, INNER, (1, 2))
    owns = [own, all_features(near)]
    picked, got = send(0, own)
    gots = [got]
    windows = span_windows(after(queries, picked), incoming, span_count)
    if outer == 4:
        second, outward = after((second, outward), windows)
        far = jnp.where(inside, second, outward)
        third = along(second, INNER, (1, 2))
    else:
        far = swapped(near, "seq", 3 * INNER)
    owns.append(all_features(far))
    picked, got = send(1, owns[1], far)
    gots.append(got)
    held = attend(0, owns[0], gots[0], None, picked)
    parts = [neighbours, near, far]
    for j in range(3, outer):
        if outer == 4:
            part = jnp.where(inside, *after((across, third), held))
        else:
            low = j & -j
            part = swapped(after(parts[j ^ low], held), "seq", INNER * low)
        parts.append(part)
        owns.append(all_features(part))
        picked, got = send(j - 1, owns[j - 1], part)
        gots.append(got)
        held = attend(j - 2, owns[j - 2], gots[j - 2], held, picked)
    picked, got = send(outer - 1, owns[outer - 1], held)
    gots.append(got)
    held = attend(outer - 2, owns[outer - 2], gots[outer - 2], held, picked)
    held = attend(outer - 1, owns[outer - 1], gots[outer - 1], held)

    partials, log_totals = held
    last = mix_last(places, partials, log_totals, span_count)
    carried = passed_along(last, "seq", 1)
    rows = mix(places, partials, log_totals, span_count)
    return with_head(carried, rows)


def solution(mesh):
    in_specs = (P("seq", "tp"), P("seq", "tp", None), P(None, "tp"), P(None, "tp"), P("seq", None))
    out_specs = P("seq", "tp")
    return jax.shard_map(shards, mesh=mesh, in_specs=in_specs, out_specs=out_specs, check_vma=False)
```

```python
import jax
import jax.numpy as jnp
from jax import lax
from jax.experimental import pallas as pl
from jax.experimental.pallas import tpu as pltpu
from jax.sharding import PartitionSpec as P

HDIM = 128
SPAN = 64
PAIR = 2 * HDIM
INNER = 4
LANES = 128
VMEM_LIMIT = 56 * 1024 * 1024


LIGHT = pl.CostEstimate(flops=1000, bytes_accessed=1000, transcendentals=0)
HEAVY = pl.CostEstimate(flops=20 * 10**9, bytes_accessed=10**7, transcendentals=0)


def passed_along(x, axis, by):
    peers = lax.axis_size(axis)
    pairs = [(i, i + by) for i in range(peers) if 0 <= i + by < peers]
    return lax.ppermute(x, axis, pairs)


def swapped(x, axis, offset):
    peers = lax.axis_size(axis)
    return lax.ppermute(x, axis, [(i, i ^ offset) for i in range(peers)])


def slot_ranks(sources):
    positions = sources.shape[-1]
    alike = sources[..., :, None] == sources[..., None, :]
    earlier = jnp.arange(positions)[None, :] < jnp.arange(positions)[:, None]
    return jnp.sum(jnp.where(alike & earlier, 1, 0), axis=-1).astype(jnp.int32)


def windows_kernel(own_ref, next_ref, incoming_ref, out_ref):
    spans = out_ref.shape[0]
    last = pl.program_id(0) == pl.num_programs(0) - 1
    tile = 16
    cut = SPAN - tile
    late = lax.broadcasted_iota(jnp.int32, (tile, out_ref.shape[-1]), 0) == tile - 1
    for n in range(spans):
        if n + 1 < spans:
            later = own_ref[(n + 1) * SPAN : (n + 2) * SPAN, :]
        else:
            later = jnp.where(last, incoming_ref[...], next_ref[...])
        out_ref[n, :cut, :] = later[:cut]
        own = own_ref[n * SPAN + cut : (n + 1) * SPAN, :]
        out_ref[n, cut:, :] = jnp.where(
            late, own.astype(jnp.float32), later[cut:].astype(jnp.float32)
        ).astype(jnp.bfloat16)


def span_windows(queries, incoming, span_count):
    columns = queries.shape[-1]
    per = 4
    steps = span_count // per
    return pl.pallas_call(
        windows_kernel,
        grid=(steps,),
        in_specs=[
            pl.BlockSpec((per * SPAN, columns), lambda u: (u, 0)),
            pl.BlockSpec(
                (SPAN, columns), lambda u: (jnp.minimum(per * (u + 1), span_count - 1), 0)
            ),
            pl.BlockSpec((SPAN, columns), lambda u: (0, 0)),
        ],
        out_specs=pl.BlockSpec((per, SPAN, columns), lambda u: (u, 0, 0)),
        out_shape=jax.ShapeDtypeStruct((span_count, SPAN, columns), jnp.bfloat16),
        compiler_params=pltpu.CompilerParams(vmem_limit_bytes=VMEM_LIMIT),
        cost_estimate=LIGHT,
        name="windows",
    )(queries, queries, incoming)


def pick_kernel(part, ranks, table, *refs):
    sources, outs = refs[:2], refs[2:4]
    held, in_sems, out_sems = refs[-3:]
    fetches, stores = [], []
    for e in range(2):
        for a in range(2):
            for r in range(ranks):
                n = len(fetches)
                block = table[((part * 2 + e) * 2 + a) * ranks + r]
                fetches.append(
                    pltpu.make_async_copy(sources[a].at[block], held.at[n], in_sems.at[n])
                )
                stores.append(
                    pltpu.make_async_copy(held.at[n], outs[e].at[a * ranks + r], out_sems.at[n])
                )
    for fetch in fetches:
        fetch.start()
    for fetch, store in zip(fetches, stores):
        fetch.wait()
        store.start()
    for store in stores:
        store.wait()


def pick_blocks(part, ranks, table, sources):
    shape = sources[0].shape[1:]
    copies = 4 * ranks

    def body(*refs):
        pick_kernel(part, ranks, *refs)

    return pl.pallas_call(
        body,
        grid_spec=pltpu.PrefetchScalarGridSpec(
            num_scalar_prefetch=1,
            grid=(1,),
            in_specs=[pl.BlockSpec(memory_space=pltpu.HBM)] * 2,
            out_specs=[pl.BlockSpec(memory_space=pltpu.HBM)] * 2,
            scratch_shapes=[
                pltpu.VMEM((copies,) + shape, sources[0].dtype),
                pltpu.SemaphoreType.DMA((copies,)),
                pltpu.SemaphoreType.DMA((copies,)),
            ],
        ),
        out_shape=[jax.ShapeDtypeStruct((2 * ranks,) + shape, sources[0].dtype)] * 2,
        compiler_params=pltpu.CompilerParams(vmem_limit_bytes=VMEM_LIMIT),
        cost_estimate=LIGHT,
        name="pick_blocks",
    )(table, *sources)


def attend_kernel(part, cap, pieces, steps, tp_index, spans, *refs):
    x_refs = refs[:pieces]
    q_ref, wk_first, wk_next, wv_first, wv_next = refs[pieces : pieces + 5]
    out_ref, lse_ref, x_all, scores_ref, weights_ref, k_even, v_even, k_odd, v_odd = refs[-9:]
    nlen = scores_ref.shape[-1]
    pairs = scores_ref.shape[0] // cap
    step = pl.program_id(0)
    scale = HDIM ** (-0.5)
    lanes = lax.broadcasted_iota(jnp.int32, (SPAN, LANES), 1)

    def project(w_ref, out):
        out[...] = jnp.dot(w_ref[...], x_all[...], preferred_element_type=jnp.float32).astype(
            jnp.bfloat16
        )

    def block(ref, pair, i):
        return ref[pair * PAIR : (pair + 1) * PAIR, i * nlen : (i + 1) * nlen]

    def score(k_ref):
        none = jnp.zeros((SPAN, HDIM), jnp.bfloat16)
        for pair in range(pairs):
            for i in range(cap):
                q = q_ref[spans[part * cap + i], :, pair * PAIR : (pair + 1) * PAIR]
                upper = jnp.concatenate([q[:, :HDIM], none], axis=1)
                lower = jnp.concatenate([none, q[:, HDIM:]], axis=1)
                scores_ref[pair * cap + i] = jnp.dot(
                    jnp.concatenate([upper, lower], axis=0),
                    block(k_ref, pair, i),
                    preferred_element_type=jnp.float32,
                )

    def soften():
        for i in range(cap):
            held = lse_ref[i]
            for pair in range(pairs):
                scores = scores_ref[pair * cap + i]
                highest = jnp.max(scores, axis=1, keepdims=True)
                exponent = jnp.exp((scores - highest) * scale)
                totals = jnp.sum(exponent, axis=1, keepdims=True)
                weights_ref[pair * cap + i] = (exponent * (1.0 / totals)).astype(jnp.bfloat16)
                lse = highest * scale + jnp.log(totals)
                at = pairs * step + pair
                held = jnp.where(lanes == at, lse[:SPAN], held)
                held = jnp.where(lanes == LANES // 8 + at, lse[SPAN:], held)
            lse_ref[i] = held

    def blend(v_ref):
        for pair in range(pairs):
            cols = slice(pair * PAIR, (pair + 1) * PAIR)
            for i in range(cap):
                blended = lax.dot_general(
                    weights_ref[pair * cap + i],
                    block(v_ref, pair, i),
                    (((1,), (1,)), ((), ())),
                    preferred_element_type=jnp.float32,
                )
                out_ref[i, :, cols] = jnp.concatenate(
                    [blended[:SPAN, :HDIM], blended[SPAN:, HDIM:]], axis=1
                ).astype(jnp.bfloat16)

    @pl.when(step == 0)
    def _():
        lse_ref[...] = jnp.zeros_like(lse_ref)
        for piece, x_ref in enumerate(x_refs):
            width = x_ref.shape[1]
            top = 0
            if pieces == 2:
                place = tp_index[0] if piece == 0 else 1 - tp_index[0]
                top = pl.multiple_of(place * width, 16)
            for i in range(cap):
                x_all[pl.ds(top, width), i * nlen : (i + 1) * nlen] = x_ref[i]
        project(wk_first, k_even)
        project(wv_first, v_even)

    def work(k_now, v_now, k_later, v_later):
        score(k_now)
        project(wk_next, k_later)
        soften()
        project(wv_next, v_later)
        blend(v_now)

    def finish(k_now, v_now):
        score(k_now)
        soften()
        blend(v_now)

    if steps > 1:
        pl.when((step < steps - 1) & (step % 2 == 0))(lambda: work(k_even, v_even, k_odd, v_odd))
    if steps > 2:
        pl.when((step < steps - 1) & (step % 2 == 1))(lambda: work(k_odd, v_odd, k_even, v_even))
    ends = (k_even, v_even) if steps % 2 == 1 else (k_odd, v_odd)
    pl.when(step == steps - 1)(lambda: finish(*ends))


def attend_part(part, cap, scalars, blocks, windows, weights, slots, held):
    pieces = len(blocks)
    width, nlen = blocks[0].shape[1:]
    features = width * pieces
    columns = 2 * PAIR
    steps = windows.shape[-1] // columns

    in_specs = [pl.BlockSpec(x.shape, lambda t, *_: (0, 0, 0)) for x in blocks]
    operands = list(blocks)
    in_specs += [pl.BlockSpec((windows.shape[0], SPAN, columns), lambda t, *_: (0, 0, t))]
    operands += [windows]
    for weight in weights:
        in_specs += [
            pl.BlockSpec((columns, features), lambda t, *_: (0, 0)),
            pl.BlockSpec((columns, features), lambda t, *_: (jnp.minimum(t + 1, steps - 1), 0)),
        ]
        operands += [weight] * 2
    aliases = {}
    if held is not None:
        in_specs += [pl.BlockSpec(memory_space=pl.ANY)] * 2
        aliases = {2 + len(operands): 0, 3 + len(operands): 1}
        operands += list(held)
    kv = pltpu.VMEM((columns, cap * nlen), jnp.bfloat16)

    def body(*refs):
        attend_kernel(part, cap, pieces, steps, *refs)

    return pl.pallas_call(
        body,
        grid_spec=pltpu.PrefetchScalarGridSpec(
            num_scalar_prefetch=2,
            grid=(steps,),
            in_specs=in_specs,
            out_specs=[
                pl.BlockSpec((cap, SPAN, columns), lambda t, *_: (part, 0, t)),
                pl.BlockSpec((cap, SPAN, LANES), lambda t, *_: (part, 0, 0)),
            ],
            scratch_shapes=[
                pltpu.VMEM((features, cap * nlen), jnp.bfloat16),
                pltpu.VMEM((2 * cap, 2 * SPAN, nlen), jnp.float32),
                pltpu.VMEM((2 * cap, 2 * SPAN, nlen), jnp.bfloat16),
                kv, kv, kv, kv,
            ],
        ),
        out_shape=[
            jax.ShapeDtypeStruct((slots,) + windows.shape[1:], jnp.bfloat16),
            jax.ShapeDtypeStruct((slots, SPAN, LANES), jnp.float32),
        ],
        input_output_aliases=aliases,
        compiler_params=pltpu.CompilerParams(vmem_limit_bytes=VMEM_LIMIT),
        cost_estimate=HEAVY,
        name="attend_part",
    )(*scalars, *operands)


def spread_matrix(columns):
    per = LANES // 8
    row = lax.broadcasted_iota(jnp.int32, (4 * per, columns), 0)
    head = lax.broadcasted_iota(jnp.int32, (4 * per, columns), 1) // HDIM
    own = 2 * (row % per) + (row // per) % 2
    return jnp.where(head == own, 1.0, 0.0).astype(jnp.bfloat16)


def first_shares(l0, l1):
    largest = jnp.maximum(l0, l1)
    e0, e1 = jnp.exp(l0 - largest), jnp.exp(l1 - largest)
    share = e0 / (e0 + e1)
    high = share.astype(jnp.bfloat16).astype(jnp.float32)
    low = pltpu.roll(share - high, LANES // 4, 1)
    lanes = lax.broadcasted_iota(jnp.int32, share.shape, 1)
    return jnp.where(lanes < LANES // 4, high, low).astype(jnp.bfloat16)[:, : LANES // 2]


def mixed(p0, p1, shares, spread, cols):
    share = jnp.dot(shares, spread[:, cols], preferred_element_type=jnp.float32)
    return p0[0, :, cols].astype(jnp.float32) * share + p1[0, :, cols].astype(jnp.float32) * (
        1.0 - share
    )


def mix_last_kernel(places, p0, p1, l0, l1, out_ref, spread):
    spread[...] = spread_matrix(out_ref.shape[-1])
    shares = first_shares(l0[0], l1[0])
    for pair in range(out_ref.shape[-1] // PAIR):
        cols = slice(pair * PAIR, (pair + 1) * PAIR)
        out_ref[:, cols] = mixed(p0, p1, shares, spread, cols).astype(jnp.bfloat16)


def mix_kernel(places, *refs):
    ins, (out_ref, before, spread) = refs[:-3], refs[-3:]
    tile = 16
    late = lax.broadcasted_iota(jnp.int32, (tile, PAIR), 0) == tile - 1

    @pl.when(pl.program_id(0) == 0)
    def _():
        spread[...] = spread_matrix(out_ref.shape[-1])

    for n in range(len(ins) // 4):
        p0, p1, l0, l1 = ins[4 * n : 4 * n + 4]
        shares = first_shares(l0[0], l1[0])
        top = n * SPAN
        cut = top + SPAN - tile
        out_ref[top:cut, :] = before[: SPAN - tile, :]
        for pair in range(out_ref.shape[-1] // PAIR):
            cols = slice(pair * PAIR, (pair + 1) * PAIR)
            result = mixed(p0, p1, shares, spread, cols)
            out_ref[cut : cut + tile, cols] = jnp.where(
                late, result[SPAN - tile :], before[SPAN - tile :, cols].astype(jnp.float32)
            ).astype(jnp.bfloat16)
            before[:, cols] = result.astype(jnp.bfloat16)


def mix_specs(partials, log_totals, span_of):
    def place(j, shape):
        return pl.BlockSpec((1,) + shape, lambda k, places: (places[2 * span_of(k) + j], 0, 0))

    rows, stats = partials.shape[1:], log_totals.shape[1:]
    return [place(0, rows), place(1, rows), place(0, stats), place(1, stats)]


def mix_last(places, partials, log_totals, span_count):
    columns = partials.shape[-1]
    return pl.pallas_call(
        mix_last_kernel,
        grid_spec=pltpu.PrefetchScalarGridSpec(
            num_scalar_prefetch=1,
            grid=(1,),
            in_specs=mix_specs(partials, log_totals, lambda k: span_count - 1),
            out_specs=pl.BlockSpec((SPAN, columns), lambda k, places: (0, 0)),
            scratch_shapes=[pltpu.VMEM((LANES // 2, columns), jnp.bfloat16)],
        ),
        out_shape=jax.ShapeDtypeStruct((SPAN, columns), jnp.bfloat16),
        cost_estimate=LIGHT,
        name="mix_last",
    )(places, partials, partials, log_totals, log_totals)


def mix(places, partials, log_totals, span_count):
    columns = partials.shape[-1]
    per = 4
    in_specs = []
    for n in range(per):
        in_specs += mix_specs(partials, log_totals, lambda k, n=n: per * k + n)
    return pl.pallas_call(
        mix_kernel,
        grid_spec=pltpu.PrefetchScalarGridSpec(
            num_scalar_prefetch=1,
            grid=(span_count // per,),
            in_specs=in_specs,
            out_specs=pl.BlockSpec((per * SPAN, columns), lambda k, places: (k, 0)),
            scratch_shapes=[
                pltpu.VMEM((SPAN, columns), jnp.bfloat16),
                pltpu.VMEM((LANES // 2, columns), jnp.bfloat16),
            ],
        ),
        out_shape=jax.ShapeDtypeStruct((span_count * SPAN, columns), jnp.bfloat16),
        compiler_params=pltpu.CompilerParams(vmem_limit_bytes=VMEM_LIMIT),
        cost_estimate=LIGHT,
        name="mix",
    )(places, *([partials, partials, log_totals, log_totals] * per))


def head_kernel(carried, rows, out_ref):
    early = lax.broadcasted_iota(jnp.int32, out_ref.shape, 0) < SPAN - 1
    out_ref[...] = jnp.where(
        early, carried[...].astype(jnp.float32), rows[...].astype(jnp.float32)
    ).astype(jnp.bfloat16)


def with_head(carried, mixed_rows):
    spec = pl.BlockSpec((SPAN, mixed_rows.shape[-1]), lambda k: (0, 0))
    return pl.pallas_call(
        head_kernel,
        grid=(1,),
        in_specs=[spec, spec],
        out_specs=spec,
        out_shape=jax.ShapeDtypeStruct(mixed_rows.shape, mixed_rows.dtype),
        input_output_aliases={1: 0},
        cost_estimate=LIGHT,
        name="with_head",
    )(carried, mixed_rows)


def after(values, *others):
    return lax.optimization_barrier((values, others))[0]


def shards(queries, neighbours, key_weight, value_weight, neighbour_ids):
    span_count = neighbour_ids.shape[0]
    seq_count, tp_count = lax.axis_size("seq"), lax.axis_size("tp")
    block_count = neighbours.shape[0]
    wants = 2 * span_count
    ranks = (wants + seq_count - 1) // seq_count
    outer = seq_count // INNER
    slots = seq_count * ranks
    cap = INNER * ranks
    own_index = lax.axis_index("seq")
    tp_index = lax.axis_index("tp").astype(jnp.int32).reshape(1)

    def all_features(part):
        if tp_count == 2:
            return [part, swapped(part, "tp", 1)]
        return [lax.all_gather(part, "tp", axis=1, tiled=True)]

    def along(x, offset, senders):
        pairs = [(i, i ^ offset) for i in range(seq_count) if i // INNER in senders]
        return lax.ppermute(x, "seq", pairs)

    own_ids = neighbour_ids.reshape(wants)
    group_ids = jnp.stack([own_ids, swapped(own_ids, "seq", 2)])
    mate = swapped(neighbours, "seq", 1)
    incoming = passed_along(queries[:SPAN], "seq", -1)
    near = swapped(neighbours, "seq", INNER)
    across = along(neighbours, 3 * INNER, (1, 2)) if outer == 4 else near

    group_sources = group_ids // block_count
    group_ranks = slot_ranks(group_sources)
    sources = own_index ^ (INNER * jnp.arange(outer)[:, None] + jnp.arange(2))
    hit = (group_sources[None, :, None, None, :] == sources[:, None, :, None, None]) & (
        group_ranks[None, :, None, None, :] == jnp.arange(ranks)[None, None, None, :, None]
    )
    table = jnp.sum(
        jnp.where(hit, (group_ids % block_count)[None, :, None, None, :], 0), axis=-1
    )
    table = table.astype(jnp.int32).reshape(-1)

    own_sources = own_ids // block_count
    places = ((own_sources ^ own_index) * ranks + slot_ranks(own_sources)).astype(jnp.int32)
    order = jnp.arange(wants)
    spans = jnp.sum(
        jnp.where(places[None, :] == jnp.arange(slots)[:, None], order[None, :] // 2, 0), axis=1
    ).astype(jnp.int32)

    def pick(j, part, mate, *others):
        mine, outgoing = pick_blocks(j, ranks, after(table, *others), [part, mate])
        return mine, swapped(outgoing, "seq", 2)

    def join(picked, *others):
        return jnp.concatenate([picked[0], after(picked[1], *others)], axis=0)

    def attend(j, blocks, held, *others):
        scalars = (tp_index, after(spans, *others))
        return attend_part(j, cap, scalars, blocks, windows, weights, slots, held)

    weights = (key_weight.T, value_weight.T)
    picked = pick(0, neighbours, mate, weights, incoming)
    near, across = after((near, across), picked[0])
    parts = [neighbours, near]
    if outer == 4:
        inside = (own_index // INNER == 1) | (own_index // INNER == 2)
        second = along(near, 3 * INNER, (1, 2))
        outward = along(across, INNER, (1, 2))

    def part_of(j, *others):
        if outer != 4:
            low = j & -j
            return swapped(after(parts[j ^ low], *others), "seq", INNER * low)
        if j == 2:
            return jnp.where(inside, *after((second, outward), *others))
        return jnp.where(inside, *after((across, third), *others))

    wanted = join(picked)
    blocks = [all_features(wanted)]
    picked = pick(1, near, swapped(near, "seq", 1), wanted)
    windows = span_windows(after(queries, picked[0]), incoming, span_count)
    wanted = join(picked, windows)
    blocks.append(all_features(wanted))
    parts.append(part_of(2, wanted, blocks[0]))
    if outer == 4:
        third = along(second, INNER, (1, 2))
    picked = pick(2, parts[2], swapped(parts[2], "seq", 1))
    held = attend(0, blocks[0], None, picked[0])
    for j in range(3, outer):
        wanted = join(picked, held)
        blocks.append(all_features(wanted))
        parts.append(part_of(j, wanted, blocks[j - 2]))
        picked = pick(j, parts[j], swapped(parts[j], "seq", 1))
        held = attend(j - 2, blocks[j - 2], held, picked[0])
    wanted = join(picked, held)
    blocks.append(all_features(wanted))
    held = attend(outer - 2, blocks[outer - 2], held, wanted)
    held = attend(outer - 1, blocks[outer - 1], held)

    partials, log_totals = held
    last = mix_last(places, partials, log_totals, span_count)
    carried = passed_along(last, "seq", 1)
    rows = mix(places, partials, log_totals, span_count)
    return with_head(carried, rows)


def solution(mesh):
    in_specs = (P("seq", "tp"), P("seq", "tp", None), P(None, "tp"), P(None, "tp"), P("seq", None))
    out_specs = P("seq", "tp")
    return jax.shard_map(shards, mesh=mesh, in_specs=in_specs, out_specs=out_specs, check_vma=False)
```

```python
import jax
import jax.numpy as jnp
from jax import lax
from jax.experimental import pallas as pl
from jax.experimental.pallas import tpu as pltpu
from jax.sharding import PartitionSpec as P

HDIM = 128
SPAN = 64
PAIR = 2 * HDIM
INNER = 4
LANES = 128
VMEM_LIMIT = 56 * 1024 * 1024


LIGHT = pl.CostEstimate(flops=1000, bytes_accessed=1000, transcendentals=0)
HEAVY = pl.CostEstimate(flops=20 * 10**9, bytes_accessed=10**7, transcendentals=0)


def passed_along(x, axis, by):
    peers = lax.axis_size(axis)
    pairs = [(i, i + by) for i in range(peers) if 0 <= i + by < peers]
    return lax.ppermute(x, axis, pairs)


def swapped(x, axis, offset):
    peers = lax.axis_size(axis)
    return lax.ppermute(x, axis, [(i, i ^ offset) for i in range(peers)])


def slot_ranks(sources):
    positions = sources.shape[-1]
    alike = sources[..., :, None] == sources[..., None, :]
    earlier = jnp.arange(positions)[None, :] < jnp.arange(positions)[:, None]
    return jnp.sum(jnp.where(alike & earlier, 1, 0), axis=-1).astype(jnp.int32)


def windows_kernel(own_ref, next_ref, incoming_ref, out_ref):
    spans = out_ref.shape[0]
    last = pl.program_id(0) == pl.num_programs(0) - 1
    tile = 16
    cut = SPAN - tile
    late = lax.broadcasted_iota(jnp.int32, (tile, out_ref.shape[-1]), 0) == tile - 1
    for n in range(spans):
        if n + 1 < spans:
            later = own_ref[(n + 1) * SPAN : (n + 2) * SPAN, :]
        else:
            later = jnp.where(last, incoming_ref[...], next_ref[...])
        out_ref[n, :cut, :] = later[:cut]
        own = own_ref[n * SPAN + cut : (n + 1) * SPAN, :]
        out_ref[n, cut:, :] = jnp.where(
            late, own.astype(jnp.float32), later[cut:].astype(jnp.float32)
        ).astype(jnp.bfloat16)


def span_windows(queries, incoming, span_count):
    columns = queries.shape[-1]
    per = 4
    steps = span_count // per
    return pl.pallas_call(
        windows_kernel,
        grid=(steps,),
        in_specs=[
            pl.BlockSpec((per * SPAN, columns), lambda u: (u, 0)),
            pl.BlockSpec(
                (SPAN, columns), lambda u: (jnp.minimum(per * (u + 1), span_count - 1), 0)
            ),
            pl.BlockSpec((SPAN, columns), lambda u: (0, 0)),
        ],
        out_specs=pl.BlockSpec((per, SPAN, columns), lambda u: (u, 0, 0)),
        out_shape=jax.ShapeDtypeStruct((span_count, SPAN, columns), jnp.bfloat16),
        compiler_params=pltpu.CompilerParams(vmem_limit_bytes=VMEM_LIMIT),
        cost_estimate=LIGHT,
        name="windows",
    )(queries, queries, incoming)


def pick_kernel(part, ranks, table, *refs):
    sources, outs = refs[:2], refs[2:4]
    held, in_sems, out_sems = refs[-3:]
    fetches, stores = [], []
    for e in range(2):
        for a in range(2):
            for r in range(ranks):
                n = len(fetches)
                block = table[((part * 2 + e) * 2 + a) * ranks + r]
                fetches.append(
                    pltpu.make_async_copy(sources[a].at[block], held.at[n], in_sems.at[n])
                )
                stores.append(
                    pltpu.make_async_copy(held.at[n], outs[e].at[a * ranks + r], out_sems.at[n])
                )
    for fetch in fetches:
        fetch.start()
    for fetch, store in zip(fetches, stores):
        fetch.wait()
        store.start()
    for store in stores:
        store.wait()


def pick_blocks(part, ranks, table, sources):
    shape = sources[0].shape[1:]
    copies = 4 * ranks

    def body(*refs):
        pick_kernel(part, ranks, *refs)

    return pl.pallas_call(
        body,
        grid_spec=pltpu.PrefetchScalarGridSpec(
            num_scalar_prefetch=1,
            grid=(1,),
            in_specs=[pl.BlockSpec(memory_space=pltpu.HBM)] * 2,
            out_specs=[pl.BlockSpec(memory_space=pltpu.HBM)] * 2,
            scratch_shapes=[
                pltpu.VMEM((copies,) + shape, sources[0].dtype),
                pltpu.SemaphoreType.DMA((copies,)),
                pltpu.SemaphoreType.DMA((copies,)),
            ],
        ),
        out_shape=[jax.ShapeDtypeStruct((2 * ranks,) + shape, sources[0].dtype)] * 2,
        compiler_params=pltpu.CompilerParams(vmem_limit_bytes=VMEM_LIMIT),
        cost_estimate=LIGHT,
        name="pick_blocks",
    )(table, *sources)


def attend_kernel(part, cap, pieces, steps, tp_index, spans, *refs):
    x_refs = refs[:pieces]
    q_ref, wk_first, wk_next, wv_first, wv_next = refs[pieces : pieces + 5]
    out_ref, lse_ref, x_all, xt_all, scores_ref, weights_ref, k_even, v_even, k_odd, v_odd = refs[-10:]
    nlen = scores_ref.shape[-1]
    pairs = scores_ref.shape[0] // cap
    step = pl.program_id(0)
    scale = HDIM ** (-0.5)
    lanes = lax.broadcasted_iota(jnp.int32, (SPAN, LANES), 1)

    def project_keys(w_ref, out):
        out[...] = jnp.dot(w_ref[...], x_all[...], preferred_element_type=jnp.float32).astype(
            jnp.bfloat16
        )

    def project_values(w_ref, out):
        out[...] = jnp.dot(xt_all[...], w_ref[...], preferred_element_type=jnp.float32).astype(
            jnp.bfloat16
        )

    def score(k_ref):
        none = jnp.zeros((SPAN, HDIM), jnp.bfloat16)
        for pair in range(pairs):
            for i in range(cap):
                q = q_ref[spans[part * cap + i], :, pair * PAIR : (pair + 1) * PAIR]
                upper = jnp.concatenate([q[:, :HDIM], none], axis=1)
                lower = jnp.concatenate([none, q[:, HDIM:]], axis=1)
                scores_ref[pair * cap + i] = jnp.dot(
                    jnp.concatenate([upper, lower], axis=0),
                    k_ref[pair * PAIR : (pair + 1) * PAIR, i * nlen : (i + 1) * nlen],
                    preferred_element_type=jnp.float32,
                )

    def soften():
        for i in range(cap):
            held = lse_ref[i]
            for pair in range(pairs):
                scores = scores_ref[pair * cap + i]
                highest = jnp.max(scores, axis=1, keepdims=True)
                exponent = jnp.exp((scores - highest) * scale)
                totals = jnp.sum(exponent, axis=1, keepdims=True)
                weights_ref[pair * cap + i] = (exponent * (1.0 / totals)).astype(jnp.bfloat16)
                lse = highest * scale + jnp.log(totals)
                at = pairs * step + pair
                held = jnp.where(lanes == at, lse[:SPAN], held)
                held = jnp.where(lanes == LANES // 8 + at, lse[SPAN:], held)
            lse_ref[i] = held

    def blend(v_ref):
        for pair in range(pairs):
            cols = slice(pair * PAIR, (pair + 1) * PAIR)
            for i in range(cap):
                blended = jnp.dot(
                    weights_ref[pair * cap + i],
                    v_ref[i * nlen : (i + 1) * nlen, cols],
                    preferred_element_type=jnp.float32,
                )
                out_ref[i, :, cols] = jnp.concatenate(
                    [blended[:SPAN, :HDIM], blended[SPAN:, HDIM:]], axis=1
                ).astype(jnp.bfloat16)

    @pl.when(step == 0)
    def _():
        lse_ref[...] = jnp.zeros_like(lse_ref)
        for piece, x_ref in enumerate(x_refs):
            width = x_ref.shape[1]
            top = 0
            if pieces == 2:
                place = tp_index[0] if piece == 0 else 1 - tp_index[0]
                top = pl.multiple_of(place * width, 16)
            for i in range(cap):
                x_all[pl.ds(top, width), i * nlen : (i + 1) * nlen] = x_ref[i]
        for i in range(cap):
            at = slice(i * nlen, (i + 1) * nlen)
            xt_all[at, :] = x_all[:, at].T
        project_keys(wk_first, k_even)
        project_values(wv_first, v_even)

    def work(k_now, v_now, k_later, v_later):
        score(k_now)
        project_keys(wk_next, k_later)
        soften()
        project_values(wv_next, v_later)
        blend(v_now)

    def finish(k_now, v_now):
        score(k_now)
        soften()
        blend(v_now)

    if steps > 1:
        pl.when((step < steps - 1) & (step % 2 == 0))(lambda: work(k_even, v_even, k_odd, v_odd))
    if steps > 2:
        pl.when((step < steps - 1) & (step % 2 == 1))(lambda: work(k_odd, v_odd, k_even, v_even))
    ends = (k_even, v_even) if steps % 2 == 1 else (k_odd, v_odd)
    pl.when(step == steps - 1)(lambda: finish(*ends))


def attend_part(part, cap, scalars, blocks, windows, weights, slots, held):
    pieces = len(blocks)
    width, nlen = blocks[0].shape[1:]
    features = width * pieces
    columns = 2 * PAIR
    steps = windows.shape[-1] // columns

    in_specs = [pl.BlockSpec(x.shape, lambda t, *_: (0, 0, 0)) for x in blocks]
    operands = list(blocks)
    in_specs += [pl.BlockSpec((windows.shape[0], SPAN, columns), lambda t, *_: (0, 0, t))]
    operands += [windows]
    key_weight, value_weight = weights
    in_specs += [
        pl.BlockSpec((columns, features), lambda t, *_: (0, 0)),
        pl.BlockSpec((columns, features), lambda t, *_: (jnp.minimum(t + 1, steps - 1), 0)),
        pl.BlockSpec((features, columns), lambda t, *_: (0, 0)),
        pl.BlockSpec((features, columns), lambda t, *_: (0, jnp.minimum(t + 1, steps - 1))),
    ]
    operands += [key_weight] * 2 + [value_weight] * 2
    aliases = {}
    if held is not None:
        in_specs += [pl.BlockSpec(memory_space=pl.ANY)] * 2
        aliases = {2 + len(operands): 0, 3 + len(operands): 1}
        operands += list(held)
    keys = pltpu.VMEM((columns, cap * nlen), jnp.bfloat16)
    values = pltpu.VMEM((cap * nlen, columns), jnp.bfloat16)

    def body(*refs):
        attend_kernel(part, cap, pieces, steps, *refs)

    return pl.pallas_call(
        body,
        grid_spec=pltpu.PrefetchScalarGridSpec(
            num_scalar_prefetch=2,
            grid=(steps,),
            in_specs=in_specs,
            out_specs=[
                pl.BlockSpec((cap, SPAN, columns), lambda t, *_: (part, 0, t)),
                pl.BlockSpec((cap, SPAN, LANES), lambda t, *_: (part, 0, 0)),
            ],
            scratch_shapes=[
                pltpu.VMEM((features, cap * nlen), jnp.bfloat16),
                pltpu.VMEM((cap * nlen, features), jnp.bfloat16),
                pltpu.VMEM((2 * cap, 2 * SPAN, nlen), jnp.float32),
                pltpu.VMEM((2 * cap, 2 * SPAN, nlen), jnp.bfloat16),
                keys, values, keys, values,
            ],
        ),
        out_shape=[
            jax.ShapeDtypeStruct((slots,) + windows.shape[1:], jnp.bfloat16),
            jax.ShapeDtypeStruct((slots, SPAN, LANES), jnp.float32),
        ],
        input_output_aliases=aliases,
        compiler_params=pltpu.CompilerParams(vmem_limit_bytes=VMEM_LIMIT),
        cost_estimate=HEAVY,
        name="attend_part",
    )(*scalars, *operands)


def spread_matrix(columns):
    per = LANES // 8
    row = lax.broadcasted_iota(jnp.int32, (4 * per, columns), 0)
    head = lax.broadcasted_iota(jnp.int32, (4 * per, columns), 1) // HDIM
    own = 2 * (row % per) + (row // per) % 2
    return jnp.where(head == own, 1.0, 0.0).astype(jnp.bfloat16)


def first_shares(l0, l1):
    largest = jnp.maximum(l0, l1)
    e0, e1 = jnp.exp(l0 - largest), jnp.exp(l1 - largest)
    share = e0 / (e0 + e1)
    high = share.astype(jnp.bfloat16).astype(jnp.float32)
    low = pltpu.roll(share - high, LANES // 4, 1)
    lanes = lax.broadcasted_iota(jnp.int32, share.shape, 1)
    return jnp.where(lanes < LANES // 4, high, low).astype(jnp.bfloat16)[:, : LANES // 2]


def mixed(p0, p1, shares, spread, cols):
    share = jnp.dot(shares, spread[:, cols], preferred_element_type=jnp.float32)
    return p0[0, :, cols].astype(jnp.float32) * share + p1[0, :, cols].astype(jnp.float32) * (
        1.0 - share
    )


def mix_last_kernel(places, p0, p1, l0, l1, out_ref, spread):
    spread[...] = spread_matrix(out_ref.shape[-1])
    shares = first_shares(l0[0], l1[0])
    for pair in range(out_ref.shape[-1] // PAIR):
        cols = slice(pair * PAIR, (pair + 1) * PAIR)
        out_ref[:, cols] = mixed(p0, p1, shares, spread, cols).astype(jnp.bfloat16)


def mix_kernel(places, *refs):
    ins, (out_ref, before, spread) = refs[:-3], refs[-3:]
    tile = 16
    late = lax.broadcasted_iota(jnp.int32, (tile, PAIR), 0) == tile - 1

    @pl.when(pl.program_id(0) == 0)
    def _():
        spread[...] = spread_matrix(out_ref.shape[-1])

    for n in range(len(ins) // 4):
        p0, p1, l0, l1 = ins[4 * n : 4 * n + 4]
        shares = first_shares(l0[0], l1[0])
        top = n * SPAN
        cut = top + SPAN - tile
        out_ref[top:cut, :] = before[: SPAN - tile, :]
        for pair in range(out_ref.shape[-1] // PAIR):
            cols = slice(pair * PAIR, (pair + 1) * PAIR)
            result = mixed(p0, p1, shares, spread, cols)
            out_ref[cut : cut + tile, cols] = jnp.where(
                late, result[SPAN - tile :], before[SPAN - tile :, cols].astype(jnp.float32)
            ).astype(jnp.bfloat16)
            before[:, cols] = result.astype(jnp.bfloat16)


def mix_specs(partials, log_totals, span_of):
    def place(j, shape):
        return pl.BlockSpec((1,) + shape, lambda k, places: (places[2 * span_of(k) + j], 0, 0))

    rows, stats = partials.shape[1:], log_totals.shape[1:]
    return [place(0, rows), place(1, rows), place(0, stats), place(1, stats)]


def mix_last(places, partials, log_totals, span_count):
    columns = partials.shape[-1]
    return pl.pallas_call(
        mix_last_kernel,
        grid_spec=pltpu.PrefetchScalarGridSpec(
            num_scalar_prefetch=1,
            grid=(1,),
            in_specs=mix_specs(partials, log_totals, lambda k: span_count - 1),
            out_specs=pl.BlockSpec((SPAN, columns), lambda k, places: (0, 0)),
            scratch_shapes=[pltpu.VMEM((LANES // 2, columns), jnp.bfloat16)],
        ),
        out_shape=jax.ShapeDtypeStruct((SPAN, columns), jnp.bfloat16),
        cost_estimate=LIGHT,
        name="mix_last",
    )(places, partials, partials, log_totals, log_totals)


def mix(places, partials, log_totals, span_count):
    columns = partials.shape[-1]
    per = 4
    in_specs = []
    for n in range(per):
        in_specs += mix_specs(partials, log_totals, lambda k, n=n: per * k + n)
    return pl.pallas_call(
        mix_kernel,
        grid_spec=pltpu.PrefetchScalarGridSpec(
            num_scalar_prefetch=1,
            grid=(span_count // per,),
            in_specs=in_specs,
            out_specs=pl.BlockSpec((per * SPAN, columns), lambda k, places: (k, 0)),
            scratch_shapes=[
                pltpu.VMEM((SPAN, columns), jnp.bfloat16),
                pltpu.VMEM((LANES // 2, columns), jnp.bfloat16),
            ],
        ),
        out_shape=jax.ShapeDtypeStruct((span_count * SPAN, columns), jnp.bfloat16),
        compiler_params=pltpu.CompilerParams(vmem_limit_bytes=VMEM_LIMIT),
        cost_estimate=LIGHT,
        name="mix",
    )(places, *([partials, partials, log_totals, log_totals] * per))


def head_kernel(carried, rows, out_ref):
    early = lax.broadcasted_iota(jnp.int32, out_ref.shape, 0) < SPAN - 1
    out_ref[...] = jnp.where(
        early, carried[...].astype(jnp.float32), rows[...].astype(jnp.float32)
    ).astype(jnp.bfloat16)


def with_head(carried, mixed_rows):
    spec = pl.BlockSpec((SPAN, mixed_rows.shape[-1]), lambda k: (0, 0))
    return pl.pallas_call(
        head_kernel,
        grid=(1,),
        in_specs=[spec, spec],
        out_specs=spec,
        out_shape=jax.ShapeDtypeStruct(mixed_rows.shape, mixed_rows.dtype),
        input_output_aliases={1: 0},
        cost_estimate=LIGHT,
        name="with_head",
    )(carried, mixed_rows)


def after(values, *others):
    return lax.optimization_barrier((values, others))[0]


def shards(queries, neighbours, key_weight, value_weight, neighbour_ids):
    span_count = neighbour_ids.shape[0]
    seq_count, tp_count = lax.axis_size("seq"), lax.axis_size("tp")
    block_count = neighbours.shape[0]
    wants = 2 * span_count
    ranks = (wants + seq_count - 1) // seq_count
    outer = seq_count // INNER
    slots = seq_count * ranks
    cap = INNER * ranks
    own_index = lax.axis_index("seq")
    tp_index = lax.axis_index("tp").astype(jnp.int32).reshape(1)

    def all_features(part):
        if tp_count == 2:
            return [part, swapped(part, "tp", 1)]
        return [lax.all_gather(part, "tp", axis=1, tiled=True)]

    def along(x, offset, senders):
        pairs = [(i, i ^ offset) for i in range(seq_count) if i // INNER in senders]
        return lax.ppermute(x, "seq", pairs)

    own_ids = neighbour_ids.reshape(wants)
    group_ids = jnp.stack([own_ids, swapped(own_ids, "seq", 2)])
    mate = swapped(neighbours, "seq", 1)
    incoming = passed_along(queries[:SPAN], "seq", -1)
    near = swapped(neighbours, "seq", INNER)
    across = along(neighbours, 3 * INNER, (1, 2)) if outer == 4 else near

    group_sources = group_ids // block_count
    group_ranks = slot_ranks(group_sources)
    sources = own_index ^ (INNER * jnp.arange(outer)[:, None] + jnp.arange(2))
    hit = (group_sources[None, :, None, None, :] == sources[:, None, :, None, None]) & (
        group_ranks[None, :, None, None, :] == jnp.arange(ranks)[None, None, None, :, None]
    )
    table = jnp.sum(
        jnp.where(hit, (group_ids % block_count)[None, :, None, None, :], 0), axis=-1
    )
    table = table.astype(jnp.int32).reshape(-1)

    own_sources = own_ids // block_count
    places = ((own_sources ^ own_index) * ranks + slot_ranks(own_sources)).astype(jnp.int32)
    order = jnp.arange(wants)
    spans = jnp.sum(
        jnp.where(places[None, :] == jnp.arange(slots)[:, None], order[None, :] // 2, 0), axis=1
    ).astype(jnp.int32)

    def pick(j, part, mate, *others):
        mine, outgoing = pick_blocks(j, ranks, after(table, *others), [part, mate])
        return mine, swapped(outgoing, "seq", 2)

    def join(picked, *others):
        return jnp.concatenate([picked[0], after(picked[1], *others)], axis=0)

    def attend(j, blocks, held, *others):
        scalars = (tp_index, after(spans, *others))
        return attend_part(j, cap, scalars, blocks, windows, weights, slots, held)

    weights = (key_weight.T, value_weight)
    picked = pick(0, neighbours, mate, weights[0], incoming)
    near, across = after((near, across), picked[0])
    parts = [neighbours, near]
    if outer == 4:
        inside = (own_index // INNER == 1) | (own_index // INNER == 2)
        second = along(near, 3 * INNER, (1, 2))
        outward = along(across, INNER, (1, 2))

    def part_of(j, *others):
        if outer != 4:
            low = j & -j
            return swapped(after(parts[j ^ low], *others), "seq", INNER * low)
        if j == 2:
            return jnp.where(inside, *after((second, outward), *others))
        return jnp.where(inside, *after((across, third), *others))

    wanted = join(picked)
    blocks = [all_features(wanted)]
    picked = pick(1, near, swapped(near, "seq", 1), wanted)
    windows = span_windows(after(queries, picked[0]), incoming, span_count)
    wanted = join(picked, windows)
    blocks.append(all_features(wanted))
    parts.append(part_of(2, wanted, blocks[0]))
    if outer == 4:
        third = along(second, INNER, (1, 2))
    picked = pick(2, parts[2], swapped(parts[2], "seq", 1))
    held = attend(0, blocks[0], None, picked[0])
    for j in range(3, outer):
        wanted = join(picked, held)
        blocks.append(all_features(wanted))
        parts.append(part_of(j, wanted, blocks[j - 2]))
        picked = pick(j, parts[j], swapped(parts[j], "seq", 1))
        held = attend(j - 2, blocks[j - 2], held, picked[0])
    wanted = join(picked, held)
    blocks.append(all_features(wanted))
    held = attend(outer - 2, blocks[outer - 2], held, wanted)
    held = attend(outer - 1, blocks[outer - 1], held)

    partials, log_totals = held
    last = mix_last(places, partials, log_totals, span_count)
    carried = passed_along(last, "seq", 1)
    rows = mix(places, partials, log_totals, span_count)
    return with_head(carried, rows)


def solution(mesh):
    in_specs = (P("seq", "tp"), P("seq", "tp", None), P(None, "tp"), P(None, "tp"), P("seq", None))
    out_specs = P("seq", "tp")
    return jax.shard_map(shards, mesh=mesh, in_specs=in_specs, out_specs=out_specs, check_vma=False)
```

```python
import jax
import jax.numpy as jnp
from jax import lax
from jax.experimental import pallas as pl
from jax.experimental.pallas import tpu as pltpu
from jax.sharding import PartitionSpec as P

HDIM = 128
SPAN = 64
PAIR = 2 * HDIM
INNER = 4
LANES = 128
VMEM_LIMIT = 56 * 1024 * 1024


LIGHT = pl.CostEstimate(flops=1000, bytes_accessed=1000, transcendentals=0)
HEAVY = pl.CostEstimate(flops=20 * 10**9, bytes_accessed=10**7, transcendentals=0)


def passed_along(x, axis, by):
    peers = lax.axis_size(axis)
    pairs = [(i, i + by) for i in range(peers) if 0 <= i + by < peers]
    return lax.ppermute(x, axis, pairs)


def swapped(x, axis, offset):
    peers = lax.axis_size(axis)
    return lax.ppermute(x, axis, [(i, i ^ offset) for i in range(peers)])


def slot_ranks(sources):
    positions = sources.shape[-1]
    alike = sources[..., :, None] == sources[..., None, :]
    earlier = jnp.arange(positions)[None, :] < jnp.arange(positions)[:, None]
    return jnp.sum(jnp.where(alike & earlier, 1, 0), axis=-1).astype(jnp.int32)


def windows_kernel(own_ref, next_ref, incoming_ref, out_ref):
    spans = out_ref.shape[0]
    last = pl.program_id(0) == pl.num_programs(0) - 1
    tile = 16
    cut = SPAN - tile
    late = lax.broadcasted_iota(jnp.int32, (tile, out_ref.shape[-1]), 0) == tile - 1
    for n in range(spans):
        if n + 1 < spans:
            later = own_ref[(n + 1) * SPAN : (n + 2) * SPAN, :]
        else:
            later = jnp.where(last, incoming_ref[...], next_ref[...])
        out_ref[n, :cut, :] = later[:cut]
        own = own_ref[n * SPAN + cut : (n + 1) * SPAN, :]
        out_ref[n, cut:, :] = jnp.where(
            late, own.astype(jnp.float32), later[cut:].astype(jnp.float32)
        ).astype(jnp.bfloat16)


def span_windows(queries, incoming, span_count):
    columns = queries.shape[-1]
    per = 4
    steps = span_count // per
    return pl.pallas_call(
        windows_kernel,
        grid=(steps,),
        in_specs=[
            pl.BlockSpec((per * SPAN, columns), lambda u: (u, 0)),
            pl.BlockSpec(
                (SPAN, columns), lambda u: (jnp.minimum(per * (u + 1), span_count - 1), 0)
            ),
            pl.BlockSpec((SPAN, columns), lambda u: (0, 0)),
        ],
        out_specs=pl.BlockSpec((per, SPAN, columns), lambda u: (u, 0, 0)),
        out_shape=jax.ShapeDtypeStruct((span_count, SPAN, columns), jnp.bfloat16),
        compiler_params=pltpu.CompilerParams(vmem_limit_bytes=VMEM_LIMIT),
        cost_estimate=LIGHT,
        name="windows",
    )(queries, queries, incoming)


def pick_kernel(part, ranks, table, *refs):
    sources, outs = refs[:2], refs[2:4]
    held, in_sems, out_sems = refs[-3:]
    fetches, stores = [], []
    for e in range(2):
        for a in range(2):
            for r in range(ranks):
                n = len(fetches)
                block = table[((part * 2 + e) * 2 + a) * ranks + r]
                fetches.append(
                    pltpu.make_async_copy(sources[a].at[block], held.at[n], in_sems.at[n])
                )
                stores.append(
                    pltpu.make_async_copy(held.at[n], outs[e].at[a * ranks + r], out_sems.at[n])
                )
    for fetch in fetches:
        fetch.start()
    for fetch, store in zip(fetches, stores):
        fetch.wait()
        store.start()
    for store in stores:
        store.wait()


def pick_blocks(part, ranks, table, sources):
    shape = sources[0].shape[1:]
    copies = 4 * ranks

    def body(*refs):
        pick_kernel(part, ranks, *refs)

    return pl.pallas_call(
        body,
        grid_spec=pltpu.PrefetchScalarGridSpec(
            num_scalar_prefetch=1,
            grid=(1,),
            in_specs=[pl.BlockSpec(memory_space=pltpu.HBM)] * 2,
            out_specs=[pl.BlockSpec(memory_space=pltpu.HBM)] * 2,
            scratch_shapes=[
                pltpu.VMEM((copies,) + shape, sources[0].dtype),
                pltpu.SemaphoreType.DMA((copies,)),
                pltpu.SemaphoreType.DMA((copies,)),
            ],
        ),
        out_shape=[jax.ShapeDtypeStruct((2 * ranks,) + shape, sources[0].dtype)] * 2,
        compiler_params=pltpu.CompilerParams(vmem_limit_bytes=VMEM_LIMIT),
        cost_estimate=LIGHT,
        name="pick_blocks",
    )(table, *sources)


def attend_kernel(part, cap, pieces, steps, tp_index, spans, *refs):
    x_refs = refs[:pieces]
    q_ref, wk_first, wk_next, wv_first, wv_next = refs[pieces : pieces + 5]
    out_ref, lse_ref, x_all, xt_all, scores_ref, weights_ref, k_even, v_even, k_odd, v_odd = refs[-10:]
    nlen = scores_ref.shape[-1]
    pairs = scores_ref.shape[0] // cap
    step = pl.program_id(0)
    scale = HDIM ** (-0.5)
    lanes = lax.broadcasted_iota(jnp.int32, (SPAN, LANES), 1)

    def deep_product(a_ref, b_ref):
        depth = a_ref.shape[1]
        whole = depth // PAIR * PAIR
        total = jnp.dot(a_ref[:, :whole], b_ref[:whole, :], preferred_element_type=jnp.float32)
        if whole < depth:
            total += jnp.dot(a_ref[:, whole:], b_ref[whole:, :], preferred_element_type=jnp.float32)
        return total.astype(jnp.bfloat16)

    def project_keys(w_ref, out):
        out[...] = deep_product(w_ref, x_all)

    def project_values(w_ref, out):
        out[...] = deep_product(xt_all, w_ref)

    def score(k_ref):
        none = jnp.zeros((SPAN, HDIM), jnp.bfloat16)
        for pair in range(pairs):
            for i in range(cap):
                q = q_ref[spans[part * cap + i], :, pair * PAIR : (pair + 1) * PAIR]
                upper = jnp.concatenate([q[:, :HDIM], none], axis=1)
                lower = jnp.concatenate([none, q[:, HDIM:]], axis=1)
                scores_ref[pair * cap + i] = jnp.dot(
                    jnp.concatenate([upper, lower], axis=0),
                    k_ref[pair * PAIR : (pair + 1) * PAIR, i * nlen : (i + 1) * nlen],
                    preferred_element_type=jnp.float32,
                )

    def soften():
        for i in range(cap):
            held = lse_ref[i]
            for pair in range(pairs):
                scores = scores_ref[pair * cap + i]
                highest = jnp.max(scores, axis=1, keepdims=True)
                exponent = jnp.exp((scores - highest) * scale)
                totals = jnp.sum(exponent, axis=1, keepdims=True)
                weights_ref[pair * cap + i] = (exponent * (1.0 / totals)).astype(jnp.bfloat16)
                lse = highest * scale + jnp.log(totals)
                at = pairs * step + pair
                held = jnp.where(lanes == at, lse[:SPAN], held)
                held = jnp.where(lanes == LANES // 8 + at, lse[SPAN:], held)
            lse_ref[i] = held

    def blend(v_ref):
        for pair in range(pairs):
            cols = slice(pair * PAIR, (pair + 1) * PAIR)
            for i in range(cap):
                blended = jnp.dot(
                    weights_ref[pair * cap + i],
                    v_ref[i * nlen : (i + 1) * nlen, cols],
                    preferred_element_type=jnp.float32,
                )
                out_ref[i, :, cols] = jnp.concatenate(
                    [blended[:SPAN, :HDIM], blended[SPAN:, HDIM:]], axis=1
                ).astype(jnp.bfloat16)

    @pl.when(step == 0)
    def _():
        lse_ref[...] = jnp.zeros_like(lse_ref)
        for piece, x_ref in enumerate(x_refs):
            width = x_ref.shape[1]
            top = 0
            if pieces == 2:
                place = tp_index[0] if piece == 0 else 1 - tp_index[0]
                top = pl.multiple_of(place * width, 16)
            for i in range(cap):
                x_all[pl.ds(top, width), i * nlen : (i + 1) * nlen] = x_ref[i]
        for i in range(cap):
            at = slice(i * nlen, (i + 1) * nlen)
            xt_all[at, :] = x_all[:, at].T
        project_keys(wk_first, k_even)
        project_values(wv_first, v_even)

    def work(k_now, v_now, k_later, v_later):
        score(k_now)
        project_keys(wk_next, k_later)
        soften()
        project_values(wv_next, v_later)
        blend(v_now)

    def finish(k_now, v_now):
        score(k_now)
        soften()
        blend(v_now)

    if steps > 1:
        pl.when((step < steps - 1) & (step % 2 == 0))(lambda: work(k_even, v_even, k_odd, v_odd))
    if steps > 2:
        pl.when((step < steps - 1) & (step % 2 == 1))(lambda: work(k_odd, v_odd, k_even, v_even))
    ends = (k_even, v_even) if steps % 2 == 1 else (k_odd, v_odd)
    pl.when(step == steps - 1)(lambda: finish(*ends))


def attend_part(part, cap, scalars, blocks, windows, weights, slots, held):
    pieces = len(blocks)
    width, nlen = blocks[0].shape[1:]
    features = width * pieces
    columns = 2 * PAIR
    steps = windows.shape[-1] // columns

    in_specs = [pl.BlockSpec(x.shape, lambda t, *_: (0, 0, 0)) for x in blocks]
    operands = list(blocks)
    in_specs += [pl.BlockSpec((windows.shape[0], SPAN, columns), lambda t, *_: (0, 0, t))]
    operands += [windows]
    key_weight, value_weight = weights
    in_specs += [
        pl.BlockSpec((columns, features), lambda t, *_: (0, 0)),
        pl.BlockSpec((columns, features), lambda t, *_: (jnp.minimum(t + 1, steps - 1), 0)),
        pl.BlockSpec((features, columns), lambda t, *_: (0, 0)),
        pl.BlockSpec((features, columns), lambda t, *_: (0, jnp.minimum(t + 1, steps - 1))),
    ]
    operands += [key_weight] * 2 + [value_weight] * 2
    aliases = {}
    if held is not None:
        in_specs += [pl.BlockSpec(memory_space=pl.ANY)] * 2
        aliases = {2 + len(operands): 0, 3 + len(operands): 1}
        operands += list(held)
    keys = pltpu.VMEM((columns, cap * nlen), jnp.bfloat16)
    values = pltpu.VMEM((cap * nlen, columns), jnp.bfloat16)

    def body(*refs):
        attend_kernel(part, cap, pieces, steps, *refs)

    return pl.pallas_call(
        body,
        grid_spec=pltpu.PrefetchScalarGridSpec(
            num_scalar_prefetch=2,
            grid=(steps,),
            in_specs=in_specs,
            out_specs=[
                pl.BlockSpec((cap, SPAN, columns), lambda t, *_: (part, 0, t)),
                pl.BlockSpec((cap, SPAN, LANES), lambda t, *_: (part, 0, 0)),
            ],
            scratch_shapes=[
                pltpu.VMEM((features, cap * nlen), jnp.bfloat16),
                pltpu.VMEM((cap * nlen, features), jnp.bfloat16),
                pltpu.VMEM((2 * cap, 2 * SPAN, nlen), jnp.float32),
                pltpu.VMEM((2 * cap, 2 * SPAN, nlen), jnp.bfloat16),
                keys, values, keys, values,
            ],
        ),
        out_shape=[
            jax.ShapeDtypeStruct((slots,) + windows.shape[1:], jnp.bfloat16),
            jax.ShapeDtypeStruct((slots, SPAN, LANES), jnp.float32),
        ],
        input_output_aliases=aliases,
        compiler_params=pltpu.CompilerParams(vmem_limit_bytes=VMEM_LIMIT),
        cost_estimate=HEAVY,
        name="attend_part",
    )(*scalars, *operands)


def spread_matrix(columns):
    per = LANES // 8
    row = lax.broadcasted_iota(jnp.int32, (4 * per, columns), 0)
    head = lax.broadcasted_iota(jnp.int32, (4 * per, columns), 1) // HDIM
    own = 2 * (row % per) + (row // per) % 2
    return jnp.where(head == own, 1.0, 0.0).astype(jnp.bfloat16)


def first_shares(l0, l1):
    largest = jnp.maximum(l0, l1)
    e0, e1 = jnp.exp(l0 - largest), jnp.exp(l1 - largest)
    share = e0 / (e0 + e1)
    high = share.astype(jnp.bfloat16).astype(jnp.float32)
    low = pltpu.roll(share - high, LANES // 4, 1)
    lanes = lax.broadcasted_iota(jnp.int32, share.shape, 1)
    return jnp.where(lanes < LANES // 4, high, low).astype(jnp.bfloat16)[:, : LANES // 2]


def mixed(p0, p1, shares, spread, cols):
    share = jnp.dot(shares, spread[:, cols], preferred_element_type=jnp.float32)
    return p0[0, :, cols].astype(jnp.float32) * share + p1[0, :, cols].astype(jnp.float32) * (
        1.0 - share
    )


def mix_last_kernel(places, p0, p1, l0, l1, out_ref, spread):
    spread[...] = spread_matrix(out_ref.shape[-1])
    shares = first_shares(l0[0], l1[0])
    for pair in range(out_ref.shape[-1] // PAIR):
        cols = slice(pair * PAIR, (pair + 1) * PAIR)
        out_ref[:, cols] = mixed(p0, p1, shares, spread, cols).astype(jnp.bfloat16)


def mix_kernel(places, *refs):
    ins, (out_ref, before, spread) = refs[:-3], refs[-3:]
    tile = 16
    late = lax.broadcasted_iota(jnp.int32, (tile, PAIR), 0) == tile - 1

    @pl.when(pl.program_id(0) == 0)
    def _():
        spread[...] = spread_matrix(out_ref.shape[-1])

    for n in range(len(ins) // 4):
        p0, p1, l0, l1 = ins[4 * n : 4 * n + 4]
        shares = first_shares(l0[0], l1[0])
        top = n * SPAN
        cut = top + SPAN - tile
        out_ref[top:cut, :] = before[: SPAN - tile, :]
        for pair in range(out_ref.shape[-1] // PAIR):
            cols = slice(pair * PAIR, (pair + 1) * PAIR)
            result = mixed(p0, p1, shares, spread, cols)
            out_ref[cut : cut + tile, cols] = jnp.where(
                late, result[SPAN - tile :], before[SPAN - tile :, cols].astype(jnp.float32)
            ).astype(jnp.bfloat16)
            before[:, cols] = result.astype(jnp.bfloat16)


def mix_specs(partials, log_totals, span_of):
    def place(j, shape):
        return pl.BlockSpec((1,) + shape, lambda k, places: (places[2 * span_of(k) + j], 0, 0))

    rows, stats = partials.shape[1:], log_totals.shape[1:]
    return [place(0, rows), place(1, rows), place(0, stats), place(1, stats)]


def mix_last(places, partials, log_totals, span_count):
    columns = partials.shape[-1]
    return pl.pallas_call(
        mix_last_kernel,
        grid_spec=pltpu.PrefetchScalarGridSpec(
            num_scalar_prefetch=1,
            grid=(1,),
            in_specs=mix_specs(partials, log_totals, lambda k: span_count - 1),
            out_specs=pl.BlockSpec((SPAN, columns), lambda k, places: (0, 0)),
            scratch_shapes=[pltpu.VMEM((LANES // 2, columns), jnp.bfloat16)],
        ),
        out_shape=jax.ShapeDtypeStruct((SPAN, columns), jnp.bfloat16),
        cost_estimate=LIGHT,
        name="mix_last",
    )(places, partials, partials, log_totals, log_totals)


def mix(places, partials, log_totals, span_count):
    columns = partials.shape[-1]
    per = 4
    in_specs = []
    for n in range(per):
        in_specs += mix_specs(partials, log_totals, lambda k, n=n: per * k + n)
    return pl.pallas_call(
        mix_kernel,
        grid_spec=pltpu.PrefetchScalarGridSpec(
            num_scalar_prefetch=1,
            grid=(span_count // per,),
            in_specs=in_specs,
            out_specs=pl.BlockSpec((per * SPAN, columns), lambda k, places: (k, 0)),
            scratch_shapes=[
                pltpu.VMEM((SPAN, columns), jnp.bfloat16),
                pltpu.VMEM((LANES // 2, columns), jnp.bfloat16),
            ],
        ),
        out_shape=jax.ShapeDtypeStruct((span_count * SPAN, columns), jnp.bfloat16),
        compiler_params=pltpu.CompilerParams(vmem_limit_bytes=VMEM_LIMIT),
        cost_estimate=LIGHT,
        name="mix",
    )(places, *([partials, partials, log_totals, log_totals] * per))


def head_kernel(carried, rows, out_ref):
    early = lax.broadcasted_iota(jnp.int32, out_ref.shape, 0) < SPAN - 1
    out_ref[...] = jnp.where(
        early, carried[...].astype(jnp.float32), rows[...].astype(jnp.float32)
    ).astype(jnp.bfloat16)


def with_head(carried, mixed_rows):
    spec = pl.BlockSpec((SPAN, mixed_rows.shape[-1]), lambda k: (0, 0))
    return pl.pallas_call(
        head_kernel,
        grid=(1,),
        in_specs=[spec, spec],
        out_specs=spec,
        out_shape=jax.ShapeDtypeStruct(mixed_rows.shape, mixed_rows.dtype),
        input_output_aliases={1: 0},
        cost_estimate=LIGHT,
        name="with_head",
    )(carried, mixed_rows)


def after(values, *others):
    return lax.optimization_barrier((values, others))[0]


def shards(queries, neighbours, key_weight, value_weight, neighbour_ids):
    span_count = neighbour_ids.shape[0]
    seq_count, tp_count = lax.axis_size("seq"), lax.axis_size("tp")
    block_count = neighbours.shape[0]
    wants = 2 * span_count
    ranks = (wants + seq_count - 1) // seq_count
    outer = seq_count // INNER
    slots = seq_count * ranks
    cap = INNER * ranks
    own_index = lax.axis_index("seq")
    tp_index = lax.axis_index("tp").astype(jnp.int32).reshape(1)

    def all_features(part):
        if tp_count == 2:
            return [part, swapped(part, "tp", 1)]
        return [lax.all_gather(part, "tp", axis=1, tiled=True)]

    def along(x, offset, senders):
        pairs = [(i, i ^ offset) for i in range(seq_count) if i // INNER in senders]
        return lax.ppermute(x, "seq", pairs)

    own_ids = neighbour_ids.reshape(wants)
    group_ids = jnp.stack([own_ids, swapped(own_ids, "seq", 2)])
    mate = swapped(neighbours, "seq", 1)
    incoming = passed_along(queries[:SPAN], "seq", -1)
    near = swapped(neighbours, "seq", INNER)
    across = along(neighbours, 3 * INNER, (1, 2)) if outer == 4 else near

    group_sources = group_ids // block_count
    group_ranks = slot_ranks(group_sources)
    sources = own_index ^ (INNER * jnp.arange(outer)[:, None] + jnp.arange(2))
    hit = (group_sources[None, :, None, None, :] == sources[:, None, :, None, None]) & (
        group_ranks[None, :, None, None, :] == jnp.arange(ranks)[None, None, None, :, None]
    )
    table = jnp.sum(
        jnp.where(hit, (group_ids % block_count)[None, :, None, None, :], 0), axis=-1
    )
    table = table.astype(jnp.int32).reshape(-1)

    own_sources = own_ids // block_count
    places = ((own_sources ^ own_index) * ranks + slot_ranks(own_sources)).astype(jnp.int32)
    order = jnp.arange(wants)
    spans = jnp.sum(
        jnp.where(places[None, :] == jnp.arange(slots)[:, None], order[None, :] // 2, 0), axis=1
    ).astype(jnp.int32)

    def pick(j, part, mate, *others):
        mine, outgoing = pick_blocks(j, ranks, after(table, *others), [part, mate])
        return mine, swapped(outgoing, "seq", 2)

    def join(picked, *others):
        return jnp.concatenate([picked[0], after(picked[1], *others)], axis=0)

    def attend(j, blocks, held, *others):
        scalars = (tp_index, after(spans, *others))
        return attend_part(j, cap, scalars, blocks, windows, weights, slots, held)

    weights = (key_weight.T, value_weight)
    picked = pick(0, neighbours, mate, weights[0], incoming)
    near, across = after((near, across), picked[0])
    parts = [neighbours, near]
    if outer == 4:
        inside = (own_index // INNER == 1) | (own_index // INNER == 2)
        second = along(near, 3 * INNER, (1, 2))
        outward = along(across, INNER, (1, 2))

    def part_of(j, *others):
        if outer != 4:
            low = j & -j
            return swapped(after(parts[j ^ low], *others), "seq", INNER * low)
        if j == 2:
            return jnp.where(inside, *after((second, outward), *others))
        return jnp.where(inside, *after((across, third), *others))

    wanted = join(picked)
    blocks = [all_features(wanted)]
    picked = pick(1, near, swapped(near, "seq", 1), wanted)
    windows = span_windows(after(queries, picked[0]), incoming, span_count)
    wanted = join(picked, windows)
    blocks.append(all_features(wanted))
    parts.append(part_of(2, wanted, blocks[0]))
    if outer == 4:
        third = along(second, INNER, (1, 2))
    picked = pick(2, parts[2], swapped(parts[2], "seq", 1))
    held = attend(0, blocks[0], None, picked[0])
    for j in range(3, outer):
        wanted = join(picked, held)
        blocks.append(all_features(wanted))
        parts.append(part_of(j, wanted, blocks[j - 2]))
        picked = pick(j, parts[j], swapped(parts[j], "seq", 1))
        held = attend(j - 2, blocks[j - 2], held, picked[0])
    wanted = join(picked, held)
    blocks.append(all_features(wanted))
    held = attend(outer - 2, blocks[outer - 2], held, wanted)
    held = attend(outer - 1, blocks[outer - 1], held)

    partials, log_totals = held
    last = mix_last(places, partials, log_totals, span_count)
    carried = passed_along(last, "seq", 1)
    rows = mix(places, partials, log_totals, span_count)
    return with_head(carried, rows)


def solution(mesh):
    in_specs = (P("seq", "tp"), P("seq", "tp", None), P(None, "tp"), P(None, "tp"), P("seq", None))
    out_specs = P("seq", "tp")
    return jax.shard_map(shards, mesh=mesh, in_specs=in_specs, out_specs=out_specs, check_vma=False)
```

```python
import jax
import jax.numpy as jnp
from jax import lax
from jax.experimental import pallas as pl
from jax.experimental.pallas import tpu as pltpu
from jax.sharding import PartitionSpec as P

HDIM = 128
SPAN = 64
PAIR = 2 * HDIM
INNER = 4
LANES = 128
VMEM_LIMIT = 56 * 1024 * 1024


LIGHT = pl.CostEstimate(flops=1000, bytes_accessed=1000, transcendentals=0)
HEAVY = pl.CostEstimate(flops=20 * 10**9, bytes_accessed=10**7, transcendentals=0)


def passed_along(x, axis, by):
    peers = lax.axis_size(axis)
    pairs = [(i, i + by) for i in range(peers) if 0 <= i + by < peers]
    return lax.ppermute(x, axis, pairs)


def swapped(x, axis, offset):
    peers = lax.axis_size(axis)
    return lax.ppermute(x, axis, [(i, i ^ offset) for i in range(peers)])


def slot_ranks(sources):
    positions = sources.shape[-1]
    alike = sources[..., :, None] == sources[..., None, :]
    earlier = jnp.arange(positions)[None, :] < jnp.arange(positions)[:, None]
    return jnp.sum(jnp.where(alike & earlier, 1, 0), axis=-1).astype(jnp.int32)


def windows_kernel(own_ref, next_ref, incoming_ref, out_ref):
    spans = out_ref.shape[0]
    last = pl.program_id(0) == pl.num_programs(0) - 1
    tile = 16
    cut = SPAN - tile
    late = lax.broadcasted_iota(jnp.int32, (tile, out_ref.shape[-1]), 0) == tile - 1
    for n in range(spans):
        if n + 1 < spans:
            later = own_ref[(n + 1) * SPAN : (n + 2) * SPAN, :]
        else:
            later = jnp.where(last, incoming_ref[...], next_ref[...])
        out_ref[n, :cut, :] = later[:cut]
        own = own_ref[n * SPAN + cut : (n + 1) * SPAN, :]
        out_ref[n, cut:, :] = jnp.where(
            late, own.astype(jnp.float32), later[cut:].astype(jnp.float32)
        ).astype(jnp.bfloat16)


def span_windows(queries, incoming, span_count):
    columns = queries.shape[-1]
    per = 4
    steps = span_count // per
    return pl.pallas_call(
        windows_kernel,
        grid=(steps,),
        in_specs=[
            pl.BlockSpec((per * SPAN, columns), lambda u: (u, 0)),
            pl.BlockSpec(
                (SPAN, columns), lambda u: (jnp.minimum(per * (u + 1), span_count - 1), 0)
            ),
            pl.BlockSpec((SPAN, columns), lambda u: (0, 0)),
        ],
        out_specs=pl.BlockSpec((per, SPAN, columns), lambda u: (u, 0, 0)),
        out_shape=jax.ShapeDtypeStruct((span_count, SPAN, columns), jnp.bfloat16),
        compiler_params=pltpu.CompilerParams(vmem_limit_bytes=VMEM_LIMIT),
        cost_estimate=LIGHT,
        name="windows",
    )(queries, queries, incoming)


def pick_kernel(part, ranks, table, *refs):
    sources, outs = refs[:2], refs[2:4]
    held, in_sems, out_sems = refs[-3:]
    fetches, stores = [], []
    for e in range(2):
        for a in range(2):
            for r in range(ranks):
                n = len(fetches)
                block = table[((part * 2 + e) * 2 + a) * ranks + r]
                fetches.append(
                    pltpu.make_async_copy(sources[a].at[block], held.at[n], in_sems.at[n])
                )
                stores.append(
                    pltpu.make_async_copy(held.at[n], outs[e].at[a * ranks + r], out_sems.at[n])
                )
    for fetch in fetches:
        fetch.start()
    for fetch, store in zip(fetches, stores):
        fetch.wait()
        store.start()
    for store in stores:
        store.wait()


def pick_blocks(part, ranks, table, sources):
    shape = sources[0].shape[1:]
    copies = 4 * ranks

    def body(*refs):
        pick_kernel(part, ranks, *refs)

    return pl.pallas_call(
        body,
        grid_spec=pltpu.PrefetchScalarGridSpec(
            num_scalar_prefetch=1,
            grid=(1,),
            in_specs=[pl.BlockSpec(memory_space=pltpu.HBM)] * 2,
            out_specs=[pl.BlockSpec(memory_space=pltpu.HBM)] * 2,
            scratch_shapes=[
                pltpu.VMEM((copies,) + shape, sources[0].dtype),
                pltpu.SemaphoreType.DMA((copies,)),
                pltpu.SemaphoreType.DMA((copies,)),
            ],
        ),
        out_shape=[jax.ShapeDtypeStruct((2 * ranks,) + shape, sources[0].dtype)] * 2,
        compiler_params=pltpu.CompilerParams(vmem_limit_bytes=VMEM_LIMIT),
        cost_estimate=LIGHT,
        name="pick_blocks",
    )(table, *sources)


def attend_kernel(first, cap, pieces, groups, steps, tp_index, spans, *refs):
    count = pieces * groups
    x_refs = refs[:count]
    q_ref, wk_first, wk_next, wv_first, wv_next = refs[count : count + 5]
    out_ref, lse_ref, x_all, xt_all, scores_ref, weights_ref, k_even, v_even, k_odd, v_odd = refs[-10:]
    nlen = scores_ref.shape[-1]
    pairs = scores_ref.shape[0] // cap
    step = pl.program_id(0)
    scale = HDIM ** (-0.5)
    lanes = lax.broadcasted_iota(jnp.int32, (SPAN, LANES), 1)

    def project_keys(w_ref, out):
        out[...] = jnp.dot(w_ref[...], x_all[...], preferred_element_type=jnp.float32).astype(
            jnp.bfloat16
        )

    def project_values(w_ref, out):
        out[...] = jnp.dot(xt_all[...], w_ref[...], preferred_element_type=jnp.float32).astype(
            jnp.bfloat16
        )

    def score(k_ref):
        none = jnp.zeros((SPAN, HDIM), jnp.bfloat16)
        for pair in range(pairs):
            for i in range(cap):
                q = q_ref[spans[first + i], :, pair * PAIR : (pair + 1) * PAIR]
                upper = jnp.concatenate([q[:, :HDIM], none], axis=1)
                lower = jnp.concatenate([none, q[:, HDIM:]], axis=1)
                scores_ref[pair * cap + i] = jnp.dot(
                    jnp.concatenate([upper, lower], axis=0),
                    k_ref[pair * PAIR : (pair + 1) * PAIR, i * nlen : (i + 1) * nlen],
                    preferred_element_type=jnp.float32,
                )

    def soften():
        for i in range(cap):
            held = lse_ref[i]
            for pair in range(pairs):
                scores = scores_ref[pair * cap + i]
                highest = jnp.max(scores, axis=1, keepdims=True)
                exponent = jnp.exp((scores - highest) * scale)
                totals = jnp.sum(exponent, axis=1, keepdims=True)
                weights_ref[pair * cap + i] = (exponent * (1.0 / totals)).astype(jnp.bfloat16)
                lse = highest * scale + jnp.log(totals)
                at = pairs * step + pair
                held = jnp.where(lanes == at, lse[:SPAN], held)
                held = jnp.where(lanes == LANES // 8 + at, lse[SPAN:], held)
            lse_ref[i] = held

    def blend(v_ref):
        for pair in range(pairs):
            cols = slice(pair * PAIR, (pair + 1) * PAIR)
            for i in range(cap):
                blended = jnp.dot(
                    weights_ref[pair * cap + i],
                    v_ref[i * nlen : (i + 1) * nlen, cols],
                    preferred_element_type=jnp.float32,
                )
                out_ref[i, :, cols] = jnp.concatenate(
                    [blended[:SPAN, :HDIM], blended[SPAN:, HDIM:]], axis=1
                ).astype(jnp.bfloat16)

    @pl.when(step == 0)
    def _():
        lse_ref[...] = jnp.zeros_like(lse_ref)
        per = cap // groups
        for n, x_ref in enumerate(x_refs):
            group, piece = n // pieces, n % pieces
            width = x_ref.shape[1]
            top = 0
            if pieces == 2:
                place = tp_index[0] if piece == 0 else 1 - tp_index[0]
                top = pl.multiple_of(place * width, 16)
            for i in range(per):
                left = (group * per + i) * nlen
                x_all[pl.ds(top, width), left : left + nlen] = x_ref[i]
        for i in range(cap):
            at = slice(i * nlen, (i + 1) * nlen)
            xt_all[at, :] = x_all[:, at].T
        project_keys(wk_first, k_even)
        project_values(wv_first, v_even)

    def work(k_now, v_now, k_later, v_later):
        score(k_now)
        project_keys(wk_next, k_later)
        soften()
        project_values(wv_next, v_later)
        blend(v_now)

    def finish(k_now, v_now):
        score(k_now)
        soften()
        blend(v_now)

    if steps > 1:
        pl.when((step < steps - 1) & (step % 2 == 0))(lambda: work(k_even, v_even, k_odd, v_odd))
    if steps > 2:
        pl.when((step < steps - 1) & (step % 2 == 1))(lambda: work(k_odd, v_odd, k_even, v_even))
    ends = (k_even, v_even) if steps % 2 == 1 else (k_odd, v_odd)
    pl.when(step == steps - 1)(lambda: finish(*ends))


def attend_part(first, scalars, groups, windows, weights, slots, held):
    blocks = [x for group in groups for x in group]
    pieces = len(groups[0])
    per, width, nlen = blocks[0].shape
    cap = per * len(groups)
    place = first // cap
    features = width * pieces
    columns = 2 * PAIR
    steps = windows.shape[-1] // columns

    in_specs = [pl.BlockSpec(x.shape, lambda t, *_: (0, 0, 0)) for x in blocks]
    operands = list(blocks)
    in_specs += [pl.BlockSpec((windows.shape[0], SPAN, columns), lambda t, *_: (0, 0, t))]
    operands += [windows]
    key_weight, value_weight = weights
    in_specs += [
        pl.BlockSpec((columns, features), lambda t, *_: (0, 0)),
        pl.BlockSpec((columns, features), lambda t, *_: (jnp.minimum(t + 1, steps - 1), 0)),
        pl.BlockSpec((features, columns), lambda t, *_: (0, 0)),
        pl.BlockSpec((features, columns), lambda t, *_: (0, jnp.minimum(t + 1, steps - 1))),
    ]
    operands += [key_weight] * 2 + [value_weight] * 2
    aliases = {}
    if held is not None:
        in_specs += [pl.BlockSpec(memory_space=pl.ANY)] * 2
        aliases = {2 + len(operands): 0, 3 + len(operands): 1}
        operands += list(held)
    keys = pltpu.VMEM((columns, cap * nlen), jnp.bfloat16)
    values = pltpu.VMEM((cap * nlen, columns), jnp.bfloat16)

    def body(*refs):
        attend_kernel(first, cap, pieces, len(groups), steps, *refs)

    return pl.pallas_call(
        body,
        grid_spec=pltpu.PrefetchScalarGridSpec(
            num_scalar_prefetch=2,
            grid=(steps,),
            in_specs=in_specs,
            out_specs=[
                pl.BlockSpec((cap, SPAN, columns), lambda t, *_: (place, 0, t)),
                pl.BlockSpec((cap, SPAN, LANES), lambda t, *_: (place, 0, 0)),
            ],
            scratch_shapes=[
                pltpu.VMEM((features, cap * nlen), jnp.bfloat16),
                pltpu.VMEM((cap * nlen, features), jnp.bfloat16),
                pltpu.VMEM((2 * cap, 2 * SPAN, nlen), jnp.float32),
                pltpu.VMEM((2 * cap, 2 * SPAN, nlen), jnp.bfloat16),
                keys, values, keys, values,
            ],
        ),
        out_shape=[
            jax.ShapeDtypeStruct((slots,) + windows.shape[1:], jnp.bfloat16),
            jax.ShapeDtypeStruct((slots, SPAN, LANES), jnp.float32),
        ],
        input_output_aliases=aliases,
        compiler_params=pltpu.CompilerParams(vmem_limit_bytes=VMEM_LIMIT),
        cost_estimate=HEAVY,
        name="attend_part",
    )(*scalars, *operands)


def spread_matrix(columns):
    per = LANES // 8
    row = lax.broadcasted_iota(jnp.int32, (4 * per, columns), 0)
    head = lax.broadcasted_iota(jnp.int32, (4 * per, columns), 1) // HDIM
    own = 2 * (row % per) + (row // per) % 2
    return jnp.where(head == own, 1.0, 0.0).astype(jnp.bfloat16)


def first_shares(l0, l1):
    largest = jnp.maximum(l0, l1)
    e0, e1 = jnp.exp(l0 - largest), jnp.exp(l1 - largest)
    share = e0 / (e0 + e1)
    high = share.astype(jnp.bfloat16).astype(jnp.float32)
    low = pltpu.roll(share - high, LANES // 4, 1)
    lanes = lax.broadcasted_iota(jnp.int32, share.shape, 1)
    return jnp.where(lanes < LANES // 4, high, low).astype(jnp.bfloat16)[:, : LANES // 2]


def mixed(p0, p1, shares, spread, cols):
    share = jnp.dot(shares, spread[:, cols], preferred_element_type=jnp.float32)
    return p0[0, :, cols].astype(jnp.float32) * share + p1[0, :, cols].astype(jnp.float32) * (
        1.0 - share
    )


def mix_last_kernel(places, p0, p1, l0, l1, out_ref, spread):
    spread[...] = spread_matrix(out_ref.shape[-1])
    shares = first_shares(l0[0], l1[0])
    for pair in range(out_ref.shape[-1] // PAIR):
        cols = slice(pair * PAIR, (pair + 1) * PAIR)
        out_ref[:, cols] = mixed(p0, p1, shares, spread, cols).astype(jnp.bfloat16)


def mix_kernel(places, *refs):
    ins, (out_ref, before, spread) = refs[:-3], refs[-3:]
    tile = 16
    late = lax.broadcasted_iota(jnp.int32, (tile, PAIR), 0) == tile - 1

    @pl.when(pl.program_id(0) == 0)
    def _():
        spread[...] = spread_matrix(out_ref.shape[-1])

    for n in range(len(ins) // 4):
        p0, p1, l0, l1 = ins[4 * n : 4 * n + 4]
        shares = first_shares(l0[0], l1[0])
        top = n * SPAN
        cut = top + SPAN - tile
        out_ref[top:cut, :] = before[: SPAN - tile, :]
        for pair in range(out_ref.shape[-1] // PAIR):
            cols = slice(pair * PAIR, (pair + 1) * PAIR)
            result = mixed(p0, p1, shares, spread, cols)
            out_ref[cut : cut + tile, cols] = jnp.where(
                late, result[SPAN - tile :], before[SPAN - tile :, cols].astype(jnp.float32)
            ).astype(jnp.bfloat16)
            before[:, cols] = result.astype(jnp.bfloat16)


def mix_specs(partials, log_totals, span_of):
    def place(j, shape):
        return pl.BlockSpec((1,) + shape, lambda k, places: (places[2 * span_of(k) + j], 0, 0))

    rows, stats = partials.shape[1:], log_totals.shape[1:]
    return [place(0, rows), place(1, rows), place(0, stats), place(1, stats)]


def mix_last(places, partials, log_totals, span_count):
    columns = partials.shape[-1]
    return pl.pallas_call(
        mix_last_kernel,
        grid_spec=pltpu.PrefetchScalarGridSpec(
            num_scalar_prefetch=1,
            grid=(1,),
            in_specs=mix_specs(partials, log_totals, lambda k: span_count - 1),
            out_specs=pl.BlockSpec((SPAN, columns), lambda k, places: (0, 0)),
            scratch_shapes=[pltpu.VMEM((LANES // 2, columns), jnp.bfloat16)],
        ),
        out_shape=jax.ShapeDtypeStruct((SPAN, columns), jnp.bfloat16),
        cost_estimate=LIGHT,
        name="mix_last",
    )(places, partials, partials, log_totals, log_totals)


def mix(places, partials, log_totals, span_count):
    columns = partials.shape[-1]
    per = 4
    in_specs = []
    for n in range(per):
        in_specs += mix_specs(partials, log_totals, lambda k, n=n: per * k + n)
    return pl.pallas_call(
        mix_kernel,
        grid_spec=pltpu.PrefetchScalarGridSpec(
            num_scalar_prefetch=1,
            grid=(span_count // per,),
            in_specs=in_specs,
            out_specs=pl.BlockSpec((per * SPAN, columns), lambda k, places: (k, 0)),
            scratch_shapes=[
                pltpu.VMEM((SPAN, columns), jnp.bfloat16),
                pltpu.VMEM((LANES // 2, columns), jnp.bfloat16),
            ],
        ),
        out_shape=jax.ShapeDtypeStruct((span_count * SPAN, columns), jnp.bfloat16),
        compiler_params=pltpu.CompilerParams(vmem_limit_bytes=VMEM_LIMIT),
        cost_estimate=LIGHT,
        name="mix",
    )(places, *([partials, partials, log_totals, log_totals] * per))


def head_kernel(carried, rows, out_ref):
    early = lax.broadcasted_iota(jnp.int32, out_ref.shape, 0) < SPAN - 1
    out_ref[...] = jnp.where(
        early, carried[...].astype(jnp.float32), rows[...].astype(jnp.float32)
    ).astype(jnp.bfloat16)


def with_head(carried, mixed_rows):
    spec = pl.BlockSpec((SPAN, mixed_rows.shape[-1]), lambda k: (0, 0))
    return pl.pallas_call(
        head_kernel,
        grid=(1,),
        in_specs=[spec, spec],
        out_specs=spec,
        out_shape=jax.ShapeDtypeStruct(mixed_rows.shape, mixed_rows.dtype),
        input_output_aliases={1: 0},
        cost_estimate=LIGHT,
        name="with_head",
    )(carried, mixed_rows)


def after(values, *others):
    return lax.optimization_barrier((values, others))[0]


def shards(queries, neighbours, key_weight, value_weight, neighbour_ids):
    span_count = neighbour_ids.shape[0]
    seq_count, tp_count = lax.axis_size("seq"), lax.axis_size("tp")
    block_count = neighbours.shape[0]
    wants = 2 * span_count
    ranks = (wants + seq_count - 1) // seq_count
    outer = seq_count // INNER
    slots = seq_count * ranks
    cap = INNER * ranks
    own_index = lax.axis_index("seq")
    tp_index = lax.axis_index("tp").astype(jnp.int32).reshape(1)

    def all_features(part):
        if tp_count == 2:
            return [part, swapped(part, "tp", 1)]
        return [lax.all_gather(part, "tp", axis=1, tiled=True)]

    def along(x, offset, senders):
        pairs = [(i, i ^ offset) for i in range(seq_count) if i // INNER in senders]
        return lax.ppermute(x, "seq", pairs)

    own_ids = neighbour_ids.reshape(wants)
    group_ids = jnp.stack([own_ids, swapped(own_ids, "seq", 2)])
    mate = swapped(neighbours, "seq", 1)
    incoming = passed_along(queries[:SPAN], "seq", -1)
    near = swapped(neighbours, "seq", INNER)
    across = along(neighbours, 3 * INNER, (1, 2)) if outer == 4 else near

    group_sources = group_ids // block_count
    group_ranks = slot_ranks(group_sources)
    sources = own_index ^ (INNER * jnp.arange(outer)[:, None] + jnp.arange(2))
    hit = (group_sources[None, :, None, None, :] == sources[:, None, :, None, None]) & (
        group_ranks[None, :, None, None, :] == jnp.arange(ranks)[None, None, None, :, None]
    )
    table = jnp.sum(
        jnp.where(hit, (group_ids % block_count)[None, :, None, None, :], 0), axis=-1
    )
    table = table.astype(jnp.int32).reshape(-1)

    own_sources = own_ids // block_count
    places = ((own_sources ^ own_index) * ranks + slot_ranks(own_sources)).astype(jnp.int32)
    order = jnp.arange(wants)
    spans = jnp.sum(
        jnp.where(places[None, :] == jnp.arange(slots)[:, None], order[None, :] // 2, 0), axis=1
    ).astype(jnp.int32)

    def pick(j, part, mate, *others):
        mine, outgoing = pick_blocks(j, ranks, after(table, *others), [part, mate])
        return all_features(mine), swapped(outgoing, "seq", 2)

    def attend(first, groups, held, *others):
        scalars = (tp_index, after(spans, *others))
        return attend_part(first, scalars, groups, windows, weights, slots, held)

    weights = (key_weight.T, value_weight)
    mine, got = pick(0, neighbours, mate, weights[0], incoming)
    near, across = after((near, across), mine[0])
    parts = [neighbours, near]
    if outer == 4:
        inside = (own_index // INNER == 1) | (own_index // INNER == 2)
        second = along(near, 3 * INNER, (1, 2))
        outward = along(across, INNER, (1, 2))

    def part_of(j, *others):
        if outer != 4:
            low = j & -j
            return swapped(after(parts[j ^ low], *others), "seq", INNER * low)
        if j == 2:
            return jnp.where(inside, *after((second, outward), *others))
        return jnp.where(inside, *after((across, third), *others))

    half = 2 * ranks
    groups = [[mine, all_features(got)]]
    mine, got = pick(1, near, swapped(near, "seq", 1), got)
    windows = span_windows(after(queries, mine[0]), incoming, span_count)
    held = attend(0, groups[0][:1], None, mine[0])
    groups.append([mine, all_features(after(got, held))])
    parts.append(part_of(2, held, *groups[0]))
    if outer == 4:
        third = along(second, INNER, (1, 2))
    mine, got = pick(2, parts[2], swapped(parts[2], "seq", 1))
    held = attend(half, groups[0][1:], held, mine[0])
    for j in range(3, outer):
        groups.append([mine, all_features(after(got, held))])
        parts.append(part_of(j, groups[j - 1][1][0], *groups[j - 2]))
        mine, got = pick(j, parts[j], swapped(parts[j], "seq", 1))
        held = attend((j - 2) * cap, groups[j - 2], held, mine[0])
    groups.append([mine, all_features(after(got, held))])
    held = attend((outer - 2) * cap, groups[outer - 2], held, groups[outer - 1][1][0])
    held = attend((outer - 1) * cap, groups[outer - 1], held)

    partials, log_totals = held
    last = mix_last(places, partials, log_totals, span_count)
    carried = passed_along(last, "seq", 1)
    rows = mix(places, partials, log_totals, span_count)
    return with_head(carried, rows)


def solution(mesh):
    in_specs = (P("seq", "tp"), P("seq", "tp", None), P(None, "tp"), P(None, "tp"), P("seq", None))
    out_specs = P("seq", "tp")
    return jax.shard_map(shards, mesh=mesh, in_specs=in_specs, out_specs=out_specs, check_vma=False)
```

```python
import jax
import jax.numpy as jnp
from jax import lax
from jax.experimental import pallas as pl
from jax.experimental.pallas import tpu as pltpu
from jax.sharding import PartitionSpec as P

HDIM = 128
SPAN = 64
PAIR = 2 * HDIM
INNER = 4
LANES = 128
VMEM_LIMIT = 56 * 1024 * 1024


LIGHT = pl.CostEstimate(flops=1000, bytes_accessed=1000, transcendentals=0)
HEAVY = pl.CostEstimate(flops=20 * 10**9, bytes_accessed=10**7, transcendentals=0)


def passed_along(x, axis, by):
    peers = lax.axis_size(axis)
    pairs = [(i, i + by) for i in range(peers) if 0 <= i + by < peers]
    return lax.ppermute(x, axis, pairs)


def swapped(x, axis, offset):
    peers = lax.axis_size(axis)
    return lax.ppermute(x, axis, [(i, i ^ offset) for i in range(peers)])


def slot_ranks(sources):
    positions = sources.shape[-1]
    alike = sources[..., :, None] == sources[..., None, :]
    earlier = jnp.arange(positions)[None, :] < jnp.arange(positions)[:, None]
    return jnp.sum(jnp.where(alike & earlier, 1, 0), axis=-1).astype(jnp.int32)


def windows_kernel(own_ref, next_ref, incoming_ref, out_ref):
    spans = out_ref.shape[0]
    last = pl.program_id(0) == pl.num_programs(0) - 1
    tile = 16
    cut = SPAN - tile
    late = lax.broadcasted_iota(jnp.int32, (tile, out_ref.shape[-1]), 0) == tile - 1
    for n in range(spans):
        if n + 1 < spans:
            later = own_ref[(n + 1) * SPAN : (n + 2) * SPAN, :]
        else:
            later = jnp.where(last, incoming_ref[...], next_ref[...])
        out_ref[n, :cut, :] = later[:cut]
        own = own_ref[n * SPAN + cut : (n + 1) * SPAN, :]
        out_ref[n, cut:, :] = jnp.where(
            late, own.astype(jnp.float32), later[cut:].astype(jnp.float32)
        ).astype(jnp.bfloat16)


def span_windows(queries, incoming, span_count):
    columns = queries.shape[-1]
    per = 4
    steps = span_count // per
    return pl.pallas_call(
        windows_kernel,
        grid=(steps,),
        in_specs=[
            pl.BlockSpec((per * SPAN, columns), lambda u: (u, 0)),
            pl.BlockSpec(
                (SPAN, columns), lambda u: (jnp.minimum(per * (u + 1), span_count - 1), 0)
            ),
            pl.BlockSpec((SPAN, columns), lambda u: (0, 0)),
        ],
        out_specs=pl.BlockSpec((per, SPAN, columns), lambda u: (u, 0, 0)),
        out_shape=jax.ShapeDtypeStruct((span_count, SPAN, columns), jnp.bfloat16),
        compiler_params=pltpu.CompilerParams(vmem_limit_bytes=VMEM_LIMIT),
        cost_estimate=LIGHT,
        name="windows",
    )(queries, queries, incoming)


def pick_kernel(part, ranks, table, *refs):
    sources, outs = refs[:2], refs[2:4]
    held, in_sems, out_sems = refs[-3:]
    fetches, stores = [], []
    for e in range(2):
        for a in range(2):
            for r in range(ranks):
                n = len(fetches)
                block = table[((part * 2 + e) * 2 + a) * ranks + r]
                fetches.append(
                    pltpu.make_async_copy(sources[a].at[block], held.at[n], in_sems.at[n])
                )
                stores.append(
                    pltpu.make_async_copy(held.at[n], outs[e].at[a * ranks + r], out_sems.at[n])
                )
    for fetch in fetches:
        fetch.start()
    for fetch, store in zip(fetches, stores):
        fetch.wait()
        store.start()
    for store in stores:
        store.wait()


def pick_blocks(part, ranks, table, sources):
    shape = sources[0].shape[1:]
    copies = 4 * ranks

    def body(*refs):
        pick_kernel(part, ranks, *refs)

    return pl.pallas_call(
        body,
        grid_spec=pltpu.PrefetchScalarGridSpec(
            num_scalar_prefetch=1,
            grid=(1,),
            in_specs=[pl.BlockSpec(memory_space=pltpu.HBM)] * 2,
            out_specs=[pl.BlockSpec(memory_space=pltpu.HBM)] * 2,
            scratch_shapes=[
                pltpu.VMEM((copies,) + shape, sources[0].dtype),
                pltpu.SemaphoreType.DMA((copies,)),
                pltpu.SemaphoreType.DMA((copies,)),
            ],
        ),
        out_shape=[jax.ShapeDtypeStruct((2 * ranks,) + shape, sources[0].dtype)] * 2,
        compiler_params=pltpu.CompilerParams(vmem_limit_bytes=VMEM_LIMIT),
        cost_estimate=LIGHT,
        name="pick_blocks",
    )(table, *sources)


def attend_kernel(first, cap, pieces, groups, steps, tp_index, spans, *refs):
    count = pieces * groups
    x_refs = refs[:count]
    q_ref, wk_first, wk_next, wv_first, wv_next = refs[count : count + 5]
    out_ref, lse_ref, x_all, xt_all, scores_ref, weights_ref, k_even, v_even, k_odd, v_odd = refs[-10:]
    nlen = scores_ref.shape[-1]
    pairs = scores_ref.shape[0] // cap
    step = pl.program_id(0)
    scale = HDIM ** (-0.5)
    lanes = lax.broadcasted_iota(jnp.int32, (SPAN, LANES), 1)

    def project_keys(w_ref, out):
        out[...] = jnp.dot(w_ref[...], x_all[...], preferred_element_type=jnp.float32).astype(
            jnp.bfloat16
        )

    def project_values(w_ref, out):
        out[...] = jnp.dot(xt_all[...], w_ref[...], preferred_element_type=jnp.float32).astype(
            jnp.bfloat16
        )

    def score(k_ref):
        none = jnp.zeros((SPAN, HDIM), jnp.bfloat16)
        for pair in range(pairs):
            for i in range(cap):
                q = q_ref[spans[first + i], :, pair * PAIR : (pair + 1) * PAIR]
                upper = jnp.concatenate([q[:, :HDIM], none], axis=1)
                lower = jnp.concatenate([none, q[:, HDIM:]], axis=1)
                scores_ref[pair * cap + i] = jnp.dot(
                    jnp.concatenate([upper, lower], axis=0),
                    k_ref[pair * PAIR : (pair + 1) * PAIR, i * nlen : (i + 1) * nlen],
                    preferred_element_type=jnp.float32,
                )

    def soften():
        for i in range(cap):
            held = lse_ref[i]
            for pair in range(pairs):
                scores = scores_ref[pair * cap + i]
                highest = jnp.max(scores, axis=1, keepdims=True)
                exponent = jnp.exp((scores - highest) * scale)
                totals = jnp.sum(exponent, axis=1, keepdims=True)
                weights_ref[pair * cap + i] = (exponent * (1.0 / totals)).astype(jnp.bfloat16)
                lse = highest * scale + jnp.log(totals)
                at = pairs * step + pair
                held = jnp.where(lanes == at, lse[:SPAN], held)
                held = jnp.where(lanes == LANES // 8 + at, lse[SPAN:], held)
            lse_ref[i] = held

    def blend(v_ref):
        for pair in range(pairs):
            cols = slice(pair * PAIR, (pair + 1) * PAIR)
            for i in range(cap):
                blended = jnp.dot(
                    weights_ref[pair * cap + i],
                    v_ref[i * nlen : (i + 1) * nlen, cols],
                    preferred_element_type=jnp.float32,
                )
                out_ref[i, :, cols] = jnp.concatenate(
                    [blended[:SPAN, :HDIM], blended[SPAN:, HDIM:]], axis=1
                ).astype(jnp.bfloat16)

    @pl.when(step == 0)
    def _():
        lse_ref[...] = jnp.zeros_like(lse_ref)
        per = cap // groups
        for n, x_ref in enumerate(x_refs):
            group, piece = n // pieces, n % pieces
            width = x_ref.shape[1]
            top = 0
            if pieces == 2:
                place = tp_index[0] if piece == 0 else 1 - tp_index[0]
                top = pl.multiple_of(place * width, 16)
            for i in range(per):
                left = (group * per + i) * nlen
                x_all[pl.ds(top, width), left : left + nlen] = x_ref[i]
        for i in range(cap):
            at = slice(i * nlen, (i + 1) * nlen)
            xt_all[at, :] = x_all[:, at].T
        project_keys(wk_first, k_even)
        project_values(wv_first, v_even)

    def work(k_now, v_now, k_later, v_later):
        score(k_now)
        project_keys(wk_next, k_later)
        soften()
        project_values(wv_next, v_later)
        blend(v_now)

    def finish(k_now, v_now):
        score(k_now)
        soften()
        blend(v_now)

    if steps > 1:
        pl.when((step < steps - 1) & (step % 2 == 0))(lambda: work(k_even, v_even, k_odd, v_odd))
    if steps > 2:
        pl.when((step < steps - 1) & (step % 2 == 1))(lambda: work(k_odd, v_odd, k_even, v_even))
    ends = (k_even, v_even) if steps % 2 == 1 else (k_odd, v_odd)
    pl.when(step == steps - 1)(lambda: finish(*ends))


def attend_part(first, scalars, groups, windows, weights, slots, held):
    blocks = [x for group in groups for x in group]
    pieces = len(groups[0])
    per, width, nlen = blocks[0].shape
    cap = per * len(groups)
    place = first // cap
    features = width * pieces
    columns = 2 * PAIR
    steps = windows.shape[-1] // columns

    in_specs = [pl.BlockSpec(x.shape, lambda t, *_: (0, 0, 0)) for x in blocks]
    operands = list(blocks)
    in_specs += [pl.BlockSpec((windows.shape[0], SPAN, columns), lambda t, *_: (0, 0, t))]
    operands += [windows]
    key_weight, value_weight = weights
    in_specs += [
        pl.BlockSpec((columns, features), lambda t, *_: (0, 0)),
        pl.BlockSpec((columns, features), lambda t, *_: (jnp.minimum(t + 1, steps - 1), 0)),
        pl.BlockSpec((features, columns), lambda t, *_: (0, 0)),
        pl.BlockSpec((features, columns), lambda t, *_: (0, jnp.minimum(t + 1, steps - 1))),
    ]
    operands += [key_weight] * 2 + [value_weight] * 2
    aliases = {}
    if held is not None:
        in_specs += [pl.BlockSpec(memory_space=pl.ANY)] * 2
        aliases = {2 + len(operands): 0, 3 + len(operands): 1}
        operands += list(held)
    keys = pltpu.VMEM((columns, cap * nlen), jnp.bfloat16)
    values = pltpu.VMEM((cap * nlen, columns), jnp.bfloat16)

    def body(*refs):
        attend_kernel(first, cap, pieces, len(groups), steps, *refs)

    return pl.pallas_call(
        body,
        grid_spec=pltpu.PrefetchScalarGridSpec(
            num_scalar_prefetch=2,
            grid=(steps,),
            in_specs=in_specs,
            out_specs=[
                pl.BlockSpec((cap, SPAN, columns), lambda t, *_: (place, 0, t)),
                pl.BlockSpec((cap, SPAN, LANES), lambda t, *_: (place, 0, 0)),
            ],
            scratch_shapes=[
                pltpu.VMEM((features, cap * nlen), jnp.bfloat16),
                pltpu.VMEM((cap * nlen, features), jnp.bfloat16),
                pltpu.VMEM((2 * cap, 2 * SPAN, nlen), jnp.float32),
                pltpu.VMEM((2 * cap, 2 * SPAN, nlen), jnp.bfloat16),
                keys, values, keys, values,
            ],
        ),
        out_shape=[
            jax.ShapeDtypeStruct((slots,) + windows.shape[1:], jnp.bfloat16),
            jax.ShapeDtypeStruct((slots, SPAN, LANES), jnp.float32),
        ],
        input_output_aliases=aliases,
        compiler_params=pltpu.CompilerParams(vmem_limit_bytes=VMEM_LIMIT),
        cost_estimate=HEAVY,
        name="attend_part",
    )(*scalars, *operands)


def spread_matrix(columns):
    per = LANES // 8
    row = lax.broadcasted_iota(jnp.int32, (4 * per, columns), 0)
    head = lax.broadcasted_iota(jnp.int32, (4 * per, columns), 1) // HDIM
    own = 2 * (row % per) + (row // per) % 2
    return jnp.where(head == own, 1.0, 0.0).astype(jnp.bfloat16)


def first_shares(l0, l1):
    largest = jnp.maximum(l0, l1)
    e0, e1 = jnp.exp(l0 - largest), jnp.exp(l1 - largest)
    share = e0 / (e0 + e1)
    high = share.astype(jnp.bfloat16).astype(jnp.float32)
    low = pltpu.roll(share - high, LANES // 4, 1)
    lanes = lax.broadcasted_iota(jnp.int32, share.shape, 1)
    return jnp.where(lanes < LANES // 4, high, low).astype(jnp.bfloat16)[:, : LANES // 2]


def mixed(p0, p1, shares, spread, cols):
    share = jnp.dot(shares, spread[:, cols], preferred_element_type=jnp.float32)
    return p0[0, :, cols].astype(jnp.float32) * share + p1[0, :, cols].astype(jnp.float32) * (
        1.0 - share
    )


def mix_last_kernel(places, p0, p1, l0, l1, out_ref, spread):
    spread[...] = spread_matrix(out_ref.shape[-1])
    shares = first_shares(l0[0], l1[0])
    for pair in range(out_ref.shape[-1] // PAIR):
        cols = slice(pair * PAIR, (pair + 1) * PAIR)
        out_ref[:, cols] = mixed(p0, p1, shares, spread, cols).astype(jnp.bfloat16)


def mix_kernel(places, *refs):
    ins, (out_ref, before, spread) = refs[:-3], refs[-3:]
    tile = 16
    late = lax.broadcasted_iota(jnp.int32, (tile, PAIR), 0) == tile - 1

    @pl.when(pl.program_id(0) == 0)
    def _():
        spread[...] = spread_matrix(out_ref.shape[-1])

    for n in range(len(ins) // 4):
        p0, p1, l0, l1 = ins[4 * n : 4 * n + 4]
        shares = first_shares(l0[0], l1[0])
        top = n * SPAN
        cut = top + SPAN - tile
        out_ref[top:cut, :] = before[: SPAN - tile, :]
        for pair in range(out_ref.shape[-1] // PAIR):
            cols = slice(pair * PAIR, (pair + 1) * PAIR)
            result = mixed(p0, p1, shares, spread, cols)
            out_ref[cut : cut + tile, cols] = jnp.where(
                late, result[SPAN - tile :], before[SPAN - tile :, cols].astype(jnp.float32)
            ).astype(jnp.bfloat16)
            before[:, cols] = result.astype(jnp.bfloat16)


def mix_specs(partials, log_totals, span_of):
    def place(j, shape):
        return pl.BlockSpec((1,) + shape, lambda k, places: (places[2 * span_of(k) + j], 0, 0))

    rows, stats = partials.shape[1:], log_totals.shape[1:]
    return [place(0, rows), place(1, rows), place(0, stats), place(1, stats)]


def mix_last(places, partials, log_totals, span_count):
    columns = partials.shape[-1]
    return pl.pallas_call(
        mix_last_kernel,
        grid_spec=pltpu.PrefetchScalarGridSpec(
            num_scalar_prefetch=1,
            grid=(1,),
            in_specs=mix_specs(partials, log_totals, lambda k: span_count - 1),
            out_specs=pl.BlockSpec((SPAN, columns), lambda k, places: (0, 0)),
            scratch_shapes=[pltpu.VMEM((LANES // 2, columns), jnp.bfloat16)],
        ),
        out_shape=jax.ShapeDtypeStruct((SPAN, columns), jnp.bfloat16),
        cost_estimate=LIGHT,
        name="mix_last",
    )(places, partials, partials, log_totals, log_totals)


def mix(places, partials, log_totals, span_count):
    columns = partials.shape[-1]
    per = 4
    in_specs = []
    for n in range(per):
        in_specs += mix_specs(partials, log_totals, lambda k, n=n: per * k + n)
    return pl.pallas_call(
        mix_kernel,
        grid_spec=pltpu.PrefetchScalarGridSpec(
            num_scalar_prefetch=1,
            grid=(span_count // per,),
            in_specs=in_specs,
            out_specs=pl.BlockSpec((per * SPAN, columns), lambda k, places: (k, 0)),
            scratch_shapes=[
                pltpu.VMEM((SPAN, columns), jnp.bfloat16),
                pltpu.VMEM((LANES // 2, columns), jnp.bfloat16),
            ],
        ),
        out_shape=jax.ShapeDtypeStruct((span_count * SPAN, columns), jnp.bfloat16),
        compiler_params=pltpu.CompilerParams(vmem_limit_bytes=VMEM_LIMIT),
        cost_estimate=LIGHT,
        name="mix",
    )(places, *([partials, partials, log_totals, log_totals] * per))


def head_kernel(carried, rows, out_ref):
    early = lax.broadcasted_iota(jnp.int32, out_ref.shape, 0) < SPAN - 1
    out_ref[...] = jnp.where(
        early, carried[...].astype(jnp.float32), rows[...].astype(jnp.float32)
    ).astype(jnp.bfloat16)


def with_head(carried, mixed_rows):
    spec = pl.BlockSpec((SPAN, mixed_rows.shape[-1]), lambda k: (0, 0))
    return pl.pallas_call(
        head_kernel,
        grid=(1,),
        in_specs=[spec, spec],
        out_specs=spec,
        out_shape=jax.ShapeDtypeStruct(mixed_rows.shape, mixed_rows.dtype),
        input_output_aliases={1: 0},
        cost_estimate=LIGHT,
        name="with_head",
    )(carried, mixed_rows)


def after(values, *others):
    return lax.optimization_barrier((values, others))[0]


def shards(queries, neighbours, key_weight, value_weight, neighbour_ids):
    span_count = neighbour_ids.shape[0]
    seq_count, tp_count = lax.axis_size("seq"), lax.axis_size("tp")
    block_count = neighbours.shape[0]
    wants = 2 * span_count
    ranks = (wants + seq_count - 1) // seq_count
    outer = seq_count // INNER
    slots = seq_count * ranks
    cap = INNER * ranks
    own_index = lax.axis_index("seq")
    tp_index = lax.axis_index("tp").astype(jnp.int32).reshape(1)

    def all_features(part):
        if tp_count == 2:
            return [part, swapped(part, "tp", 1)]
        return [lax.all_gather(part, "tp", axis=1, tiled=True)]

    def along(x, offset, senders):
        pairs = [(i, i ^ offset) for i in range(seq_count) if i // INNER in senders]
        return lax.ppermute(x, "seq", pairs)

    own_ids = neighbour_ids.reshape(wants)
    group_ids = jnp.stack([own_ids, swapped(own_ids, "seq", 2)])
    mate = swapped(neighbours, "seq", 1)
    incoming = passed_along(queries[:SPAN], "seq", -1)
    own_blocks = after(neighbours, incoming)
    near = swapped(own_blocks, "seq", INNER)
    across = along(own_blocks, 3 * INNER, (1, 2)) if outer == 4 else near

    group_sources = group_ids // block_count
    group_ranks = slot_ranks(group_sources)
    sources = own_index ^ (INNER * jnp.arange(outer)[:, None] + jnp.arange(2))
    hit = (group_sources[None, :, None, None, :] == sources[:, None, :, None, None]) & (
        group_ranks[None, :, None, None, :] == jnp.arange(ranks)[None, None, None, :, None]
    )
    table = jnp.sum(
        jnp.where(hit, (group_ids % block_count)[None, :, None, None, :], 0), axis=-1
    )
    table = table.astype(jnp.int32).reshape(-1)

    own_sources = own_ids // block_count
    places = ((own_sources ^ own_index) * ranks + slot_ranks(own_sources)).astype(jnp.int32)
    order = jnp.arange(wants)
    spans = jnp.sum(
        jnp.where(places[None, :] == jnp.arange(slots)[:, None], order[None, :] // 2, 0), axis=1
    ).astype(jnp.int32)

    def pick(j, part, mate, *others):
        mine, outgoing = pick_blocks(j, ranks, after(table, *others), [part, mate])
        return all_features(mine), swapped(outgoing, "seq", 2)

    def attend(first, groups, held, *others):
        scalars = (tp_index, after(spans, *others))
        return attend_part(first, scalars, groups, windows, weights, slots, held)

    weights = (key_weight.T, value_weight)
    mine, got = pick(0, neighbours, mate, weights[0], incoming)
    near, across = after((near, across), mine[0])
    parts = [neighbours, near]
    if outer == 4:
        inside = (own_index // INNER == 1) | (own_index // INNER == 2)
        second = along(near, 3 * INNER, (1, 2))
        outward = along(across, INNER, (1, 2))

    def part_of(j, *others):
        if outer != 4:
            low = j & -j
            return swapped(after(parts[j ^ low], *others), "seq", INNER * low)
        if j == 2:
            return jnp.where(inside, *after((second, outward), *others))
        return jnp.where(inside, *after((across, third), *others))

    groups = [[mine, all_features(got)]]
    mine, got = pick(1, near, swapped(near, "seq", 1), got, *mine)
    windows = span_windows(after(queries, mine[0]), incoming, span_count)
    groups.append([mine, all_features(after(got, windows))])
    parts.append(part_of(2, groups[1][1][0], *groups[0]))
    if outer == 4:
        third = along(second, INNER, (1, 2))
    mine, got = pick(2, parts[2], swapped(parts[2], "seq", 1))
    held = attend(0, groups[0], None, mine[0])
    for j in range(3, outer):
        groups.append([mine, all_features(after(got, held))])
        parts.append(part_of(j, groups[j - 1][1][0], *groups[j - 2]))
        mine, got = pick(j, parts[j], swapped(parts[j], "seq", 1))
        held = attend((j - 2) * cap, groups[j - 2], held, mine[0])
    groups.append([mine, all_features(after(got, held))])
    held = attend((outer - 2) * cap, groups[outer - 2], held, groups[outer - 1][1][0])
    held = attend((outer - 1) * cap, groups[outer - 1], held)

    partials, log_totals = held
    last = mix_last(places, partials, log_totals, span_count)
    carried = passed_along(last, "seq", 1)
    rows = mix(places, partials, log_totals, span_count)
    return with_head(carried, rows)


def solution(mesh):
    in_specs = (P("seq", "tp"), P("seq", "tp", None), P(None, "tp"), P(None, "tp"), P("seq", None))
    out_specs = P("seq", "tp")
    return jax.shard_map(shards, mesh=mesh, in_specs=in_specs, out_specs=out_specs, check_vma=False)
```

```python
import jax
import jax.numpy as jnp
from jax import lax
from jax.experimental import pallas as pl
from jax.experimental.pallas import tpu as pltpu
from jax.sharding import PartitionSpec as P

HDIM = 128
SPAN = 64
PAIR = 2 * HDIM
INNER = 4
LANES = 128
VMEM_LIMIT = 56 * 1024 * 1024


LIGHT = pl.CostEstimate(flops=1000, bytes_accessed=1000, transcendentals=0)
HEAVY = pl.CostEstimate(flops=20 * 10**9, bytes_accessed=10**7, transcendentals=0)


def passed_along(x, axis, by):
    peers = lax.axis_size(axis)
    pairs = [(i, i + by) for i in range(peers) if 0 <= i + by < peers]
    return lax.ppermute(x, axis, pairs)


def swapped(x, axis, offset):
    peers = lax.axis_size(axis)
    return lax.ppermute(x, axis, [(i, i ^ offset) for i in range(peers)])


def slot_ranks(sources):
    positions = sources.shape[-1]
    alike = sources[..., :, None] == sources[..., None, :]
    earlier = jnp.arange(positions)[None, :] < jnp.arange(positions)[:, None]
    return jnp.sum(jnp.where(alike & earlier, 1, 0), axis=-1).astype(jnp.int32)


def windows_kernel(own_ref, next_ref, incoming_ref, out_ref):
    spans = out_ref.shape[0]
    last = pl.program_id(0) == pl.num_programs(0) - 1
    tile = 16
    cut = SPAN - tile
    late = lax.broadcasted_iota(jnp.int32, (tile, out_ref.shape[-1]), 0) == tile - 1
    for n in range(spans):
        if n + 1 < spans:
            later = own_ref[(n + 1) * SPAN : (n + 2) * SPAN, :]
        else:
            later = jnp.where(last, incoming_ref[...], next_ref[...])
        out_ref[n, :cut, :] = later[:cut]
        own = own_ref[n * SPAN + cut : (n + 1) * SPAN, :]
        out_ref[n, cut:, :] = jnp.where(
            late, own.astype(jnp.float32), later[cut:].astype(jnp.float32)
        ).astype(jnp.bfloat16)


def span_windows(queries, incoming, span_count):
    columns = queries.shape[-1]
    per = 4
    steps = span_count // per
    return pl.pallas_call(
        windows_kernel,
        grid=(steps,),
        in_specs=[
            pl.BlockSpec((per * SPAN, columns), lambda u: (u, 0)),
            pl.BlockSpec(
                (SPAN, columns), lambda u: (jnp.minimum(per * (u + 1), span_count - 1), 0)
            ),
            pl.BlockSpec((SPAN, columns), lambda u: (0, 0)),
        ],
        out_specs=pl.BlockSpec((per, SPAN, columns), lambda u: (u, 0, 0)),
        out_shape=jax.ShapeDtypeStruct((span_count, SPAN, columns), jnp.bfloat16),
        compiler_params=pltpu.CompilerParams(vmem_limit_bytes=VMEM_LIMIT),
        cost_estimate=LIGHT,
        name="windows",
    )(queries, queries, incoming)


def pick_kernel(part, ranks, table, *refs):
    sources, outs = refs[:2], refs[2:4]
    held, in_sems, out_sems = refs[-3:]
    fetches, stores = [], []
    for e in range(2):
        for a in range(2):
            for r in range(ranks):
                n = len(fetches)
                block = table[((part * 2 + e) * 2 + a) * ranks + r]
                fetches.append(
                    pltpu.make_async_copy(sources[a].at[block], held.at[n], in_sems.at[n])
                )
                stores.append(
                    pltpu.make_async_copy(held.at[n], outs[e].at[a * ranks + r], out_sems.at[n])
                )
    for fetch in fetches:
        fetch.start()
    for fetch, store in zip(fetches, stores):
        fetch.wait()
        store.start()
    for store in stores:
        store.wait()


def pick_blocks(part, ranks, table, sources):
    shape = sources[0].shape[1:]
    copies = 4 * ranks

    def body(*refs):
        pick_kernel(part, ranks, *refs)

    return pl.pallas_call(
        body,
        grid_spec=pltpu.PrefetchScalarGridSpec(
            num_scalar_prefetch=1,
            grid=(1,),
            in_specs=[pl.BlockSpec(memory_space=pltpu.HBM)] * 2,
            out_specs=[pl.BlockSpec(memory_space=pltpu.HBM)] * 2,
            scratch_shapes=[
                pltpu.VMEM((copies,) + shape, sources[0].dtype),
                pltpu.SemaphoreType.DMA((copies,)),
                pltpu.SemaphoreType.DMA((copies,)),
            ],
        ),
        out_shape=[jax.ShapeDtypeStruct((2 * ranks,) + shape, sources[0].dtype)] * 2,
        compiler_params=pltpu.CompilerParams(vmem_limit_bytes=VMEM_LIMIT),
        cost_estimate=LIGHT,
        name="pick_blocks",
    )(table, *sources)


def attend_kernel(first, cap, pieces, groups, steps, tp_index, spans, *refs):
    count = pieces * groups
    x_refs = refs[:count]
    q_ref, wk_first, wk_next, wv_first, wv_next = refs[count : count + 5]
    out_ref, lse_ref, x_all, xt_all, scores_ref, weights_ref, k_even, v_even, k_odd, v_odd = refs[-10:]
    nlen = scores_ref.shape[-1]
    pairs = scores_ref.shape[0] // cap
    step = pl.program_id(0)
    scale = HDIM ** (-0.5)
    lanes = lax.broadcasted_iota(jnp.int32, (SPAN, LANES), 1)

    def project_keys(w_ref, out):
        out[...] = jnp.dot(w_ref[...], x_all[...], preferred_element_type=jnp.float32).astype(
            jnp.bfloat16
        )

    def project_values(w_ref, out):
        out[...] = jnp.dot(xt_all[...], w_ref[...], preferred_element_type=jnp.float32).astype(
            jnp.bfloat16
        )

    def score(k_ref):
        none = jnp.zeros((SPAN, HDIM), jnp.bfloat16)
        for pair in range(pairs):
            for i in range(cap):
                q = q_ref[spans[first + i], :, pair * PAIR : (pair + 1) * PAIR]
                upper = jnp.concatenate([q[:, :HDIM], none], axis=1)
                lower = jnp.concatenate([none, q[:, HDIM:]], axis=1)
                scores_ref[pair * cap + i] = jnp.dot(
                    jnp.concatenate([upper, lower], axis=0),
                    k_ref[pair * PAIR : (pair + 1) * PAIR, i * nlen : (i + 1) * nlen],
                    preferred_element_type=jnp.float32,
                )

    def soften():
        for i in range(cap):
            held = lse_ref[i]
            for pair in range(pairs):
                scores = scores_ref[pair * cap + i]
                highest = jnp.max(scores, axis=1, keepdims=True)
                exponent = jnp.exp((scores - highest) * scale)
                totals = jnp.sum(exponent, axis=1, keepdims=True)
                weights_ref[pair * cap + i] = (exponent * (1.0 / totals)).astype(jnp.bfloat16)
                lse = highest * scale + jnp.log(totals)
                at = pairs * step + pair
                held = jnp.where(lanes == at, lse[:SPAN], held)
                held = jnp.where(lanes == LANES // 8 + at, lse[SPAN:], held)
            lse_ref[i] = held

    def blend(v_ref):
        for pair in range(pairs):
            cols = slice(pair * PAIR, (pair + 1) * PAIR)
            for i in range(cap):
                blended = jnp.dot(
                    weights_ref[pair * cap + i],
                    v_ref[i * nlen : (i + 1) * nlen, cols],
                    preferred_element_type=jnp.float32,
                )
                out_ref[i, :, cols] = jnp.concatenate(
                    [blended[:SPAN, :HDIM], blended[SPAN:, HDIM:]], axis=1
                ).astype(jnp.bfloat16)

    @pl.when(step == 0)
    def _():
        lse_ref[...] = jnp.zeros_like(lse_ref)
        per = cap // groups
        for n, x_ref in enumerate(x_refs):
            group, piece = n // pieces, n % pieces
            width = x_ref.shape[1]
            top = 0
            if pieces == 2:
                place = tp_index[0] if piece == 0 else 1 - tp_index[0]
                top = pl.multiple_of(place * width, 16)
            for i in range(per):
                left = (group * per + i) * nlen
                x_all[pl.ds(top, width), left : left + nlen] = x_ref[i]
        for i in range(cap):
            at = slice(i * nlen, (i + 1) * nlen)
            xt_all[at, :] = x_all[:, at].T
        project_keys(wk_first, k_even)
        project_values(wv_first, v_even)

    def work(k_now, v_now, k_later, v_later):
        score(k_now)
        project_keys(wk_next, k_later)
        soften()
        project_values(wv_next, v_later)
        blend(v_now)

    def finish(k_now, v_now):
        score(k_now)
        soften()
        blend(v_now)

    if steps > 1:
        pl.when((step < steps - 1) & (step % 2 == 0))(lambda: work(k_even, v_even, k_odd, v_odd))
    if steps > 2:
        pl.when((step < steps - 1) & (step % 2 == 1))(lambda: work(k_odd, v_odd, k_even, v_even))
    ends = (k_even, v_even) if steps % 2 == 1 else (k_odd, v_odd)
    pl.when(step == steps - 1)(lambda: finish(*ends))


def attend_part(first, scalars, groups, windows, weights, slots, held):
    blocks = [x for group in groups for x in group]
    pieces = len(groups[0])
    per, width, nlen = blocks[0].shape
    cap = per * len(groups)
    place = first // cap
    features = width * pieces
    columns = 2 * PAIR
    steps = windows.shape[-1] // columns

    in_specs = [pl.BlockSpec(x.shape, lambda t, *_: (0, 0, 0)) for x in blocks]
    operands = list(blocks)
    in_specs += [pl.BlockSpec((windows.shape[0], SPAN, columns), lambda t, *_: (0, 0, t))]
    operands += [windows]
    key_weight, value_weight = weights
    in_specs += [
        pl.BlockSpec((columns, features), lambda t, *_: (0, 0)),
        pl.BlockSpec((columns, features), lambda t, *_: (jnp.minimum(t + 1, steps - 1), 0)),
        pl.BlockSpec((features, columns), lambda t, *_: (0, 0)),
        pl.BlockSpec((features, columns), lambda t, *_: (0, jnp.minimum(t + 1, steps - 1))),
    ]
    operands += [key_weight] * 2 + [value_weight] * 2
    aliases = {}
    if held is not None:
        in_specs += [pl.BlockSpec(memory_space=pl.ANY)] * 2
        aliases = {2 + len(operands): 0, 3 + len(operands): 1}
        operands += list(held)
    keys = pltpu.VMEM((columns, cap * nlen), jnp.bfloat16)
    values = pltpu.VMEM((cap * nlen, columns), jnp.bfloat16)

    def body(*refs):
        attend_kernel(first, cap, pieces, len(groups), steps, *refs)

    return pl.pallas_call(
        body,
        grid_spec=pltpu.PrefetchScalarGridSpec(
            num_scalar_prefetch=2,
            grid=(steps,),
            in_specs=in_specs,
            out_specs=[
                pl.BlockSpec((cap, SPAN, columns), lambda t, *_: (place, 0, t)),
                pl.BlockSpec((cap, SPAN, LANES), lambda t, *_: (place, 0, 0)),
            ],
            scratch_shapes=[
                pltpu.VMEM((features, cap * nlen), jnp.bfloat16),
                pltpu.VMEM((cap * nlen, features), jnp.bfloat16),
                pltpu.VMEM((2 * cap, 2 * SPAN, nlen), jnp.float32),
                pltpu.VMEM((2 * cap, 2 * SPAN, nlen), jnp.bfloat16),
                keys, values, keys, values,
            ],
        ),
        out_shape=[
            jax.ShapeDtypeStruct((slots,) + windows.shape[1:], jnp.bfloat16),
            jax.ShapeDtypeStruct((slots, SPAN, LANES), jnp.float32),
        ],
        input_output_aliases=aliases,
        compiler_params=pltpu.CompilerParams(vmem_limit_bytes=VMEM_LIMIT),
        cost_estimate=HEAVY,
        name="attend_part",
    )(*scalars, *operands)


def spread_matrix(columns):
    per = LANES // 8
    row = lax.broadcasted_iota(jnp.int32, (4 * per, columns), 0)
    head = lax.broadcasted_iota(jnp.int32, (4 * per, columns), 1) // HDIM
    own = 2 * (row % per) + (row // per) % 2
    return jnp.where(head == own, 1.0, 0.0).astype(jnp.bfloat16)


def first_shares(l0, l1):
    largest = jnp.maximum(l0, l1)
    e0, e1 = jnp.exp(l0 - largest), jnp.exp(l1 - largest)
    share = e0 / (e0 + e1)
    high = share.astype(jnp.bfloat16).astype(jnp.float32)
    low = pltpu.roll(share - high, LANES // 4, 1)
    lanes = lax.broadcasted_iota(jnp.int32, share.shape, 1)
    return jnp.where(lanes < LANES // 4, high, low).astype(jnp.bfloat16)[:, : LANES // 2]


def mixed(p0, p1, shares, spread, cols):
    share = jnp.dot(shares, spread[:, cols], preferred_element_type=jnp.float32)
    return p0[0, :, cols].astype(jnp.float32) * share + p1[0, :, cols].astype(jnp.float32) * (
        1.0 - share
    )


def mix_last_kernel(places, p0, p1, l0, l1, out_ref, spread):
    spread[...] = spread_matrix(out_ref.shape[-1])
    shares = first_shares(l0[0], l1[0])
    for pair in range(out_ref.shape[-1] // PAIR):
        cols = slice(pair * PAIR, (pair + 1) * PAIR)
        out_ref[:, cols] = mixed(p0, p1, shares, spread, cols).astype(jnp.bfloat16)


def mix_kernel(places, *refs):
    ins, (out_ref, before, spread) = refs[:-3], refs[-3:]
    tile = 16
    late = lax.broadcasted_iota(jnp.int32, (tile, PAIR), 0) == tile - 1

    @pl.when(pl.program_id(0) == 0)
    def _():
        spread[...] = spread_matrix(out_ref.shape[-1])

    for n in range(len(ins) // 4):
        p0, p1, l0, l1 = ins[4 * n : 4 * n + 4]
        shares = first_shares(l0[0], l1[0])
        top = n * SPAN
        cut = top + SPAN - tile
        out_ref[top:cut, :] = before[: SPAN - tile, :]
        for pair in range(out_ref.shape[-1] // PAIR):
            cols = slice(pair * PAIR, (pair + 1) * PAIR)
            result = mixed(p0, p1, shares, spread, cols)
            out_ref[cut : cut + tile, cols] = jnp.where(
                late, result[SPAN - tile :], before[SPAN - tile :, cols].astype(jnp.float32)
            ).astype(jnp.bfloat16)
            before[:, cols] = result.astype(jnp.bfloat16)


def mix_specs(partials, log_totals, span_of):
    def place(j, shape):
        return pl.BlockSpec((1,) + shape, lambda k, places: (places[2 * span_of(k) + j], 0, 0))

    rows, stats = partials.shape[1:], log_totals.shape[1:]
    return [place(0, rows), place(1, rows), place(0, stats), place(1, stats)]


def mix_last(places, partials, log_totals, span_count):
    columns = partials.shape[-1]
    return pl.pallas_call(
        mix_last_kernel,
        grid_spec=pltpu.PrefetchScalarGridSpec(
            num_scalar_prefetch=1,
            grid=(1,),
            in_specs=mix_specs(partials, log_totals, lambda k: span_count - 1),
            out_specs=pl.BlockSpec((SPAN, columns), lambda k, places: (0, 0)),
            scratch_shapes=[pltpu.VMEM((LANES // 2, columns), jnp.bfloat16)],
        ),
        out_shape=jax.ShapeDtypeStruct((SPAN, columns), jnp.bfloat16),
        cost_estimate=LIGHT,
        name="mix_last",
    )(places, partials, partials, log_totals, log_totals)


def mix(places, partials, log_totals, span_count):
    columns = partials.shape[-1]
    per = 4
    in_specs = []
    for n in range(per):
        in_specs += mix_specs(partials, log_totals, lambda k, n=n: per * k + n)
    return pl.pallas_call(
        mix_kernel,
        grid_spec=pltpu.PrefetchScalarGridSpec(
            num_scalar_prefetch=1,
            grid=(span_count // per,),
            in_specs=in_specs,
            out_specs=pl.BlockSpec((per * SPAN, columns), lambda k, places: (k, 0)),
            scratch_shapes=[
                pltpu.VMEM((SPAN, columns), jnp.bfloat16),
                pltpu.VMEM((LANES // 2, columns), jnp.bfloat16),
            ],
        ),
        out_shape=jax.ShapeDtypeStruct((span_count * SPAN, columns), jnp.bfloat16),
        compiler_params=pltpu.CompilerParams(vmem_limit_bytes=VMEM_LIMIT),
        cost_estimate=LIGHT,
        name="mix",
    )(places, *([partials, partials, log_totals, log_totals] * per))


def head_kernel(carried, rows, out_ref):
    early = lax.broadcasted_iota(jnp.int32, out_ref.shape, 0) < SPAN - 1
    out_ref[...] = jnp.where(
        early, carried[...].astype(jnp.float32), rows[...].astype(jnp.float32)
    ).astype(jnp.bfloat16)


def with_head(carried, mixed_rows):
    spec = pl.BlockSpec((SPAN, mixed_rows.shape[-1]), lambda k: (0, 0))
    return pl.pallas_call(
        head_kernel,
        grid=(1,),
        in_specs=[spec, spec],
        out_specs=spec,
        out_shape=jax.ShapeDtypeStruct(mixed_rows.shape, mixed_rows.dtype),
        input_output_aliases={1: 0},
        cost_estimate=LIGHT,
        name="with_head",
    )(carried, mixed_rows)


def after(values, *others):
    return lax.optimization_barrier((values, others))[0]


def shards(queries, neighbours, key_weight, value_weight, neighbour_ids):
    span_count = neighbour_ids.shape[0]
    seq_count, tp_count = lax.axis_size("seq"), lax.axis_size("tp")
    block_count = neighbours.shape[0]
    wants = 2 * span_count
    ranks = (wants + seq_count - 1) // seq_count
    outer = seq_count // INNER
    slots = seq_count * ranks
    cap = INNER * ranks
    own_index = lax.axis_index("seq")
    tp_index = lax.axis_index("tp").astype(jnp.int32).reshape(1)

    def all_features(part):
        if tp_count == 2:
            return [part, swapped(part, "tp", 1)]
        return [lax.all_gather(part, "tp", axis=1, tiled=True)]

    def along(x, offset, senders):
        pairs = [(i, i ^ offset) for i in range(seq_count) if i // INNER in senders]
        return lax.ppermute(x, "seq", pairs)

    own_ids = neighbour_ids.reshape(wants)
    group_ids = jnp.stack([own_ids, swapped(own_ids, "seq", 2)])
    mate = swapped(neighbours, "seq", 1)
    incoming = passed_along(queries[:SPAN], "seq", -1)
    own_blocks = after(neighbours, incoming)
    near = swapped(own_blocks, "seq", INNER)
    across = along(own_blocks, 3 * INNER, (1, 2)) if outer == 4 else near

    group_sources = group_ids // block_count
    group_ranks = slot_ranks(group_sources)
    sources = own_index ^ (INNER * jnp.arange(outer)[:, None] + jnp.arange(2))
    hit = (group_sources[None, :, None, None, :] == sources[:, None, :, None, None]) & (
        group_ranks[None, :, None, None, :] == jnp.arange(ranks)[None, None, None, :, None]
    )
    table = jnp.sum(
        jnp.where(hit, (group_ids % block_count)[None, :, None, None, :], 0), axis=-1
    )
    table = table.astype(jnp.int32).reshape(-1)

    own_sources = own_ids // block_count
    places = ((own_sources ^ own_index) * ranks + slot_ranks(own_sources)).astype(jnp.int32)
    order = jnp.arange(wants)
    spans = jnp.sum(
        jnp.where(places[None, :] == jnp.arange(slots)[:, None], order[None, :] // 2, 0), axis=1
    ).astype(jnp.int32)

    def pick(j, part, mate, *others):
        mine, outgoing = pick_blocks(j, ranks, after(table, *others), [part, mate])
        return all_features(mine), swapped(outgoing, "seq", 2)

    def attend(first, groups, held, *others):
        scalars = (tp_index, after(spans, *others))
        return attend_part(first, scalars, groups, windows, weights, slots, held)

    weights = (key_weight.T, value_weight)
    mine, got = pick(0, neighbours, mate, weights[0])
    windows = span_windows(after(queries, mine[0]), incoming, span_count)
    near, across = after((near, across), windows, *mine, got)
    parts = [neighbours, near]
    if outer == 4:
        inside = (own_index // INNER == 1) | (own_index // INNER == 2)
        second = along(near, 3 * INNER, (1, 2))
        outward = along(across, INNER, (1, 2))

    def part_of(j, *others):
        if outer != 4:
            low = j & -j
            return swapped(after(parts[j ^ low], *others), "seq", INNER * low)
        if j == 2:
            return jnp.where(inside, *after((second, outward), *others))
        return jnp.where(inside, *after((across, third), *others))

    groups = [[mine, all_features(got)]]
    mine, got = pick(1, near, swapped(near, "seq", 1))
    held = attend(0, groups[0], None, mine[0])
    for j in range(2, outer):
        parts.append(part_of(j, held, got, mine[-1]))
        if j == 2 and outer == 4:
            third = along(second, INNER, (1, 2))
        groups.append([mine, all_features(after(got, held))])
        mine, got = pick(j, parts[j], swapped(parts[j], "seq", 1))
        held = attend((j - 1) * cap, groups[j - 1], held, mine[0])
    others = all_features(after(got, held))
    held = attend((outer - 1) * cap, [mine], held)
    held = attend((outer - 1) * cap + 2 * ranks, [others], held)

    partials, log_totals = held
    last = mix_last(places, partials, log_totals, span_count)
    carried = passed_along(last, "seq", 1)
    rows = mix(places, partials, log_totals, span_count)
    return with_head(carried, rows)


def solution(mesh):
    in_specs = (P("seq", "tp"), P("seq", "tp", None), P(None, "tp"), P(None, "tp"), P("seq", None))
    out_specs = P("seq", "tp")
    return jax.shard_map(shards, mesh=mesh, in_specs=in_specs, out_specs=out_specs, check_vma=False)
```

```python
import jax
import jax.numpy as jnp
from jax import lax
from jax.experimental import pallas as pl
from jax.experimental.pallas import tpu as pltpu
from jax.sharding import PartitionSpec as P

HDIM = 128
SPAN = 64
PAIR = 2 * HDIM
INNER = 4
LANES = 128
VMEM_LIMIT = 28 * 1024 * 1024


LIGHT = pl.CostEstimate(flops=1000, bytes_accessed=1000, transcendentals=0)
HEAVY = pl.CostEstimate(flops=20 * 10**9, bytes_accessed=10**7, transcendentals=0)


def passed_along(x, axis, by):
    peers = lax.axis_size(axis)
    pairs = [(i, i + by) for i in range(peers) if 0 <= i + by < peers]
    return lax.ppermute(x, axis, pairs)


def swapped(x, axis, offset):
    peers = lax.axis_size(axis)
    return lax.ppermute(x, axis, [(i, i ^ offset) for i in range(peers)])


def slot_ranks(sources):
    positions = sources.shape[-1]
    alike = sources[..., :, None] == sources[..., None, :]
    earlier = jnp.arange(positions)[None, :] < jnp.arange(positions)[:, None]
    return jnp.sum(jnp.where(alike & earlier, 1, 0), axis=-1).astype(jnp.int32)


def windows_kernel(own_ref, next_ref, incoming_ref, out_ref):
    spans = out_ref.shape[0]
    last = pl.program_id(0) == pl.num_programs(0) - 1
    tile = 16
    cut = SPAN - tile
    late = lax.broadcasted_iota(jnp.int32, (tile, out_ref.shape[-1]), 0) == tile - 1
    for n in range(spans):
        if n + 1 < spans:
            later = own_ref[(n + 1) * SPAN : (n + 2) * SPAN, :]
        else:
            later = jnp.where(last, incoming_ref[...], next_ref[...])
        out_ref[n, :cut, :] = later[:cut]
        own = own_ref[n * SPAN + cut : (n + 1) * SPAN, :]
        out_ref[n, cut:, :] = jnp.where(
            late, own.astype(jnp.float32), later[cut:].astype(jnp.float32)
        ).astype(jnp.bfloat16)


def span_windows(queries, incoming, span_count):
    columns = queries.shape[-1]
    per = 4
    steps = span_count // per
    return pl.pallas_call(
        windows_kernel,
        grid=(steps,),
        in_specs=[
            pl.BlockSpec((per * SPAN, columns), lambda u: (u, 0)),
            pl.BlockSpec(
                (SPAN, columns), lambda u: (jnp.minimum(per * (u + 1), span_count - 1), 0)
            ),
            pl.BlockSpec((SPAN, columns), lambda u: (0, 0)),
        ],
        out_specs=pl.BlockSpec((per, SPAN, columns), lambda u: (u, 0, 0)),
        out_shape=jax.ShapeDtypeStruct((span_count, SPAN, columns), jnp.bfloat16),
        compiler_params=pltpu.CompilerParams(vmem_limit_bytes=VMEM_LIMIT),
        cost_estimate=LIGHT,
        name="windows",
    )(queries, queries, incoming)


def pick_kernel(part, ranks, table, *refs):
    sources, outs = refs[:2], refs[2:4]
    held, in_sems, out_sems = refs[-3:]
    fetches, stores = [], []
    for e in range(2):
        for a in range(2):
            for r in range(ranks):
                n = len(fetches)
                block = table[((part * 2 + e) * 2 + a) * ranks + r]
                fetches.append(
                    pltpu.make_async_copy(sources[a].at[block], held.at[n], in_sems.at[n])
                )
                stores.append(
                    pltpu.make_async_copy(held.at[n], outs[e].at[a * ranks + r], out_sems.at[n])
                )
    for fetch in fetches:
        fetch.start()
    for fetch, store in zip(fetches, stores):
        fetch.wait()
        store.start()
    for store in stores:
        store.wait()


def pick_blocks(part, ranks, table, sources):
    shape = sources[0].shape[1:]
    copies = 4 * ranks

    def body(*refs):
        pick_kernel(part, ranks, *refs)

    return pl.pallas_call(
        body,
        grid_spec=pltpu.PrefetchScalarGridSpec(
            num_scalar_prefetch=1,
            grid=(1,),
            in_specs=[pl.BlockSpec(memory_space=pltpu.HBM)] * 2,
            out_specs=[pl.BlockSpec(memory_space=pltpu.HBM)] * 2,
            scratch_shapes=[
                pltpu.VMEM((copies,) + shape, sources[0].dtype),
                pltpu.SemaphoreType.DMA((copies,)),
                pltpu.SemaphoreType.DMA((copies,)),
            ],
        ),
        out_shape=[jax.ShapeDtypeStruct((2 * ranks,) + shape, sources[0].dtype)] * 2,
        compiler_params=pltpu.CompilerParams(vmem_limit_bytes=VMEM_LIMIT),
        cost_estimate=LIGHT,
        name="pick_blocks",
    )(table, *sources)


def attend_kernel(first, cap, pieces, groups, steps, tp_index, spans, *refs):
    count = pieces * groups
    x_refs = refs[:count]
    q_ref, wk_first, wk_next, wv_first, wv_next = refs[count : count + 5]
    out_ref, lse_ref, x_all, xt_all, scores_ref, weights_ref, k_even, v_even, k_odd, v_odd = refs[-10:]
    nlen = scores_ref.shape[-1]
    pairs = scores_ref.shape[0] // cap
    step = pl.program_id(0)
    scale = HDIM ** (-0.5)
    lanes = lax.broadcasted_iota(jnp.int32, (SPAN, LANES), 1)

    def project_keys(w_ref, out):
        out[...] = jnp.dot(w_ref[...], x_all[...], preferred_element_type=jnp.float32).astype(
            jnp.bfloat16
        )

    def project_values(w_ref, out):
        out[...] = jnp.dot(xt_all[...], w_ref[...], preferred_element_type=jnp.float32).astype(
            jnp.bfloat16
        )

    def score(k_ref):
        none = jnp.zeros((SPAN, HDIM), jnp.bfloat16)
        for pair in range(pairs):
            for i in range(cap):
                q = q_ref[spans[first + i], :, pair * PAIR : (pair + 1) * PAIR]
                upper = jnp.concatenate([q[:, :HDIM], none], axis=1)
                lower = jnp.concatenate([none, q[:, HDIM:]], axis=1)
                scores_ref[pair * cap + i] = jnp.dot(
                    jnp.concatenate([upper, lower], axis=0),
                    k_ref[pair * PAIR : (pair + 1) * PAIR, i * nlen : (i + 1) * nlen],
                    preferred_element_type=jnp.float32,
                )

    def soften():
        for i in range(cap):
            held = lse_ref[i]
            for pair in range(pairs):
                scores = scores_ref[pair * cap + i]
                highest = jnp.max(scores, axis=1, keepdims=True)
                exponent = jnp.exp((scores - highest) * scale)
                totals = jnp.sum(exponent, axis=1, keepdims=True)
                weights_ref[pair * cap + i] = (exponent * (1.0 / totals)).astype(jnp.bfloat16)
                lse = highest * scale + jnp.log(totals)
                at = pairs * step + pair
                held = jnp.where(lanes == at, lse[:SPAN], held)
                held = jnp.where(lanes == LANES // 8 + at, lse[SPAN:], held)
            lse_ref[i] = held

    def blend(v_ref):
        for pair in range(pairs):
            cols = slice(pair * PAIR, (pair + 1) * PAIR)
            for i in range(cap):
                blended = jnp.dot(
                    weights_ref[pair * cap + i],
                    v_ref[i * nlen : (i + 1) * nlen, cols],
                    preferred_element_type=jnp.float32,
                )
                out_ref[i, :, cols] = jnp.concatenate(
                    [blended[:SPAN, :HDIM], blended[SPAN:, HDIM:]], axis=1
                ).astype(jnp.bfloat16)

    @pl.when(step == 0)
    def _():
        lse_ref[...] = jnp.zeros_like(lse_ref)
        per = cap // groups
        for n, x_ref in enumerate(x_refs):
            group, piece = n // pieces, n % pieces
            width = x_ref.shape[1]
            top = 0
            if pieces == 2:
                place = tp_index[0] if piece == 0 else 1 - tp_index[0]
                top = pl.multiple_of(place * width, 16)
            for i in range(per):
                left = (group * per + i) * nlen
                x_all[pl.ds(top, width), left : left + nlen] = x_ref[i]
        for i in range(cap):
            at = slice(i * nlen, (i + 1) * nlen)
            xt_all[at, :] = x_all[:, at].T
        project_keys(wk_first, k_even)
        project_values(wv_first, v_even)

    def work(k_now, v_now, k_later, v_later):
        score(k_now)
        project_keys(wk_next, k_later)
        soften()
        project_values(wv_next, v_later)
        blend(v_now)

    def finish(k_now, v_now):
        score(k_now)
        soften()
        blend(v_now)

    if steps > 1:
        pl.when((step < steps - 1) & (step % 2 == 0))(lambda: work(k_even, v_even, k_odd, v_odd))
    if steps > 2:
        pl.when((step < steps - 1) & (step % 2 == 1))(lambda: work(k_odd, v_odd, k_even, v_even))
    ends = (k_even, v_even) if steps % 2 == 1 else (k_odd, v_odd)
    pl.when(step == steps - 1)(lambda: finish(*ends))


def attend_part(first, scalars, groups, windows, weights, slots, held):
    blocks = [x for group in groups for x in group]
    pieces = len(groups[0])
    per, width, nlen = blocks[0].shape
    cap = per * len(groups)
    place = first // cap
    features = width * pieces
    columns = 2 * PAIR
    steps = windows.shape[-1] // columns

    in_specs = [pl.BlockSpec(x.shape, lambda t, *_: (0, 0, 0)) for x in blocks]
    operands = list(blocks)
    in_specs += [pl.BlockSpec((windows.shape[0], SPAN, columns), lambda t, *_: (0, 0, t))]
    operands += [windows]
    key_weight, value_weight = weights
    in_specs += [
        pl.BlockSpec((columns, features), lambda t, *_: (0, 0)),
        pl.BlockSpec((columns, features), lambda t, *_: (jnp.minimum(t + 1, steps - 1), 0)),
        pl.BlockSpec((features, columns), lambda t, *_: (0, 0)),
        pl.BlockSpec((features, columns), lambda t, *_: (0, jnp.minimum(t + 1, steps - 1))),
    ]
    operands += [key_weight] * 2 + [value_weight] * 2
    aliases = {}
    if held is not None:
        in_specs += [pl.BlockSpec(memory_space=pl.ANY)] * 2
        aliases = {2 + len(operands): 0, 3 + len(operands): 1}
        operands += list(held)
    keys = pltpu.VMEM((columns, cap * nlen), jnp.bfloat16)
    values = pltpu.VMEM((cap * nlen, columns), jnp.bfloat16)

    def body(*refs):
        attend_kernel(first, cap, pieces, len(groups), steps, *refs)

    return pl.pallas_call(
        body,
        grid_spec=pltpu.PrefetchScalarGridSpec(
            num_scalar_prefetch=2,
            grid=(steps,),
            in_specs=in_specs,
            out_specs=[
                pl.BlockSpec((cap, SPAN, columns), lambda t, *_: (place, 0, t)),
                pl.BlockSpec((cap, SPAN, LANES), lambda t, *_: (place, 0, 0)),
            ],
            scratch_shapes=[
                pltpu.VMEM((features, cap * nlen), jnp.bfloat16),
                pltpu.VMEM((cap * nlen, features), jnp.bfloat16),
                pltpu.VMEM((2 * cap, 2 * SPAN, nlen), jnp.float32),
                pltpu.VMEM((2 * cap, 2 * SPAN, nlen), jnp.bfloat16),
                keys, values, keys, values,
            ],
        ),
        out_shape=[
            jax.ShapeDtypeStruct((slots,) + windows.shape[1:], jnp.bfloat16),
            jax.ShapeDtypeStruct((slots, SPAN, LANES), jnp.float32),
        ],
        input_output_aliases=aliases,
        compiler_params=pltpu.CompilerParams(vmem_limit_bytes=VMEM_LIMIT),
        cost_estimate=HEAVY,
        name="attend_part",
    )(*scalars, *operands)


def spread_matrix(columns):
    per = LANES // 8
    row = lax.broadcasted_iota(jnp.int32, (4 * per, columns), 0)
    head = lax.broadcasted_iota(jnp.int32, (4 * per, columns), 1) // HDIM
    own = 2 * (row % per) + (row // per) % 2
    return jnp.where(head == own, 1.0, 0.0).astype(jnp.bfloat16)


def first_shares(l0, l1):
    largest = jnp.maximum(l0, l1)
    e0, e1 = jnp.exp(l0 - largest), jnp.exp(l1 - largest)
    share = e0 / (e0 + e1)
    high = share.astype(jnp.bfloat16).astype(jnp.float32)
    low = pltpu.roll(share - high, LANES // 4, 1)
    lanes = lax.broadcasted_iota(jnp.int32, share.shape, 1)
    return jnp.where(lanes < LANES // 4, high, low).astype(jnp.bfloat16)[:, : LANES // 2]


def mixed(p0, p1, shares, spread, cols):
    share = jnp.dot(shares, spread[:, cols], preferred_element_type=jnp.float32)
    return p0[0, :, cols].astype(jnp.float32) * share + p1[0, :, cols].astype(jnp.float32) * (
        1.0 - share
    )


def mix_last_kernel(places, p0, p1, l0, l1, out_ref, spread):
    spread[...] = spread_matrix(out_ref.shape[-1])
    shares = first_shares(l0[0], l1[0])
    for pair in range(out_ref.shape[-1] // PAIR):
        cols = slice(pair * PAIR, (pair + 1) * PAIR)
        out_ref[:, cols] = mixed(p0, p1, shares, spread, cols).astype(jnp.bfloat16)


def mix_kernel(places, *refs):
    ins, (out_ref, before, spread) = refs[:-3], refs[-3:]
    tile = 16
    late = lax.broadcasted_iota(jnp.int32, (tile, PAIR), 0) == tile - 1

    @pl.when(pl.program_id(0) == 0)
    def _():
        spread[...] = spread_matrix(out_ref.shape[-1])

    for n in range(len(ins) // 4):
        p0, p1, l0, l1 = ins[4 * n : 4 * n + 4]
        shares = first_shares(l0[0], l1[0])
        top = n * SPAN
        cut = top + SPAN - tile
        out_ref[top:cut, :] = before[: SPAN - tile, :]
        for pair in range(out_ref.shape[-1] // PAIR):
            cols = slice(pair * PAIR, (pair + 1) * PAIR)
            result = mixed(p0, p1, shares, spread, cols)
            out_ref[cut : cut + tile, cols] = jnp.where(
                late, result[SPAN - tile :], before[SPAN - tile :, cols].astype(jnp.float32)
            ).astype(jnp.bfloat16)
            before[:, cols] = result.astype(jnp.bfloat16)


def mix_specs(partials, log_totals, span_of):
    def place(j, shape):
        return pl.BlockSpec((1,) + shape, lambda k, places: (places[2 * span_of(k) + j], 0, 0))

    rows, stats = partials.shape[1:], log_totals.shape[1:]
    return [place(0, rows), place(1, rows), place(0, stats), place(1, stats)]


def mix_last(places, partials, log_totals, span_count):
    columns = partials.shape[-1]
    return pl.pallas_call(
        mix_last_kernel,
        grid_spec=pltpu.PrefetchScalarGridSpec(
            num_scalar_prefetch=1,
            grid=(1,),
            in_specs=mix_specs(partials, log_totals, lambda k: span_count - 1),
            out_specs=pl.BlockSpec((SPAN, columns), lambda k, places: (0, 0)),
            scratch_shapes=[pltpu.VMEM((LANES // 2, columns), jnp.bfloat16)],
        ),
        out_shape=jax.ShapeDtypeStruct((SPAN, columns), jnp.bfloat16),
        cost_estimate=LIGHT,
        name="mix_last",
    )(places, partials, partials, log_totals, log_totals)


def mix(places, partials, log_totals, span_count):
    columns = partials.shape[-1]
    per = 4
    in_specs = []
    for n in range(per):
        in_specs += mix_specs(partials, log_totals, lambda k, n=n: per * k + n)
    return pl.pallas_call(
        mix_kernel,
        grid_spec=pltpu.PrefetchScalarGridSpec(
            num_scalar_prefetch=1,
            grid=(span_count // per,),
            in_specs=in_specs,
            out_specs=pl.BlockSpec((per * SPAN, columns), lambda k, places: (k, 0)),
            scratch_shapes=[
                pltpu.VMEM((SPAN, columns), jnp.bfloat16),
                pltpu.VMEM((LANES // 2, columns), jnp.bfloat16),
            ],
        ),
        out_shape=jax.ShapeDtypeStruct((span_count * SPAN, columns), jnp.bfloat16),
        compiler_params=pltpu.CompilerParams(vmem_limit_bytes=VMEM_LIMIT),
        cost_estimate=LIGHT,
        name="mix",
    )(places, *([partials, partials, log_totals, log_totals] * per))


def head_kernel(carried, rows, out_ref):
    early = lax.broadcasted_iota(jnp.int32, out_ref.shape, 0) < SPAN - 1
    out_ref[...] = jnp.where(
        early, carried[...].astype(jnp.float32), rows[...].astype(jnp.float32)
    ).astype(jnp.bfloat16)


def with_head(carried, mixed_rows):
    spec = pl.BlockSpec((SPAN, mixed_rows.shape[-1]), lambda k: (0, 0))
    return pl.pallas_call(
        head_kernel,
        grid=(1,),
        in_specs=[spec, spec],
        out_specs=spec,
        out_shape=jax.ShapeDtypeStruct(mixed_rows.shape, mixed_rows.dtype),
        input_output_aliases={1: 0},
        cost_estimate=LIGHT,
        name="with_head",
    )(carried, mixed_rows)


def after(values, *others):
    return lax.optimization_barrier((values, others))[0]


def shards(queries, neighbours, key_weight, value_weight, neighbour_ids):
    span_count = neighbour_ids.shape[0]
    seq_count, tp_count = lax.axis_size("seq"), lax.axis_size("tp")
    block_count = neighbours.shape[0]
    wants = 2 * span_count
    ranks = (wants + seq_count - 1) // seq_count
    outer = seq_count // INNER
    slots = seq_count * ranks
    cap = INNER * ranks
    own_index = lax.axis_index("seq")
    tp_index = lax.axis_index("tp").astype(jnp.int32).reshape(1)

    def all_features(part):
        if tp_count == 2:
            return [part, swapped(part, "tp", 1)]
        return [lax.all_gather(part, "tp", axis=1, tiled=True)]

    def along(x, offset, senders):
        pairs = [(i, i ^ offset) for i in range(seq_count) if i // INNER in senders]
        return lax.ppermute(x, "seq", pairs)

    own_ids = neighbour_ids.reshape(wants)
    group_ids = jnp.stack([own_ids, swapped(own_ids, "seq", 2)])
    mate = swapped(neighbours, "seq", 1)
    incoming = passed_along(queries[:SPAN], "seq", -1)
    own_blocks = after(neighbours, incoming)
    near = swapped(own_blocks, "seq", INNER)
    across = along(own_blocks, 3 * INNER, (1, 2)) if outer == 4 else near

    group_sources = group_ids // block_count
    group_ranks = slot_ranks(group_sources)
    sources = own_index ^ (INNER * jnp.arange(outer)[:, None] + jnp.arange(2))
    hit = (group_sources[None, :, None, None, :] == sources[:, None, :, None, None]) & (
        group_ranks[None, :, None, None, :] == jnp.arange(ranks)[None, None, None, :, None]
    )
    table = jnp.sum(
        jnp.where(hit, (group_ids % block_count)[None, :, None, None, :], 0), axis=-1
    )
    table = table.astype(jnp.int32).reshape(-1)

    own_sources = own_ids // block_count
    places = ((own_sources ^ own_index) * ranks + slot_ranks(own_sources)).astype(jnp.int32)
    order = jnp.arange(wants)
    spans = jnp.sum(
        jnp.where(places[None, :] == jnp.arange(slots)[:, None], order[None, :] // 2, 0), axis=1
    ).astype(jnp.int32)

    def pick(j, part, mate, *others):
        mine, outgoing = pick_blocks(j, ranks, after(table, *others), [part, mate])
        return all_features(mine), swapped(outgoing, "seq", 2)

    def attend(first, groups, held, *others):
        scalars = (tp_index, after(spans, *others))
        return attend_part(first, scalars, groups, windows, weights, slots, held)

    weights = (key_weight.T, value_weight)
    mine, got = pick(0, neighbours, mate, weights[0], incoming)
    near, across = after((near, across), mine[0])
    parts = [neighbours, near]
    if outer == 4:
        inside = (own_index // INNER == 1) | (own_index // INNER == 2)
        second = along(near, 3 * INNER, (1, 2))
        outward = along(across, INNER, (1, 2))

    def part_of(j, *others):
        if outer != 4:
            low = j & -j
            return swapped(after(parts[j ^ low], *others), "seq", INNER * low)
        if j == 2:
            return jnp.where(inside, *after((second, outward), *others))
        return jnp.where(inside, *after((across, third), *others))

    groups = [[mine, all_features(got)]]
    mine, got = pick(1, near, swapped(near, "seq", 1), got, *mine)
    windows = span_windows(after(queries, mine[0]), incoming, span_count)
    groups.append([mine, all_features(after(got, windows))])
    parts.append(part_of(2, groups[1][1][0], *groups[0]))
    if outer == 4:
        third = along(second, INNER, (1, 2))
    mine, got = pick(2, parts[2], swapped(parts[2], "seq", 1))
    held = attend(0, groups[0], None, mine[0])
    for j in range(3, outer):
        groups.append([mine, all_features(after(got, held))])
        parts.append(part_of(j, groups[j - 1][1][0], *groups[j - 2]))
        mine, got = pick(j, parts[j], swapped(parts[j], "seq", 1))
        held = attend((j - 2) * cap, groups[j - 2], held, mine[0])
    groups.append([mine, all_features(after(got, held))])
    held = attend((outer - 2) * cap, groups[outer - 2], held, groups[outer - 1][1][0])
    held = attend((outer - 1) * cap, groups[outer - 1], held)

    partials, log_totals = held
    last = mix_last(places, partials, log_totals, span_count)
    carried = passed_along(last, "seq", 1)
    rows = mix(places, partials, log_totals, span_count)
    return with_head(carried, rows)


def solution(mesh):
    in_specs = (P("seq", "tp"), P("seq", "tp", None), P(None, "tp"), P(None, "tp"), P("seq", None))
    out_specs = P("seq", "tp")
    return jax.shard_map(shards, mesh=mesh, in_specs=in_specs, out_specs=out_specs, check_vma=False)
```

```python
import jax
import jax.numpy as jnp
from jax import lax
from jax.experimental import pallas as pl
from jax.experimental.pallas import tpu as pltpu
from jax.sharding import PartitionSpec as P

HDIM = 128
SPAN = 64
PAIR = 2 * HDIM
INNER = 4
LANES = 128
VMEM_LIMIT = 56 * 1024 * 1024


LIGHT = pl.CostEstimate(flops=1000, bytes_accessed=1000, transcendentals=0)
HEAVY = pl.CostEstimate(flops=20 * 10**9, bytes_accessed=10**7, transcendentals=0)


def passed_along(x, axis, by):
    peers = lax.axis_size(axis)
    pairs = [(i, i + by) for i in range(peers) if 0 <= i + by < peers]
    return lax.ppermute(x, axis, pairs)


def swapped(x, axis, offset):
    peers = lax.axis_size(axis)
    return lax.ppermute(x, axis, [(i, i ^ offset) for i in range(peers)])


def slot_ranks(sources):
    positions = sources.shape[-1]
    alike = sources[..., :, None] == sources[..., None, :]
    earlier = jnp.arange(positions)[None, :] < jnp.arange(positions)[:, None]
    return jnp.sum(jnp.where(alike & earlier, 1, 0), axis=-1).astype(jnp.int32)


def windows_kernel(own_ref, next_ref, incoming_ref, out_ref):
    spans = out_ref.shape[0]
    last = pl.program_id(0) == pl.num_programs(0) - 1
    tile = 16
    cut = SPAN - tile
    late = lax.broadcasted_iota(jnp.int32, (tile, out_ref.shape[-1]), 0) == tile - 1
    for n in range(spans):
        if n + 1 < spans:
            later = own_ref[(n + 1) * SPAN : (n + 2) * SPAN, :]
        else:
            later = jnp.where(last, incoming_ref[...], next_ref[...])
        out_ref[n, :cut, :] = later[:cut]
        own = own_ref[n * SPAN + cut : (n + 1) * SPAN, :]
        out_ref[n, cut:, :] = jnp.where(
            late, own.astype(jnp.float32), later[cut:].astype(jnp.float32)
        ).astype(jnp.bfloat16)


def span_windows(queries, incoming, span_count):
    columns = queries.shape[-1]
    per = 4
    steps = span_count // per
    return pl.pallas_call(
        windows_kernel,
        grid=(steps,),
        in_specs=[
            pl.BlockSpec((per * SPAN, columns), lambda u: (u, 0)),
            pl.BlockSpec(
                (SPAN, columns), lambda u: (jnp.minimum(per * (u + 1), span_count - 1), 0)
            ),
            pl.BlockSpec((SPAN, columns), lambda u: (0, 0)),
        ],
        out_specs=pl.BlockSpec((per, SPAN, columns), lambda u: (u, 0, 0)),
        out_shape=jax.ShapeDtypeStruct((span_count, SPAN, columns), jnp.bfloat16),
        compiler_params=pltpu.CompilerParams(vmem_limit_bytes=VMEM_LIMIT),
        cost_estimate=LIGHT,
        name="windows",
    )(queries, queries, incoming)


def pick_kernel(part, ranks, table, *refs):
    sources, outs = refs[:2], refs[2:4]
    held, in_sems, out_sems = refs[-3:]
    fetches, stores = [], []
    for e in range(2):
        for a in range(2):
            for r in range(ranks):
                n = len(fetches)
                block = table[((part * 2 + e) * 2 + a) * ranks + r]
                fetches.append(
                    pltpu.make_async_copy(sources[a].at[block], held.at[n], in_sems.at[n])
                )
                stores.append(
                    pltpu.make_async_copy(held.at[n], outs[e].at[a * ranks + r], out_sems.at[n])
                )
    for fetch in fetches:
        fetch.start()
    for fetch, store in zip(fetches, stores):
        fetch.wait()
        store.start()
    for store in stores:
        store.wait()


def pick_blocks(part, ranks, table, sources):
    shape = sources[0].shape[1:]
    copies = 4 * ranks

    def body(*refs):
        pick_kernel(part, ranks, *refs)

    return pl.pallas_call(
        body,
        grid_spec=pltpu.PrefetchScalarGridSpec(
            num_scalar_prefetch=1,
            grid=(1,),
            in_specs=[pl.BlockSpec(memory_space=pltpu.HBM)] * 2,
            out_specs=[pl.BlockSpec(memory_space=pltpu.HBM)] * 2,
            scratch_shapes=[
                pltpu.VMEM((copies,) + shape, sources[0].dtype),
                pltpu.SemaphoreType.DMA((copies,)),
                pltpu.SemaphoreType.DMA((copies,)),
            ],
        ),
        out_shape=[jax.ShapeDtypeStruct((2 * ranks,) + shape, sources[0].dtype)] * 2,
        compiler_params=pltpu.CompilerParams(vmem_limit_bytes=VMEM_LIMIT),
        cost_estimate=LIGHT,
        name="pick_blocks",
    )(table, *sources)


def attend_kernel(first, cap, pieces, groups, steps, tp_index, spans, *refs):
    count = pieces * groups
    x_refs = refs[:count]
    q_ref, wk_all, wv_all = refs[count : count + 3]
    out_ref, lse_ref, x_all, xt_all, scores_ref, weights_ref = refs[-13:-7]
    k_even, v_even, k_odd, v_odd, wk_held, wv_held, sems = refs[-7:]
    nlen = scores_ref.shape[-1]
    pairs = scores_ref.shape[0] // cap
    step = pl.program_id(0)
    scale = HDIM ** (-0.5)
    lanes = lax.broadcasted_iota(jnp.int32, (SPAN, LANES), 1)

    columns = wk_held.shape[1]

    def fetches(at, slot):
        cols = pl.ds(pl.multiple_of(at * columns, columns), columns)
        return (
            pltpu.make_async_copy(wk_all.at[cols, :], wk_held.at[slot], sems.at[0, slot]),
            pltpu.make_async_copy(wv_all.at[:, cols], wv_held.at[slot], sems.at[1, slot]),
        )

    def start(at, slot):
        for fetch in fetches(at, slot):
            fetch.start()

    def project_keys(at, slot, out):
        fetches(at, slot)[0].wait()
        out[...] = jnp.dot(wk_held[slot], x_all[...], preferred_element_type=jnp.float32).astype(
            jnp.bfloat16
        )

    def project_values(at, slot, out):
        fetches(at, slot)[1].wait()
        out[...] = jnp.dot(xt_all[...], wv_held[slot], preferred_element_type=jnp.float32).astype(
            jnp.bfloat16
        )

    def score(k_ref):
        none = jnp.zeros((SPAN, HDIM), jnp.bfloat16)
        for pair in range(pairs):
            for i in range(cap):
                q = q_ref[spans[first + i], :, pair * PAIR : (pair + 1) * PAIR]
                upper = jnp.concatenate([q[:, :HDIM], none], axis=1)
                lower = jnp.concatenate([none, q[:, HDIM:]], axis=1)
                scores_ref[pair * cap + i] = jnp.dot(
                    jnp.concatenate([upper, lower], axis=0),
                    k_ref[pair * PAIR : (pair + 1) * PAIR, i * nlen : (i + 1) * nlen],
                    preferred_element_type=jnp.float32,
                )

    def soften():
        for i in range(cap):
            held = lse_ref[i]
            for pair in range(pairs):
                scores = scores_ref[pair * cap + i]
                highest = jnp.max(scores, axis=1, keepdims=True)
                exponent = jnp.exp((scores - highest) * scale)
                totals = jnp.sum(exponent, axis=1, keepdims=True)
                weights_ref[pair * cap + i] = (exponent * (1.0 / totals)).astype(jnp.bfloat16)
                lse = highest * scale + jnp.log(totals)
                at = pairs * step + pair
                held = jnp.where(lanes == at, lse[:SPAN], held)
                held = jnp.where(lanes == LANES // 8 + at, lse[SPAN:], held)
            lse_ref[i] = held

    def blend(v_ref):
        for pair in range(pairs):
            cols = slice(pair * PAIR, (pair + 1) * PAIR)
            for i in range(cap):
                blended = jnp.dot(
                    weights_ref[pair * cap + i],
                    v_ref[i * nlen : (i + 1) * nlen, cols],
                    preferred_element_type=jnp.float32,
                )
                out_ref[i, :, cols] = jnp.concatenate(
                    [blended[:SPAN, :HDIM], blended[SPAN:, HDIM:]], axis=1
                ).astype(jnp.bfloat16)

    @pl.when(step == 0)
    def _():
        for at in range(min(2, steps)):
            start(at, at)
        lse_ref[...] = jnp.zeros_like(lse_ref)
        per = cap // groups
        for n, x_ref in enumerate(x_refs):
            group, piece = n // pieces, n % pieces
            width = x_ref.shape[1]
            top = 0
            if pieces == 2:
                place = tp_index[0] if piece == 0 else 1 - tp_index[0]
                top = pl.multiple_of(place * width, 16)
            for i in range(per):
                left = (group * per + i) * nlen
                x_all[pl.ds(top, width), left : left + nlen] = x_ref[i]
        for i in range(cap):
            at = slice(i * nlen, (i + 1) * nlen)
            xt_all[at, :] = x_all[:, at].T
        project_keys(0, 0, k_even)
        project_values(0, 0, v_even)

    for slot in range(2):
        pl.when((step % 2 == slot) & (step + 2 < steps))(lambda slot=slot: start(step + 2, slot))

    def work(slot, k_now, v_now, k_later, v_later):
        score(k_now)
        project_keys(step + 1, slot, k_later)
        soften()
        project_values(step + 1, slot, v_later)
        blend(v_now)

    def finish(k_now, v_now):
        score(k_now)
        soften()
        blend(v_now)

    if steps > 1:
        pl.when((step < steps - 1) & (step % 2 == 0))(
            lambda: work(1, k_even, v_even, k_odd, v_odd)
        )
    if steps > 2:
        pl.when((step < steps - 1) & (step % 2 == 1))(
            lambda: work(0, k_odd, v_odd, k_even, v_even)
        )
    ends = (k_even, v_even) if steps % 2 == 1 else (k_odd, v_odd)
    pl.when(step == steps - 1)(lambda: finish(*ends))


def attend_part(first, scalars, groups, windows, weights, slots, held):
    blocks = [x for group in groups for x in group]
    pieces = len(groups[0])
    per, width, nlen = blocks[0].shape
    cap = per * len(groups)
    place = first // cap
    features = width * pieces
    columns = 2 * PAIR
    steps = windows.shape[-1] // columns

    in_specs = [pl.BlockSpec(x.shape, lambda t, *_: (0, 0, 0)) for x in blocks]
    operands = list(blocks)
    in_specs += [pl.BlockSpec((windows.shape[0], SPAN, columns), lambda t, *_: (0, 0, t))]
    operands += [windows]
    in_specs += [pl.BlockSpec(memory_space=pl.ANY)] * 2
    operands += list(weights)
    aliases = {}
    if held is not None:
        in_specs += [pl.BlockSpec(memory_space=pl.ANY)] * 2
        aliases = {2 + len(operands): 0, 3 + len(operands): 1}
        operands += list(held)
    keys = pltpu.VMEM((columns, cap * nlen), jnp.bfloat16)
    values = pltpu.VMEM((cap * nlen, columns), jnp.bfloat16)

    def body(*refs):
        attend_kernel(first, cap, pieces, len(groups), steps, *refs)

    return pl.pallas_call(
        body,
        grid_spec=pltpu.PrefetchScalarGridSpec(
            num_scalar_prefetch=2,
            grid=(steps,),
            in_specs=in_specs,
            out_specs=[
                pl.BlockSpec((cap, SPAN, columns), lambda t, *_: (place, 0, t)),
                pl.BlockSpec((cap, SPAN, LANES), lambda t, *_: (place, 0, 0)),
            ],
            scratch_shapes=[
                pltpu.VMEM((features, cap * nlen), jnp.bfloat16),
                pltpu.VMEM((cap * nlen, features), jnp.bfloat16),
                pltpu.VMEM((2 * cap, 2 * SPAN, nlen), jnp.float32),
                pltpu.VMEM((2 * cap, 2 * SPAN, nlen), jnp.bfloat16),
                keys, values, keys, values,
                pltpu.VMEM((2, columns, features), jnp.bfloat16),
                pltpu.VMEM((2, features, columns), jnp.bfloat16),
                pltpu.SemaphoreType.DMA((2, 2)),
            ],
        ),
        out_shape=[
            jax.ShapeDtypeStruct((slots,) + windows.shape[1:], jnp.bfloat16),
            jax.ShapeDtypeStruct((slots, SPAN, LANES), jnp.float32),
        ],
        input_output_aliases=aliases,
        compiler_params=pltpu.CompilerParams(vmem_limit_bytes=VMEM_LIMIT),
        cost_estimate=HEAVY,
        name="attend_part",
    )(*scalars, *operands)


def spread_matrix(columns):
    per = LANES // 8
    row = lax.broadcasted_iota(jnp.int32, (4 * per, columns), 0)
    head = lax.broadcasted_iota(jnp.int32, (4 * per, columns), 1) // HDIM
    own = 2 * (row % per) + (row // per) % 2
    return jnp.where(head == own, 1.0, 0.0).astype(jnp.bfloat16)


def first_shares(l0, l1):
    largest = jnp.maximum(l0, l1)
    e0, e1 = jnp.exp(l0 - largest), jnp.exp(l1 - largest)
    share = e0 / (e0 + e1)
    high = share.astype(jnp.bfloat16).astype(jnp.float32)
    low = pltpu.roll(share - high, LANES // 4, 1)
    lanes = lax.broadcasted_iota(jnp.int32, share.shape, 1)
    return jnp.where(lanes < LANES // 4, high, low).astype(jnp.bfloat16)[:, : LANES // 2]


def mixed(p0, p1, shares, spread, cols):
    share = jnp.dot(shares, spread[:, cols], preferred_element_type=jnp.float32)
    return p0[0, :, cols].astype(jnp.float32) * share + p1[0, :, cols].astype(jnp.float32) * (
        1.0 - share
    )


def mix_last_kernel(places, p0, p1, l0, l1, out_ref, spread):
    spread[...] = spread_matrix(out_ref.shape[-1])
    shares = first_shares(l0[0], l1[0])
    for pair in range(out_ref.shape[-1] // PAIR):
        cols = slice(pair * PAIR, (pair + 1) * PAIR)
        out_ref[:, cols] = mixed(p0, p1, shares, spread, cols).astype(jnp.bfloat16)


def mix_kernel(places, *refs):
    ins, (out_ref, before, spread) = refs[:-3], refs[-3:]
    tile = 16
    late = lax.broadcasted_iota(jnp.int32, (tile, PAIR), 0) == tile - 1

    @pl.when(pl.program_id(0) == 0)
    def _():
        spread[...] = spread_matrix(out_ref.shape[-1])

    for n in range(len(ins) // 4):
        p0, p1, l0, l1 = ins[4 * n : 4 * n + 4]
        shares = first_shares(l0[0], l1[0])
        top = n * SPAN
        cut = top + SPAN - tile
        out_ref[top:cut, :] = before[: SPAN - tile, :]
        for pair in range(out_ref.shape[-1] // PAIR):
            cols = slice(pair * PAIR, (pair + 1) * PAIR)
            result = mixed(p0, p1, shares, spread, cols)
            out_ref[cut : cut + tile, cols] = jnp.where(
                late, result[SPAN - tile :], before[SPAN - tile :, cols].astype(jnp.float32)
            ).astype(jnp.bfloat16)
            before[:, cols] = result.astype(jnp.bfloat16)


def mix_specs(partials, log_totals, span_of):
    def place(j, shape):
        return pl.BlockSpec((1,) + shape, lambda k, places: (places[2 * span_of(k) + j], 0, 0))

    rows, stats = partials.shape[1:], log_totals.shape[1:]
    return [place(0, rows), place(1, rows), place(0, stats), place(1, stats)]


def mix_last(places, partials, log_totals, span_count):
    columns = partials.shape[-1]
    return pl.pallas_call(
        mix_last_kernel,
        grid_spec=pltpu.PrefetchScalarGridSpec(
            num_scalar_prefetch=1,
            grid=(1,),
            in_specs=mix_specs(partials, log_totals, lambda k: span_count - 1),
            out_specs=pl.BlockSpec((SPAN, columns), lambda k, places: (0, 0)),
            scratch_shapes=[pltpu.VMEM((LANES // 2, columns), jnp.bfloat16)],
        ),
        out_shape=jax.ShapeDtypeStruct((SPAN, columns), jnp.bfloat16),
        cost_estimate=LIGHT,
        name="mix_last",
    )(places, partials, partials, log_totals, log_totals)


def mix(places, partials, log_totals, span_count):
    columns = partials.shape[-1]
    per = 4
    in_specs = []
    for n in range(per):
        in_specs += mix_specs(partials, log_totals, lambda k, n=n: per * k + n)
    return pl.pallas_call(
        mix_kernel,
        grid_spec=pltpu.PrefetchScalarGridSpec(
            num_scalar_prefetch=1,
            grid=(span_count // per,),
            in_specs=in_specs,
            out_specs=pl.BlockSpec((per * SPAN, columns), lambda k, places: (k, 0)),
            scratch_shapes=[
                pltpu.VMEM((SPAN, columns), jnp.bfloat16),
                pltpu.VMEM((LANES // 2, columns), jnp.bfloat16),
            ],
        ),
        out_shape=jax.ShapeDtypeStruct((span_count * SPAN, columns), jnp.bfloat16),
        compiler_params=pltpu.CompilerParams(vmem_limit_bytes=VMEM_LIMIT),
        cost_estimate=LIGHT,
        name="mix",
    )(places, *([partials, partials, log_totals, log_totals] * per))


def head_kernel(carried, rows, out_ref):
    early = lax.broadcasted_iota(jnp.int32, out_ref.shape, 0) < SPAN - 1
    out_ref[...] = jnp.where(
        early, carried[...].astype(jnp.float32), rows[...].astype(jnp.float32)
    ).astype(jnp.bfloat16)


def with_head(carried, mixed_rows):
    spec = pl.BlockSpec((SPAN, mixed_rows.shape[-1]), lambda k: (0, 0))
    return pl.pallas_call(
        head_kernel,
        grid=(1,),
        in_specs=[spec, spec],
        out_specs=spec,
        out_shape=jax.ShapeDtypeStruct(mixed_rows.shape, mixed_rows.dtype),
        input_output_aliases={1: 0},
        cost_estimate=LIGHT,
        name="with_head",
    )(carried, mixed_rows)


def after(values, *others):
    return lax.optimization_barrier((values, others))[0]


def shards(queries, neighbours, key_weight, value_weight, neighbour_ids):
    span_count = neighbour_ids.shape[0]
    seq_count, tp_count = lax.axis_size("seq"), lax.axis_size("tp")
    block_count = neighbours.shape[0]
    wants = 2 * span_count
    ranks = (wants + seq_count - 1) // seq_count
    outer = seq_count // INNER
    slots = seq_count * ranks
    cap = INNER * ranks
    own_index = lax.axis_index("seq")
    tp_index = lax.axis_index("tp").astype(jnp.int32).reshape(1)

    def all_features(part):
        if tp_count == 2:
            return [part, swapped(part, "tp", 1)]
        return [lax.all_gather(part, "tp", axis=1, tiled=True)]

    def along(x, offset, senders):
        pairs = [(i, i ^ offset) for i in range(seq_count) if i // INNER in senders]
        return lax.ppermute(x, "seq", pairs)

    own_ids = neighbour_ids.reshape(wants)
    group_ids = jnp.stack([own_ids, swapped(own_ids, "seq", 2)])
    mate = swapped(neighbours, "seq", 1)
    incoming = passed_along(queries[:SPAN], "seq", -1)
    own_blocks = after(neighbours, incoming)
    near = swapped(own_blocks, "seq", INNER)
    across = along(own_blocks, 3 * INNER, (1, 2)) if outer == 4 else near

    group_sources = group_ids // block_count
    group_ranks = slot_ranks(group_sources)
    sources = own_index ^ (INNER * jnp.arange(outer)[:, None] + jnp.arange(2))
    hit = (group_sources[None, :, None, None, :] == sources[:, None, :, None, None]) & (
        group_ranks[None, :, None, None, :] == jnp.arange(ranks)[None, None, None, :, None]
    )
    table = jnp.sum(
        jnp.where(hit, (group_ids % block_count)[None, :, None, None, :], 0), axis=-1
    )
    table = table.astype(jnp.int32).reshape(-1)

    own_sources = own_ids // block_count
    places = ((own_sources ^ own_index) * ranks + slot_ranks(own_sources)).astype(jnp.int32)
    order = jnp.arange(wants)
    spans = jnp.sum(
        jnp.where(places[None, :] == jnp.arange(slots)[:, None], order[None, :] // 2, 0), axis=1
    ).astype(jnp.int32)

    def pick(j, part, mate, *others):
        mine, outgoing = pick_blocks(j, ranks, after(table, *others), [part, mate])
        return all_features(mine), swapped(outgoing, "seq", 2)

    def attend(first, groups, held, *others):
        scalars = (tp_index, after(spans, *others))
        return attend_part(first, scalars, groups, windows, weights, slots, held)

    weights = (key_weight.T, value_weight)
    mine, got = pick(0, neighbours, mate, weights[0], incoming)
    near, across = after((near, across), mine[0])
    parts = [neighbours, near]
    if outer == 4:
        inside = (own_index // INNER == 1) | (own_index // INNER == 2)
        second = along(near, 3 * INNER, (1, 2))
        outward = along(across, INNER, (1, 2))

    def part_of(j, *others):
        if outer != 4:
            low = j & -j
            return swapped(after(parts[j ^ low], *others), "seq", INNER * low)
        if j == 2:
            return jnp.where(inside, *after((second, outward), *others))
        return jnp.where(inside, *after((across, third), *others))

    groups = [[mine, all_features(got)]]
    mine, got = pick(1, near, swapped(near, "seq", 1), got, *mine)
    windows = span_windows(after(queries, mine[0]), incoming, span_count)
    groups.append([mine, all_features(after(got, windows))])
    parts.append(part_of(2, groups[1][1][0], *groups[0]))
    if outer == 4:
        third = along(second, INNER, (1, 2))
    mine, got = pick(2, parts[2], swapped(parts[2], "seq", 1))
    held = attend(0, groups[0], None, mine[0])
    for j in range(3, outer):
        groups.append([mine, all_features(after(got, held))])
        parts.append(part_of(j, groups[j - 1][1][0], *groups[j - 2]))
        mine, got = pick(j, parts[j], swapped(parts[j], "seq", 1))
        held = attend((j - 2) * cap, groups[j - 2], held, mine[0])
    groups.append([mine, all_features(after(got, held))])
    held = attend((outer - 2) * cap, groups[outer - 2], held, groups[outer - 1][1][0])
    held = attend((outer - 1) * cap, groups[outer - 1], held)

    partials, log_totals = held
    last = mix_last(places, partials, log_totals, span_count)
    carried = passed_along(last, "seq", 1)
    rows = mix(places, partials, log_totals, span_count)
    return with_head(carried, rows)


def solution(mesh):
    in_specs = (P("seq", "tp"), P("seq", "tp", None), P(None, "tp"), P(None, "tp"), P("seq", None))
    out_specs = P("seq", "tp")
    return jax.shard_map(shards, mesh=mesh, in_specs=in_specs, out_specs=out_specs, check_vma=False)
```

```python
import jax
import jax.numpy as jnp
from jax import lax
from jax.experimental import pallas as pl
from jax.experimental.pallas import tpu as pltpu
from jax.sharding import PartitionSpec as P

HDIM = 128
SPAN = 64
PAIR = 2 * HDIM
INNER = 4
LANES = 128
VMEM_LIMIT = 28 * 1024 * 1024


LIGHT = pl.CostEstimate(flops=1000, bytes_accessed=1000, transcendentals=0)
HEAVY = pl.CostEstimate(flops=20 * 10**9, bytes_accessed=10**7, transcendentals=0)


def far_from_core(x):
    return pltpu.with_memory_space_constraint(x, pltpu.HBM)


def passed_along(x, axis, by):
    peers = lax.axis_size(axis)
    pairs = [(i, i + by) for i in range(peers) if 0 <= i + by < peers]
    return lax.ppermute(x, axis, pairs)


def swapped(x, axis, offset):
    peers = lax.axis_size(axis)
    return lax.ppermute(x, axis, [(i, i ^ offset) for i in range(peers)])


def slot_ranks(sources):
    positions = sources.shape[-1]
    alike = sources[..., :, None] == sources[..., None, :]
    earlier = jnp.arange(positions)[None, :] < jnp.arange(positions)[:, None]
    return jnp.sum(jnp.where(alike & earlier, 1, 0), axis=-1).astype(jnp.int32)


def windows_kernel(own_ref, next_ref, incoming_ref, out_ref):
    spans = out_ref.shape[0]
    last = pl.program_id(0) == pl.num_programs(0) - 1
    tile = 16
    cut = SPAN - tile
    late = lax.broadcasted_iota(jnp.int32, (tile, out_ref.shape[-1]), 0) == tile - 1
    for n in range(spans):
        if n + 1 < spans:
            later = own_ref[(n + 1) * SPAN : (n + 2) * SPAN, :]
        else:
            later = jnp.where(last, incoming_ref[...], next_ref[...])
        out_ref[n, :cut, :] = later[:cut]
        own = own_ref[n * SPAN + cut : (n + 1) * SPAN, :]
        out_ref[n, cut:, :] = jnp.where(
            late, own.astype(jnp.float32), later[cut:].astype(jnp.float32)
        ).astype(jnp.bfloat16)


def span_windows(queries, incoming, span_count):
    columns = queries.shape[-1]
    per = 4
    steps = span_count // per
    return pl.pallas_call(
        windows_kernel,
        grid=(steps,),
        in_specs=[
            pl.BlockSpec((per * SPAN, columns), lambda u: (u, 0)),
            pl.BlockSpec(
                (SPAN, columns), lambda u: (jnp.minimum(per * (u + 1), span_count - 1), 0)
            ),
            pl.BlockSpec((SPAN, columns), lambda u: (0, 0)),
        ],
        out_specs=pl.BlockSpec((per, SPAN, columns), lambda u: (u, 0, 0)),
        out_shape=pltpu.HBM((span_count, SPAN, columns), jnp.bfloat16),
        compiler_params=pltpu.CompilerParams(vmem_limit_bytes=VMEM_LIMIT),
        cost_estimate=LIGHT,
        name="windows",
    )(far_from_core(queries), far_from_core(queries), incoming)


def pick_kernel(part, ranks, table, *refs):
    sources, outs = refs[:2], refs[2:4]
    held, in_sems, out_sems = refs[-3:]
    fetches, stores = [], []
    for e in range(2):
        for a in range(2):
            for r in range(ranks):
                n = len(fetches)
                block = table[((part * 2 + e) * 2 + a) * ranks + r]
                fetches.append(
                    pltpu.make_async_copy(sources[a].at[block], held.at[n], in_sems.at[n])
                )
                stores.append(
                    pltpu.make_async_copy(held.at[n], outs[e].at[a * ranks + r], out_sems.at[n])
                )
    for fetch in fetches:
        fetch.start()
    for fetch, store in zip(fetches, stores):
        fetch.wait()
        store.start()
    for store in stores:
        store.wait()


def pick_blocks(part, ranks, table, sources):
    shape = sources[0].shape[1:]
    copies = 4 * ranks

    def body(*refs):
        pick_kernel(part, ranks, *refs)

    return pl.pallas_call(
        body,
        grid_spec=pltpu.PrefetchScalarGridSpec(
            num_scalar_prefetch=1,
            grid=(1,),
            in_specs=[pl.BlockSpec(memory_space=pltpu.HBM)] * 2,
            out_specs=[pl.BlockSpec(memory_space=pltpu.HBM)] * 2,
            scratch_shapes=[
                pltpu.VMEM((copies,) + shape, sources[0].dtype),
                pltpu.SemaphoreType.DMA((copies,)),
                pltpu.SemaphoreType.DMA((copies,)),
            ],
        ),
        out_shape=[jax.ShapeDtypeStruct((2 * ranks,) + shape, sources[0].dtype)] * 2,
        compiler_params=pltpu.CompilerParams(vmem_limit_bytes=VMEM_LIMIT),
        cost_estimate=LIGHT,
        name="pick_blocks",
    )(table, *sources)


def attend_kernel(first, cap, pieces, groups, steps, tp_index, spans, *refs):
    count = pieces * groups
    x_refs = refs[:count]
    q_ref, wk_first, wk_next, wv_first, wv_next = refs[count : count + 5]
    out_ref, lse_ref, x_all, xt_all, scores_ref, weights_ref, k_even, v_even, k_odd, v_odd = refs[-10:]
    nlen = scores_ref.shape[-1]
    pairs = scores_ref.shape[0] // cap
    step = pl.program_id(0)
    scale = HDIM ** (-0.5)
    lanes = lax.broadcasted_iota(jnp.int32, (SPAN, LANES), 1)

    def project_keys(w_ref, out):
        out[...] = jnp.dot(w_ref[...], x_all[...], preferred_element_type=jnp.float32).astype(
            jnp.bfloat16
        )

    def project_values(w_ref, out):
        out[...] = jnp.dot(xt_all[...], w_ref[...], preferred_element_type=jnp.float32).astype(
            jnp.bfloat16
        )

    def score(k_ref):
        none = jnp.zeros((SPAN, HDIM), jnp.bfloat16)
        for pair in range(pairs):
            for i in range(cap):
                q = q_ref[spans[first + i], :, pair * PAIR : (pair + 1) * PAIR]
                upper = jnp.concatenate([q[:, :HDIM], none], axis=1)
                lower = jnp.concatenate([none, q[:, HDIM:]], axis=1)
                scores_ref[pair * cap + i] = jnp.dot(
                    jnp.concatenate([upper, lower], axis=0),
                    k_ref[pair * PAIR : (pair + 1) * PAIR, i * nlen : (i + 1) * nlen],
                    preferred_element_type=jnp.float32,
                )

    def soften():
        for i in range(cap):
            held = lse_ref[i]
            for pair in range(pairs):
                scores = scores_ref[pair * cap + i]
                highest = jnp.max(scores, axis=1, keepdims=True)
                exponent = jnp.exp((scores - highest) * scale)
                totals = jnp.sum(exponent, axis=1, keepdims=True)
                weights_ref[pair * cap + i] = (exponent * (1.0 / totals)).astype(jnp.bfloat16)
                lse = highest * scale + jnp.log(totals)
                at = pairs * step + pair
                held = jnp.where(lanes == at, lse[:SPAN], held)
                held = jnp.where(lanes == LANES // 8 + at, lse[SPAN:], held)
            lse_ref[i] = held

    def blend(v_ref):
        for pair in range(pairs):
            cols = slice(pair * PAIR, (pair + 1) * PAIR)
            for i in range(cap):
                blended = jnp.dot(
                    weights_ref[pair * cap + i],
                    v_ref[i * nlen : (i + 1) * nlen, cols],
                    preferred_element_type=jnp.float32,
                )
                out_ref[i, :, cols] = jnp.concatenate(
                    [blended[:SPAN, :HDIM], blended[SPAN:, HDIM:]], axis=1
                ).astype(jnp.bfloat16)

    @pl.when(step == 0)
    def _():
        lse_ref[...] = jnp.zeros_like(lse_ref)
        per = cap // groups
        for n, x_ref in enumerate(x_refs):
            group, piece = n // pieces, n % pieces
            width = x_ref.shape[1]
            top = 0
            if pieces == 2:
                place = tp_index[0] if piece == 0 else 1 - tp_index[0]
                top = pl.multiple_of(place * width, 16)
            for i in range(per):
                left = (group * per + i) * nlen
                x_all[pl.ds(top, width), left : left + nlen] = x_ref[i]
        for i in range(cap):
            at = slice(i * nlen, (i + 1) * nlen)
            xt_all[at, :] = x_all[:, at].T
        project_keys(wk_first, k_even)
        project_values(wv_first, v_even)

    def work(k_now, v_now, k_later, v_later):
        score(k_now)
        project_keys(wk_next, k_later)
        soften()
        project_values(wv_next, v_later)
        blend(v_now)

    def finish(k_now, v_now):
        score(k_now)
        soften()
        blend(v_now)

    if steps > 1:
        pl.when((step < steps - 1) & (step % 2 == 0))(lambda: work(k_even, v_even, k_odd, v_odd))
    if steps > 2:
        pl.when((step < steps - 1) & (step % 2 == 1))(lambda: work(k_odd, v_odd, k_even, v_even))
    ends = (k_even, v_even) if steps % 2 == 1 else (k_odd, v_odd)
    pl.when(step == steps - 1)(lambda: finish(*ends))


def attend_part(first, scalars, groups, windows, weights, slots, held):
    blocks = [x for group in groups for x in group]
    pieces = len(groups[0])
    per, width, nlen = blocks[0].shape
    cap = per * len(groups)
    place = first // cap
    features = width * pieces
    columns = 2 * PAIR
    steps = windows.shape[-1] // columns

    in_specs = [pl.BlockSpec(x.shape, lambda t, *_: (0, 0, 0)) for x in blocks]
    operands = list(blocks)
    in_specs += [pl.BlockSpec((windows.shape[0], SPAN, columns), lambda t, *_: (0, 0, t))]
    operands += [far_from_core(windows)]
    key_weight, value_weight = weights
    in_specs += [
        pl.BlockSpec((columns, features), lambda t, *_: (0, 0)),
        pl.BlockSpec((columns, features), lambda t, *_: (jnp.minimum(t + 1, steps - 1), 0)),
        pl.BlockSpec((features, columns), lambda t, *_: (0, 0)),
        pl.BlockSpec((features, columns), lambda t, *_: (0, jnp.minimum(t + 1, steps - 1))),
    ]
    operands += [key_weight] * 2 + [value_weight] * 2
    aliases = {}
    if held is not None:
        in_specs += [pl.BlockSpec(memory_space=pl.ANY)] * 2
        aliases = {2 + len(operands): 0, 3 + len(operands): 1}
        operands += list(held)
    keys = pltpu.VMEM((columns, cap * nlen), jnp.bfloat16)
    values = pltpu.VMEM((cap * nlen, columns), jnp.bfloat16)

    def body(*refs):
        attend_kernel(first, cap, pieces, len(groups), steps, *refs)

    return pl.pallas_call(
        body,
        grid_spec=pltpu.PrefetchScalarGridSpec(
            num_scalar_prefetch=2,
            grid=(steps,),
            in_specs=in_specs,
            out_specs=[
                pl.BlockSpec((cap, SPAN, columns), lambda t, *_: (place, 0, t)),
                pl.BlockSpec((cap, SPAN, LANES), lambda t, *_: (place, 0, 0)),
            ],
            scratch_shapes=[
                pltpu.VMEM((features, cap * nlen), jnp.bfloat16),
                pltpu.VMEM((cap * nlen, features), jnp.bfloat16),
                pltpu.VMEM((2 * cap, 2 * SPAN, nlen), jnp.float32),
                pltpu.VMEM((2 * cap, 2 * SPAN, nlen), jnp.bfloat16),
                keys, values, keys, values,
            ],
        ),
        out_shape=[
            pltpu.HBM((slots,) + windows.shape[1:], jnp.bfloat16),
            pltpu.HBM((slots, SPAN, LANES), jnp.float32),
        ],
        input_output_aliases=aliases,
        compiler_params=pltpu.CompilerParams(vmem_limit_bytes=VMEM_LIMIT),
        cost_estimate=HEAVY,
        name="attend_part",
    )(*scalars, *operands)


def spread_matrix(columns):
    per = LANES // 8
    row = lax.broadcasted_iota(jnp.int32, (4 * per, columns), 0)
    head = lax.broadcasted_iota(jnp.int32, (4 * per, columns), 1) // HDIM
    own = 2 * (row % per) + (row // per) % 2
    return jnp.where(head == own, 1.0, 0.0).astype(jnp.bfloat16)


def first_shares(l0, l1):
    largest = jnp.maximum(l0, l1)
    e0, e1 = jnp.exp(l0 - largest), jnp.exp(l1 - largest)
    share = e0 / (e0 + e1)
    high = share.astype(jnp.bfloat16).astype(jnp.float32)
    low = pltpu.roll(share - high, LANES // 4, 1)
    lanes = lax.broadcasted_iota(jnp.int32, share.shape, 1)
    return jnp.where(lanes < LANES // 4, high, low).astype(jnp.bfloat16)[:, : LANES // 2]


def mixed(p0, p1, shares, spread, cols):
    share = jnp.dot(shares, spread[:, cols], preferred_element_type=jnp.float32)
    return p0[0, :, cols].astype(jnp.float32) * share + p1[0, :, cols].astype(jnp.float32) * (
        1.0 - share
    )


def mix_last_kernel(places, p0, p1, l0, l1, out_ref, spread):
    spread[...] = spread_matrix(out_ref.shape[-1])
    shares = first_shares(l0[0], l1[0])
    for pair in range(out_ref.shape[-1] // PAIR):
        cols = slice(pair * PAIR, (pair + 1) * PAIR)
        out_ref[:, cols] = mixed(p0, p1, shares, spread, cols).astype(jnp.bfloat16)


def mix_kernel(places, *refs):
    ins, (out_ref, before, spread) = refs[:-3], refs[-3:]
    tile = 16
    late = lax.broadcasted_iota(jnp.int32, (tile, PAIR), 0) == tile - 1

    @pl.when(pl.program_id(0) == 0)
    def _():
        spread[...] = spread_matrix(out_ref.shape[-1])

    for n in range(len(ins) // 4):
        p0, p1, l0, l1 = ins[4 * n : 4 * n + 4]
        shares = first_shares(l0[0], l1[0])
        top = n * SPAN
        cut = top + SPAN - tile
        out_ref[top:cut, :] = before[: SPAN - tile, :]
        for pair in range(out_ref.shape[-1] // PAIR):
            cols = slice(pair * PAIR, (pair + 1) * PAIR)
            result = mixed(p0, p1, shares, spread, cols)
            out_ref[cut : cut + tile, cols] = jnp.where(
                late, result[SPAN - tile :], before[SPAN - tile :, cols].astype(jnp.float32)
            ).astype(jnp.bfloat16)
            before[:, cols] = result.astype(jnp.bfloat16)


def mix_specs(partials, log_totals, span_of):
    def place(j, shape):
        return pl.BlockSpec((1,) + shape, lambda k, places: (places[2 * span_of(k) + j], 0, 0))

    rows, stats = partials.shape[1:], log_totals.shape[1:]
    return [place(0, rows), place(1, rows), place(0, stats), place(1, stats)]


def mix_last(places, partials, log_totals, span_count):
    columns = partials.shape[-1]
    return pl.pallas_call(
        mix_last_kernel,
        grid_spec=pltpu.PrefetchScalarGridSpec(
            num_scalar_prefetch=1,
            grid=(1,),
            in_specs=mix_specs(partials, log_totals, lambda k: span_count - 1),
            out_specs=pl.BlockSpec((SPAN, columns), lambda k, places: (0, 0)),
            scratch_shapes=[pltpu.VMEM((LANES // 2, columns), jnp.bfloat16)],
        ),
        out_shape=jax.ShapeDtypeStruct((SPAN, columns), jnp.bfloat16),
        cost_estimate=LIGHT,
        name="mix_last",
    )(places, *[far_from_core(x) for x in (partials, partials, log_totals, log_totals)])


def mix(places, partials, log_totals, span_count):
    columns = partials.shape[-1]
    per = 4
    in_specs = []
    for n in range(per):
        in_specs += mix_specs(partials, log_totals, lambda k, n=n: per * k + n)
    return pl.pallas_call(
        mix_kernel,
        grid_spec=pltpu.PrefetchScalarGridSpec(
            num_scalar_prefetch=1,
            grid=(span_count // per,),
            in_specs=in_specs,
            out_specs=pl.BlockSpec((per * SPAN, columns), lambda k, places: (k, 0)),
            scratch_shapes=[
                pltpu.VMEM((SPAN, columns), jnp.bfloat16),
                pltpu.VMEM((LANES // 2, columns), jnp.bfloat16),
            ],
        ),
        out_shape=jax.ShapeDtypeStruct((span_count * SPAN, columns), jnp.bfloat16),
        compiler_params=pltpu.CompilerParams(vmem_limit_bytes=VMEM_LIMIT),
        cost_estimate=LIGHT,
        name="mix",
    )(places, *([far_from_core(x) for x in (partials, partials, log_totals, log_totals)] * per))


def head_kernel(carried, rows, out_ref):
    early = lax.broadcasted_iota(jnp.int32, out_ref.shape, 0) < SPAN - 1
    out_ref[...] = jnp.where(
        early, carried[...].astype(jnp.float32), rows[...].astype(jnp.float32)
    ).astype(jnp.bfloat16)


def with_head(carried, mixed_rows):
    spec = pl.BlockSpec((SPAN, mixed_rows.shape[-1]), lambda k: (0, 0))
    return pl.pallas_call(
        head_kernel,
        grid=(1,),
        in_specs=[spec, spec],
        out_specs=spec,
        out_shape=jax.ShapeDtypeStruct(mixed_rows.shape, mixed_rows.dtype),
        input_output_aliases={1: 0},
        cost_estimate=LIGHT,
        name="with_head",
    )(carried, mixed_rows)


def after(values, *others):
    return lax.optimization_barrier((values, others))[0]


def shards(queries, neighbours, key_weight, value_weight, neighbour_ids):
    span_count = neighbour_ids.shape[0]
    seq_count, tp_count = lax.axis_size("seq"), lax.axis_size("tp")
    block_count = neighbours.shape[0]
    wants = 2 * span_count
    ranks = (wants + seq_count - 1) // seq_count
    outer = seq_count // INNER
    slots = seq_count * ranks
    cap = INNER * ranks
    own_index = lax.axis_index("seq")
    tp_index = lax.axis_index("tp").astype(jnp.int32).reshape(1)

    def all_features(part):
        if tp_count == 2:
            return [part, swapped(part, "tp", 1)]
        return [lax.all_gather(part, "tp", axis=1, tiled=True)]

    def along(x, offset, senders):
        pairs = [(i, i ^ offset) for i in range(seq_count) if i // INNER in senders]
        return lax.ppermute(x, "seq", pairs)

    own_ids = neighbour_ids.reshape(wants)
    group_ids = jnp.stack([own_ids, swapped(own_ids, "seq", 2)])
    mate = swapped(neighbours, "seq", 1)
    incoming = passed_along(queries[:SPAN], "seq", -1)
    own_blocks = after(neighbours, incoming)
    near = swapped(own_blocks, "seq", INNER)
    across = along(own_blocks, 3 * INNER, (1, 2)) if outer == 4 else near

    group_sources = group_ids // block_count
    group_ranks = slot_ranks(group_sources)
    sources = own_index ^ (INNER * jnp.arange(outer)[:, None] + jnp.arange(2))
    hit = (group_sources[None, :, None, None, :] == sources[:, None, :, None, None]) & (
        group_ranks[None, :, None, None, :] == jnp.arange(ranks)[None, None, None, :, None]
    )
    table = jnp.sum(
        jnp.where(hit, (group_ids % block_count)[None, :, None, None, :], 0), axis=-1
    )
    table = table.astype(jnp.int32).reshape(-1)

    own_sources = own_ids // block_count
    places = ((own_sources ^ own_index) * ranks + slot_ranks(own_sources)).astype(jnp.int32)
    order = jnp.arange(wants)
    spans = jnp.sum(
        jnp.where(places[None, :] == jnp.arange(slots)[:, None], order[None, :] // 2, 0), axis=1
    ).astype(jnp.int32)

    def pick(j, part, mate, *others):
        mine, outgoing = pick_blocks(j, ranks, after(table, *others), [part, mate])
        return all_features(mine), swapped(outgoing, "seq", 2)

    def attend(first, groups, held, *others):
        scalars = (tp_index, after(spans, *others))
        return attend_part(first, scalars, groups, windows, weights, slots, held)

    weights = (key_weight.T, value_weight)
    mine, got = pick(0, neighbours, mate, weights[0], incoming)
    near, across = after((near, across), mine[0])
    parts = [neighbours, near]
    if outer == 4:
        inside = (own_index // INNER == 1) | (own_index // INNER == 2)
        second = along(near, 3 * INNER, (1, 2))
        outward = along(across, INNER, (1, 2))

    def part_of(j, *others):
        if outer != 4:
            low = j & -j
            return swapped(after(parts[j ^ low], *others), "seq", INNER * low)
        if j == 2:
            return jnp.where(inside, *after((second, outward), *others))
        return jnp.where(inside, *after((across, third), *others))

    groups = [[mine, all_features(got)]]
    mine, got = pick(1, near, swapped(near, "seq", 1), got, *mine)
    windows = span_windows(after(queries, mine[0]), incoming, span_count)
    groups.append([mine, all_features(after(got, windows))])
    parts.append(part_of(2, groups[1][1][0], *groups[0]))
    if outer == 4:
        third = along(second, INNER, (1, 2))
    mine, got = pick(2, parts[2], swapped(parts[2], "seq", 1))
    held = attend(0, groups[0], None, mine[0])
    for j in range(3, outer):
        groups.append([mine, all_features(after(got, held))])
        parts.append(part_of(j, groups[j - 1][1][0], *groups[j - 2]))
        mine, got = pick(j, parts[j], swapped(parts[j], "seq", 1))
        held = attend((j - 2) * cap, groups[j - 2], held, mine[0])
    groups.append([mine, all_features(after(got, held))])
    held = attend((outer - 2) * cap, groups[outer - 2], held, groups[outer - 1][1][0])
    held = attend((outer - 1) * cap, groups[outer - 1], held)

    partials, log_totals = held
    last = mix_last(places, partials, log_totals, span_count)
    carried = passed_along(last, "seq", 1)
    rows = mix(places, partials, log_totals, span_count)
    return with_head(carried, rows)


def solution(mesh):
    in_specs = (P("seq", "tp"), P("seq", "tp", None), P(None, "tp"), P(None, "tp"), P("seq", None))
    out_specs = P("seq", "tp")
    return jax.shard_map(shards, mesh=mesh, in_specs=in_specs, out_specs=out_specs, check_vma=False)
```

```python
import jax
import jax.numpy as jnp
from jax import lax
from jax.experimental import pallas as pl
from jax.experimental.pallas import tpu as pltpu
from jax.sharding import PartitionSpec as P

HDIM = 128
SPAN = 64
PAIR = 2 * HDIM
INNER = 4
LANES = 128
VMEM_LIMIT = 28 * 1024 * 1024


LIGHT = pl.CostEstimate(flops=1000, bytes_accessed=1000, transcendentals=0)
HEAVY = pl.CostEstimate(flops=20 * 10**9, bytes_accessed=10**7, transcendentals=0)


def far_from_core(x):
    return pltpu.with_memory_space_constraint(x, pltpu.HBM)


def passed_along(x, axis, by):
    peers = lax.axis_size(axis)
    pairs = [(i, i + by) for i in range(peers) if 0 <= i + by < peers]
    return lax.ppermute(x, axis, pairs)


def swapped(x, axis, offset):
    peers = lax.axis_size(axis)
    return lax.ppermute(x, axis, [(i, i ^ offset) for i in range(peers)])


def slot_ranks(sources):
    positions = sources.shape[-1]
    alike = sources[..., :, None] == sources[..., None, :]
    earlier = jnp.arange(positions)[None, :] < jnp.arange(positions)[:, None]
    return jnp.sum(jnp.where(alike & earlier, 1, 0), axis=-1).astype(jnp.int32)


def windows_kernel(own_ref, next_ref, incoming_ref, out_ref):
    spans = out_ref.shape[0]
    last = pl.program_id(0) == pl.num_programs(0) - 1
    tile = 16
    cut = SPAN - tile
    late = lax.broadcasted_iota(jnp.int32, (tile, out_ref.shape[-1]), 0) == tile - 1
    for n in range(spans):
        if n + 1 < spans:
            later = own_ref[(n + 1) * SPAN : (n + 2) * SPAN, :]
        else:
            later = jnp.where(last, incoming_ref[...], next_ref[...])
        out_ref[n, :cut, :] = later[:cut]
        own = own_ref[n * SPAN + cut : (n + 1) * SPAN, :]
        out_ref[n, cut:, :] = jnp.where(
            late, own.astype(jnp.float32), later[cut:].astype(jnp.float32)
        ).astype(jnp.bfloat16)


def span_windows(queries, incoming, span_count):
    columns = queries.shape[-1]
    per = 4
    steps = span_count // per
    return pl.pallas_call(
        windows_kernel,
        grid=(steps,),
        in_specs=[
            pl.BlockSpec((per * SPAN, columns), lambda u: (u, 0)),
            pl.BlockSpec(
                (SPAN, columns), lambda u: (jnp.minimum(per * (u + 1), span_count - 1), 0)
            ),
            pl.BlockSpec((SPAN, columns), lambda u: (0, 0)),
        ],
        out_specs=pl.BlockSpec((per, SPAN, columns), lambda u: (u, 0, 0)),
        out_shape=pltpu.HBM((span_count, SPAN, columns), jnp.bfloat16),
        compiler_params=pltpu.CompilerParams(vmem_limit_bytes=VMEM_LIMIT),
        cost_estimate=LIGHT,
        name="windows",
    )(far_from_core(queries), far_from_core(queries), incoming)


def pick_kernel(part, ranks, table, *refs):
    sources, outs = refs[:2], refs[2:4]
    held, in_sems, out_sems = refs[-3:]
    fetches, stores = [], []
    for e in range(2):
        for a in range(2):
            for r in range(ranks):
                n = len(fetches)
                block = table[((part * 2 + e) * 2 + a) * ranks + r]
                fetches.append(
                    pltpu.make_async_copy(sources[a].at[block], held.at[n], in_sems.at[n])
                )
                stores.append(
                    pltpu.make_async_copy(held.at[n], outs[e].at[a * ranks + r], out_sems.at[n])
                )
    for fetch in fetches:
        fetch.start()
    for fetch, store in zip(fetches, stores):
        fetch.wait()
        store.start()
    for store in stores:
        store.wait()


def pick_blocks(part, ranks, table, sources):
    shape = sources[0].shape[1:]
    copies = 4 * ranks

    def body(*refs):
        pick_kernel(part, ranks, *refs)

    return pl.pallas_call(
        body,
        grid_spec=pltpu.PrefetchScalarGridSpec(
            num_scalar_prefetch=1,
            grid=(1,),
            in_specs=[pl.BlockSpec(memory_space=pltpu.HBM)] * 2,
            out_specs=[pl.BlockSpec(memory_space=pltpu.HBM)] * 2,
            scratch_shapes=[
                pltpu.VMEM((copies,) + shape, sources[0].dtype),
                pltpu.SemaphoreType.DMA((copies,)),
                pltpu.SemaphoreType.DMA((copies,)),
            ],
        ),
        out_shape=[jax.ShapeDtypeStruct((2 * ranks,) + shape, sources[0].dtype)] * 2,
        compiler_params=pltpu.CompilerParams(vmem_limit_bytes=VMEM_LIMIT),
        cost_estimate=LIGHT,
        name="pick_blocks",
    )(table, *sources)


def attend_kernel(first, cap, pieces, groups, steps, tp_index, spans, *refs):
    count = pieces * groups
    x_refs = refs[:count]
    q_ref, wk_first, wk_next, wv_first, wv_next = refs[count : count + 5]
    out_ref, lse_ref, x_all, xt_all, scores_ref, weights_ref, k_even, v_even, k_odd, v_odd = refs[-10:]
    nlen = scores_ref.shape[-1]
    pairs = scores_ref.shape[0] // cap
    step = pl.program_id(0)
    scale = HDIM ** (-0.5)
    lanes = lax.broadcasted_iota(jnp.int32, (SPAN, LANES), 1)

    def project_keys(w_ref, out):
        out[...] = jnp.dot(w_ref[...], x_all[...], preferred_element_type=jnp.float32).astype(
            jnp.bfloat16
        )

    def project_values(w_ref, out):
        out[...] = jnp.dot(xt_all[...], w_ref[...], preferred_element_type=jnp.float32).astype(
            jnp.bfloat16
        )

    def score(k_ref):
        none = jnp.zeros((SPAN, HDIM), jnp.bfloat16)
        for pair in range(pairs):
            for i in range(cap):
                q = q_ref[spans[first + i], :, pair * PAIR : (pair + 1) * PAIR]
                upper = jnp.concatenate([q[:, :HDIM], none], axis=1)
                lower = jnp.concatenate([none, q[:, HDIM:]], axis=1)
                scores_ref[pair * cap + i] = jnp.dot(
                    jnp.concatenate([upper, lower], axis=0),
                    k_ref[pair * PAIR : (pair + 1) * PAIR, i * nlen : (i + 1) * nlen],
                    preferred_element_type=jnp.float32,
                )

    def soften():
        for i in range(cap):
            held = lse_ref[i]
            for pair in range(pairs):
                scores = scores_ref[pair * cap + i]
                highest = jnp.max(scores, axis=1, keepdims=True)
                exponent = jnp.exp((scores - highest) * scale)
                totals = jnp.sum(exponent, axis=1, keepdims=True)
                weights_ref[pair * cap + i] = (exponent * (1.0 / totals)).astype(jnp.bfloat16)
                lse = highest * scale + jnp.log(totals)
                at = pairs * step + pair
                held = jnp.where(lanes == at, lse[:SPAN], held)
                held = jnp.where(lanes == LANES // 8 + at, lse[SPAN:], held)
            lse_ref[i] = held

    def blend(v_ref):
        for pair in range(pairs):
            cols = slice(pair * PAIR, (pair + 1) * PAIR)
            for i in range(cap):
                blended = jnp.dot(
                    weights_ref[pair * cap + i],
                    v_ref[i * nlen : (i + 1) * nlen, cols],
                    preferred_element_type=jnp.float32,
                )
                out_ref[i, :, cols] = jnp.concatenate(
                    [blended[:SPAN, :HDIM], blended[SPAN:, HDIM:]], axis=1
                ).astype(jnp.bfloat16)

    @pl.when(step == 0)
    def _():
        lse_ref[...] = jnp.zeros_like(lse_ref)
        per = cap // groups
        for n, x_ref in enumerate(x_refs):
            group, piece = n // pieces, n % pieces
            width = x_ref.shape[1]
            top = 0
            if pieces == 2:
                place = tp_index[0] if piece == 0 else 1 - tp_index[0]
                top = pl.multiple_of(place * width, 16)
            for i in range(per):
                left = (group * per + i) * nlen
                x_all[pl.ds(top, width), left : left + nlen] = x_ref[i]
        for i in range(cap):
            at = slice(i * nlen, (i + 1) * nlen)
            xt_all[at, :] = x_all[:, at].T
        project_keys(wk_first, k_even)
        project_values(wv_first, v_even)

    def work(k_now, v_now, k_later, v_later):
        score(k_now)
        project_keys(wk_next, k_later)
        soften()
        project_values(wv_next, v_later)
        blend(v_now)

    def finish(k_now, v_now):
        score(k_now)
        soften()
        blend(v_now)

    if steps > 1:
        pl.when((step < steps - 1) & (step % 2 == 0))(lambda: work(k_even, v_even, k_odd, v_odd))
    if steps > 2:
        pl.when((step < steps - 1) & (step % 2 == 1))(lambda: work(k_odd, v_odd, k_even, v_even))
    ends = (k_even, v_even) if steps % 2 == 1 else (k_odd, v_odd)
    pl.when(step == steps - 1)(lambda: finish(*ends))


def attend_part(first, scalars, groups, windows, weights, slots, held):
    blocks = [x for group in groups for x in group]
    pieces = len(groups[0])
    per, width, nlen = blocks[0].shape
    cap = per * len(groups)
    place = first // cap
    features = width * pieces
    columns = 2 * PAIR
    steps = windows.shape[-1] // columns

    in_specs = [pl.BlockSpec(x.shape, lambda t, *_: (0, 0, 0)) for x in blocks]
    operands = list(blocks)
    in_specs += [pl.BlockSpec((windows.shape[0], SPAN, columns), lambda t, *_: (0, 0, t))]
    operands += [far_from_core(windows)]
    key_weight, value_weight = weights
    in_specs += [
        pl.BlockSpec((columns, features), lambda t, *_: (0, 0)),
        pl.BlockSpec((columns, features), lambda t, *_: (jnp.minimum(t + 1, steps - 1), 0)),
        pl.BlockSpec((features, columns), lambda t, *_: (0, 0)),
        pl.BlockSpec((features, columns), lambda t, *_: (0, jnp.minimum(t + 1, steps - 1))),
    ]
    operands += [key_weight] * 2 + [value_weight] * 2
    aliases = {}
    if held is not None:
        in_specs += [pl.BlockSpec(memory_space=pl.ANY)] * 2
        aliases = {2 + len(operands): 0, 3 + len(operands): 1}
        operands += list(held)
    keys = pltpu.VMEM((columns, cap * nlen), jnp.bfloat16)
    values = pltpu.VMEM((cap * nlen, columns), jnp.bfloat16)

    def body(*refs):
        attend_kernel(first, cap, pieces, len(groups), steps, *refs)

    return pl.pallas_call(
        body,
        grid_spec=pltpu.PrefetchScalarGridSpec(
            num_scalar_prefetch=2,
            grid=(steps,),
            in_specs=in_specs,
            out_specs=[
                pl.BlockSpec((cap, SPAN, columns), lambda t, *_: (place, 0, t)),
                pl.BlockSpec((cap, SPAN, LANES), lambda t, *_: (place, 0, 0)),
            ],
            scratch_shapes=[
                pltpu.VMEM((features, cap * nlen), jnp.bfloat16),
                pltpu.VMEM((cap * nlen, features), jnp.bfloat16),
                pltpu.VMEM((2 * cap, 2 * SPAN, nlen), jnp.float32),
                pltpu.VMEM((2 * cap, 2 * SPAN, nlen), jnp.bfloat16),
                keys, values, keys, values,
            ],
        ),
        out_shape=[
            pltpu.HBM((slots,) + windows.shape[1:], jnp.bfloat16),
            pltpu.HBM((slots, SPAN, LANES), jnp.float32),
        ],
        input_output_aliases=aliases,
        compiler_params=pltpu.CompilerParams(vmem_limit_bytes=VMEM_LIMIT),
        cost_estimate=HEAVY,
        name="attend_part",
    )(*scalars, *operands)


def spread_matrix(columns):
    per = LANES // 8
    row = lax.broadcasted_iota(jnp.int32, (4 * per, columns), 0)
    head = lax.broadcasted_iota(jnp.int32, (4 * per, columns), 1) // HDIM
    own = 2 * (row % per) + (row // per) % 2
    return jnp.where(head == own, 1.0, 0.0).astype(jnp.bfloat16)


def first_shares(l0, l1):
    largest = jnp.maximum(l0, l1)
    e0, e1 = jnp.exp(l0 - largest), jnp.exp(l1 - largest)
    share = e0 / (e0 + e1)
    high = share.astype(jnp.bfloat16).astype(jnp.float32)
    low = pltpu.roll(share - high, LANES // 4, 1)
    lanes = lax.broadcasted_iota(jnp.int32, share.shape, 1)
    return jnp.where(lanes < LANES // 4, high, low).astype(jnp.bfloat16)[:, : LANES // 2]


def mixed(p0, p1, shares, spread, cols):
    share = jnp.dot(shares, spread[:, cols], preferred_element_type=jnp.float32)
    return p0[0, :, cols].astype(jnp.float32) * share + p1[0, :, cols].astype(jnp.float32) * (
        1.0 - share
    )


def mix_last_kernel(places, p0, p1, l0, l1, out_ref, spread):
    spread[...] = spread_matrix(out_ref.shape[-1])
    shares = first_shares(l0[0], l1[0])
    for pair in range(out_ref.shape[-1] // PAIR):
        cols = slice(pair * PAIR, (pair + 1) * PAIR)
        out_ref[:, cols] = mixed(p0, p1, shares, spread, cols).astype(jnp.bfloat16)


def mix_kernel(places, *refs):
    ins, (out_ref, before, spread) = refs[:-3], refs[-3:]
    tile = 16
    late = lax.broadcasted_iota(jnp.int32, (tile, PAIR), 0) == tile - 1

    @pl.when(pl.program_id(0) == 0)
    def _():
        spread[...] = spread_matrix(out_ref.shape[-1])

    for n in range(len(ins) // 4):
        p0, p1, l0, l1 = ins[4 * n : 4 * n + 4]
        shares = first_shares(l0[0], l1[0])
        top = n * SPAN
        cut = top + SPAN - tile
        out_ref[top:cut, :] = before[: SPAN - tile, :]
        for pair in range(out_ref.shape[-1] // PAIR):
            cols = slice(pair * PAIR, (pair + 1) * PAIR)
            result = mixed(p0, p1, shares, spread, cols)
            out_ref[cut : cut + tile, cols] = jnp.where(
                late, result[SPAN - tile :], before[SPAN - tile :, cols].astype(jnp.float32)
            ).astype(jnp.bfloat16)
            before[:, cols] = result.astype(jnp.bfloat16)


def mix_specs(partials, log_totals, span_of):
    def place(j, shape):
        return pl.BlockSpec((1,) + shape, lambda k, places: (places[2 * span_of(k) + j], 0, 0))

    rows, stats = partials.shape[1:], log_totals.shape[1:]
    return [place(0, rows), place(1, rows), place(0, stats), place(1, stats)]


def mix_last(places, partials, log_totals, span_count):
    columns = partials.shape[-1]
    return pl.pallas_call(
        mix_last_kernel,
        grid_spec=pltpu.PrefetchScalarGridSpec(
            num_scalar_prefetch=1,
            grid=(1,),
            in_specs=mix_specs(partials, log_totals, lambda k: span_count - 1),
            out_specs=pl.BlockSpec((SPAN, columns), lambda k, places: (0, 0)),
            scratch_shapes=[pltpu.VMEM((LANES // 2, columns), jnp.bfloat16)],
        ),
        out_shape=jax.ShapeDtypeStruct((SPAN, columns), jnp.bfloat16),
        cost_estimate=LIGHT,
        name="mix_last",
    )(places, *[far_from_core(x) for x in (partials, partials, log_totals, log_totals)])


def mix(places, partials, log_totals, span_count):
    columns = partials.shape[-1]
    per = 4
    in_specs = []
    for n in range(per):
        in_specs += mix_specs(partials, log_totals, lambda k, n=n: per * k + n)
    return pl.pallas_call(
        mix_kernel,
        grid_spec=pltpu.PrefetchScalarGridSpec(
            num_scalar_prefetch=1,
            grid=(span_count // per,),
            in_specs=in_specs,
            out_specs=pl.BlockSpec((per * SPAN, columns), lambda k, places: (k, 0)),
            scratch_shapes=[
                pltpu.VMEM((SPAN, columns), jnp.bfloat16),
                pltpu.VMEM((LANES // 2, columns), jnp.bfloat16),
            ],
        ),
        out_shape=jax.ShapeDtypeStruct((span_count * SPAN, columns), jnp.bfloat16),
        compiler_params=pltpu.CompilerParams(vmem_limit_bytes=VMEM_LIMIT),
        cost_estimate=LIGHT,
        name="mix",
    )(places, *([far_from_core(x) for x in (partials, partials, log_totals, log_totals)] * per))


def head_kernel(carried, rows, out_ref):
    early = lax.broadcasted_iota(jnp.int32, out_ref.shape, 0) < SPAN - 1
    out_ref[...] = jnp.where(
        early, carried[...].astype(jnp.float32), rows[...].astype(jnp.float32)
    ).astype(jnp.bfloat16)


def with_head(carried, mixed_rows):
    spec = pl.BlockSpec((SPAN, mixed_rows.shape[-1]), lambda k: (0, 0))
    return pl.pallas_call(
        head_kernel,
        grid=(1,),
        in_specs=[spec, spec],
        out_specs=spec,
        out_shape=jax.ShapeDtypeStruct(mixed_rows.shape, mixed_rows.dtype),
        input_output_aliases={1: 0},
        cost_estimate=LIGHT,
        name="with_head",
    )(carried, mixed_rows)


def after(values, *others):
    return lax.optimization_barrier((values, others))[0]


def shards(queries, neighbours, key_weight, value_weight, neighbour_ids):
    span_count = neighbour_ids.shape[0]
    seq_count, tp_count = lax.axis_size("seq"), lax.axis_size("tp")
    block_count = neighbours.shape[0]
    wants = 2 * span_count
    ranks = (wants + seq_count - 1) // seq_count
    outer = seq_count // INNER
    slots = seq_count * ranks
    cap = INNER * ranks
    own_index = lax.axis_index("seq")
    tp_index = lax.axis_index("tp").astype(jnp.int32).reshape(1)

    def all_features(part):
        if tp_count == 2:
            return [part, swapped(part, "tp", 1)]
        return [lax.all_gather(part, "tp", axis=1, tiled=True)]

    def along(x, offset, senders):
        pairs = [(i, i ^ offset) for i in range(seq_count) if i // INNER in senders]
        return lax.ppermute(x, "seq", pairs)

    own_ids = neighbour_ids.reshape(wants)
    group_ids = jnp.stack([own_ids, swapped(own_ids, "seq", 2)])
    mate = swapped(neighbours, "seq", 1)
    incoming = passed_along(queries[:SPAN], "seq", -1)
    own_blocks = after(neighbours, incoming)
    near = swapped(own_blocks, "seq", INNER)
    across = along(own_blocks, 3 * INNER, (1, 2)) if outer == 4 else near

    group_sources = group_ids // block_count
    group_ranks = slot_ranks(group_sources)
    sources = own_index ^ (INNER * jnp.arange(outer)[:, None] + jnp.arange(2))
    hit = (group_sources[None, :, None, None, :] == sources[:, None, :, None, None]) & (
        group_ranks[None, :, None, None, :] == jnp.arange(ranks)[None, None, None, :, None]
    )
    table = jnp.sum(
        jnp.where(hit, (group_ids % block_count)[None, :, None, None, :], 0), axis=-1
    )
    table = table.astype(jnp.int32).reshape(-1)

    own_sources = own_ids // block_count
    places = ((own_sources ^ own_index) * ranks + slot_ranks(own_sources)).astype(jnp.int32)
    order = jnp.arange(wants)
    spans = jnp.sum(
        jnp.where(places[None, :] == jnp.arange(slots)[:, None], order[None, :] // 2, 0), axis=1
    ).astype(jnp.int32)

    def pick(j, part, mate, *others):
        mine, outgoing = pick_blocks(j, ranks, after(table, *others), [part, mate])
        return all_features(mine), swapped(outgoing, "seq", 2)

    def attend(first, groups, held, *others):
        scalars = (tp_index, after(spans, *others))
        return attend_part(first, scalars, groups, windows, weights, slots, held)

    weights = (key_weight.T, value_weight)
    mine, got = pick(0, neighbours, mate, weights[0], incoming)
    windows = span_windows(after(queries, mine[0]), incoming, span_count)
    near, across = after((near, across), windows, *mine, got)
    parts = [neighbours, near]
    if outer == 4:
        inside = (own_index // INNER == 1) | (own_index // INNER == 2)
        second = along(near, 3 * INNER, (1, 2))
        outward = along(across, INNER, (1, 2))

    def part_of(j, *others):
        if outer != 4:
            low = j & -j
            return swapped(after(parts[j ^ low], *others), "seq", INNER * low)
        if j == 2:
            return jnp.where(inside, *after((second, outward), *others))
        return jnp.where(inside, *after((across, third), *others))

    groups = [[mine, all_features(got)]]
    mine, got = pick(1, near, swapped(near, "seq", 1), got, *mine)
    groups.append([mine, all_features(got)])
    parts.append(part_of(2, groups[1][1][0], *groups[0]))
    if outer == 4:
        third = along(second, INNER, (1, 2))
    mine, got = pick(2, parts[2], swapped(parts[2], "seq", 1))
    held = attend(0, groups[0], None, mine[0])
    for j in range(3, outer):
        groups.append([mine, all_features(after(got, held))])
        parts.append(part_of(j, groups[j - 1][1][0], *groups[j - 2]))
        mine, got = pick(j, parts[j], swapped(parts[j], "seq", 1))
        held = attend((j - 2) * cap, groups[j - 2], held, mine[0])
    groups.append([mine, all_features(after(got, held))])
    held = attend((outer - 2) * cap, groups[outer - 2], held, groups[outer - 1][1][0])
    held = attend((outer - 1) * cap, groups[outer - 1], held)

    partials, log_totals = held
    last = mix_last(places, partials, log_totals, span_count)
    carried = passed_along(last, "seq", 1)
    rows = mix(places, partials, log_totals, span_count)
    return with_head(carried, rows)


def solution(mesh):
    in_specs = (P("seq", "tp"), P("seq", "tp", None), P(None, "tp"), P(None, "tp"), P("seq", None))
    out_specs = P("seq", "tp")
    return jax.shard_map(shards, mesh=mesh, in_specs=in_specs, out_specs=out_specs, check_vma=False)
```
